256 devices in a mesh: train: 32 (over y_hi, z, core), cand: 8 (over x, y_lo).
Axes of the slice: x: 4, y: 4 (y_hi: 2, y_lo: 2; y = y_hi * 2 + y_lo), z: 8, core: 2. Of those that a mesh axis runs over, the one named last changes fastest.
Arguments:
- x_train: float32 [8, 16384], P(None, 'train'), may hold values from -4 to 4
- x_cand: float32 [8, 8192], P(None, 'cand'), may hold values from -4 to 4
- targets: float32 [16384], P(('train', 'cand')), may hold values from -6 to 6
- noise: float32 [16384, 64], P(('train', 'cand')), may hold values from -5 to 5
- omega: float32 [8, 4096], replicated, may hold values from -6 to 6
- phase: float32 [4096], replicated, may hold values from -3.140625 to 3.140625
- prior_weights: bfloat16 [4096, 64], P('cand'), may hold values from -6 to 6
Outputs:
- samples: float32 [8192, 64], P(('cand', 'train'))
- solution: float32 [16384, 64], P(('train', 'cand'))
The draws below stay inside these ranges and needn't reach their ends.
All inputs are finite; a program needn't handle non-finite values.
Results may differ from the reference program's by a relative error of at most 0.0019.
The reference program's roundings to bfloat16 on the way count: a program that leaves them out, or rounds other values in their place, can miss the bound.
Values may be sent and summed in bfloat16 or wider, within the bound.
A program may use at most 64 MiB of HBM per device.

```python
import math
import jax
import jax.numpy as jnp
from jax import lax

DIM = 8
S = 64
F = 4096
ITERS = 2
N = 16384
C = 8192


def shard_levels(key, extent, shards, low, largest):
    factor_of, own = 1.0, jax.random.fold_in(key, 6)
    for dim, parts in shards:
        heights = jnp.exp(jax.random.uniform(jax.random.fold_in(own, dim), (parts,), jnp.float32, low / len(shards), largest / len(shards)))
        factor_of = factor_of * jnp.repeat(heights, extent[dim] // parts).reshape([-1 if axis == dim else 1 for axis in range(len(extent))])
    return factor_of


def gaussian(key, dims, spread, limit, pieces=(), held_as=jnp.bfloat16):
    entries = spread * jax.random.normal(key, dims, jnp.float32)
    if pieces:
        entries = entries * shard_levels(key, dims, pieces, -0.22, 0.18)
    return jnp.clip(entries, -limit, limit).astype(held_as)


def setup_inputs(seed: int = 0) -> dict:
    keys = jax.random.split(jax.random.key(seed), 8)
    x_train = gaussian(keys[0], (DIM, N), 0.7, 4.0, ((1, 32),), jnp.float32)
    x_cand = gaussian(keys[1], (DIM, C), 0.7, 4.0, ((1, 8),), jnp.float32)
    targets = gaussian(keys[2], (N,), 1.0, 6.0, ((0, 256),), jnp.float32)
    noise = gaussian(keys[3], (N, S), 0.7, 5.0, ((0, 256),), jnp.float32)
    omega = gaussian(keys[4], (DIM, F), 1.0, 6.0, (), jnp.float32)
    phase = jnp.clip(jax.random.uniform(keys[5], (F,), jnp.float32, -3.140625, 3.140625), -3.140625, 3.140625)
    prior_weights = gaussian(keys[6], (F, S), 1.0, 6.0, ((0, 8),))
    return dict(x_train=x_train, x_cand=x_cand, targets=targets, noise=noise, omega=omega, phase=phase, prior_weights=prior_weights)


noise_level = 0.5

def squares_of(points):
    return lax.optimization_barrier(jnp.sum(points * points, axis=0))

def kernel_tile(row_points, row_norms, column_points, column_norms):
    inner = jnp.dot(row_points.T, column_points, precision=lax.Precision.HIGHEST)
    return jnp.exp(-0.5 * (row_norms[:, None] + column_norms[None, :] - 2.0 * inner)).astype(jnp.bfloat16)

def features(points, omega, phase):
    angles = jnp.dot(points.T, omega, precision=lax.Precision.HIGHEST) + phase[None, :]
    return (math.sqrt(2.0 / omega.shape[1]) * jnp.cos(angles)).astype(jnp.bfloat16)

def split_points(points, size):
    total = points.shape[1]
    return points.reshape(points.shape[0], total // size, size).transpose(1, 0, 2)

def reference(x_train, x_cand, targets, noise, omega, phase, prior_weights):
    train_size = math.gcd(N, 1024)
    train_blocks = split_points(x_train, train_size)
    train_norms = squares_of(x_train)

    def prior_block(points):
        return jnp.dot(features(points, omega, phase), prior_weights, preferred_element_type=jnp.float32)
    prior_train = lax.map(prior_block, train_blocks).reshape(N, S)
    rhs = targets[:, None] - prior_train - noise

    def apply(direction):
        packed = direction.astype(jnp.bfloat16)

        def rows_of(points):
            tile = kernel_tile(points, squares_of(points), x_train, train_norms)
            return jnp.dot(tile, packed, preferred_element_type=jnp.float32)
        return lax.map(rows_of, train_blocks).reshape(N, S) + noise_level * direction
    solution = jnp.zeros((N, S), jnp.float32)
    residual = rhs
    direction = rhs
    norm_now = lax.optimization_barrier(jnp.sum(residual * residual, axis=0))
    for step in range(ITERS):
        image = apply(direction)
        alpha = norm_now / lax.optimization_barrier(jnp.sum(direction * image, axis=0))
        solution = solution + alpha * direction
        residual = residual - alpha * image
        norm_next = lax.optimization_barrier(jnp.sum(residual * residual, axis=0))
        direction = residual + norm_next / norm_now * direction
        norm_now = norm_next
    packed_solution = solution.astype(jnp.bfloat16)
    cand_size = math.gcd(C, 1024)

    def cand_block(points):
        tile = kernel_tile(points, squares_of(points), x_train, train_norms)
        return prior_block(points) + jnp.dot(tile, packed_solution, preferred_element_type=jnp.float32)
    samples = lax.map(cand_block, split_points(x_cand, cand_size)).reshape(C, S)
    return (samples, solution)
```

```python
import math

import jax
import jax.numpy as jnp
from jax import lax
from jax.experimental import pallas as pl
from jax.experimental.pallas import tpu as pltpu
from jax.sharding import PartitionSpec as P

MESH = pl.DeviceIdType.MESH
F32, BF16 = jnp.float32, jnp.bfloat16
NZ, NC, NH = 8, 8, 4
NP = NH * NC
OWN = 64
CANDS = 32
FEATS = 512
TOTAL_FEATS = 4096
NOISE_LEVEL = 0.5
COS = (
    0.9999999890590217,
    -19.73920449945381,
    64.93911745989173,
    -85.45013953082398,
    60.16763095051855,
    -25.967599246994247,
    6.528658159389057,
)


def split3(value):
    one = value.astype(BF16).astype(F32)
    two = (value - one).astype(BF16).astype(F32)
    return one, two, value - one - two


def rows8(*rows):
    index = lax.broadcasted_iota(jnp.int32, (8, rows[0].shape[1]), 0)
    out = jnp.zeros((8, rows[0].shape[1]), F32)
    for place, row in enumerate(rows):
        out = jnp.where(index == place, row, out)
    return out


def half_norm(points):
    return -0.5 * jnp.sum(points * points, axis=0, keepdims=True)


def left_side(points):
    one, two, three = split3(points)
    ones = jnp.ones((1, points.shape[1]), F32)
    tail = rows8(*split3(half_norm(points)), ones, ones, ones)
    pad = jnp.zeros((72, points.shape[1]), F32)
    return jnp.concatenate([one, one, two, two, one, three, tail, pad], axis=0).T.astype(BF16)


def right_side(points, tail):
    one, two, three = split3(points)
    pad = jnp.zeros((72, points.shape[1]), F32)
    return jnp.concatenate([one, two, one, two, three, one, tail, pad], axis=0).astype(BF16)


def kernel(
    xt, xc, tg, nz, om, ph, pw, sam, sol,
    xls, xl, xcs, xcb, xp, by, bw, atb, atc, atl, km, pwd,
    pts, ptb, pcs, pcb, own0, own1, vb0, vb1, r0l, r1l,
    o1, o2, kr, krb, kr1, ucs, ucb, vcs, vcb,
    sa_s, sa, sb_s, sb, ra_s, ra, rb_s, rb, qa_s, qa, qb_s, qb,
    hb0, hb1, ssem, rsem,
):
    t, c = lax.axis_index("train"), lax.axis_index("cand")
    y_hi, z, core = t // 16, lax.rem(t, 16) // 2, lax.rem(t, 2)
    h = y_hi * 2 + core
    q = h * NC + c

    def plane_peer(k):
        other = lax.rem(q + k, NP)
        oh, oc = other // NC, lax.rem(other, NC)
        return ((oh // 2) * 16 + z * 2 + lax.rem(oh, 2), oc)

    def line_index(k):
        return lax.rem(z + k, NZ)

    def line_peer(k):
        return (y_hi * 16 + line_index(k) * 2 + core, c)

    def cand_index(k):
        return lax.rem(c + k, NC)

    def cand_peer(k):
        return (t, cand_index(k))

    def block_peer(k):
        oh = lax.rem(h + k, NH)
        return ((oh // 2) * 16 + z * 2 + lax.rem(oh, 2), c)

    barrier = pltpu.get_barrier_semaphore()

    def greet(peer, count):
        def one(k, carry):
            pl.semaphore_signal(barrier, inc=1, device_id=peer(k), device_id_type=MESH)
            return carry

        lax.fori_loop(1, count, one, 0)

    greet(plane_peer, NP)
    greet(line_peer, NZ)

    def push(phase, count, peer, source, target):
        def one(k, carry):
            pltpu.make_async_remote_copy(
                src_ref=source(k),
                dst_ref=target,
                send_sem=ssem.at[phase],
                recv_sem=rsem.at[phase],
                device_id=peer(k),
                device_id_type=MESH,
            ).start()
            return carry

        lax.fori_loop(1, count, one, 0)

    def settle(phase, sems, buf):
        ref = buf.at[pl.ds(0, buf.shape[0] - 1)]
        pltpu.make_async_copy(ref, ref, sems.at[phase]).wait()

    def arrived(phase, buf):
        settle(phase, rsem, buf)

    lane = lax.broadcasted_iota(jnp.int32, (1, 128), 1)
    low = lane < 64

    def swap(value):
        return pltpu.roll(value, 64, 1)

    def pair(first, second):
        return jnp.where(low, first, swap(second))

    def fold(value):
        row = jnp.sum(value, axis=0, keepdims=True)
        return row + swap(row)

    mine = xt[:, pl.ds(pl.multiple_of((c // 2) * 128, 128), 128)]
    mine = jnp.where(lax.rem(c, 2) == 1, swap(mine), mine)
    xls[...] = mine
    xl[z] = mine
    xp[h] = xt[...]
    cand = xc[:, pl.ds(pl.multiple_of((t // 4) * 128, 128), 128)]
    cand = pltpu.roll(cand, lax.rem(128 - lax.rem(t, 4) * 32, 128), 1)
    xcs[...] = cand
    xcb[c] = cand

    feat = pl.ds(pl.multiple_of(c * FEATS, FEATS), FEATS)
    turn = 1.0 / (2.0 * math.pi)
    zero = jnp.zeros((1, FEATS), F32)
    bw[...] = right_side(
        om[:, feat] * turn, rows8(zero, zero, zero, *split3(ph[:, feat] * turn))
    )
    pwd[...] = jnp.concatenate([pw[...], pw[...]], axis=1)
    atb[...] = left_side(xt[...])

    def feature_rows(left, first, count):
        turns = jnp.dot(left[pl.ds(first, count), :], bw[...], preferred_element_type=F32)
        part = turns - jnp.floor(turns + 0.5)
        square = part * part
        value = jnp.full(square.shape, COS[-1], F32)
        for coefficient in COS[-2::-1]:
            value = value * square + coefficient
        packed = (value * math.sqrt(2.0 / TOTAL_FEATS)).astype(BF16)
        return jnp.dot(packed, pwd[...], preferred_element_type=F32)

    def train_features(i, carry):
        out = feature_rows(atb, pl.multiple_of(i * OWN, OWN), OWN)
        pts[i] = jnp.where(low, out[0:32], out[32:64])
        return carry

    lax.fori_loop(0, NC, train_features, 0)

    pl.semaphore_wait(barrier, NP - 1 + NZ - 1)
    push(0, NH, block_peer, lambda k: xt, xp.at[h])
    push(1, NZ, line_peer, lambda k: xls, xl.at[z])
    push(3, NC, cand_peer, lambda k: pts.at[cand_index(k)], ptb.at[c])
    push(2, NC, cand_peer, lambda k: xcs, xcb.at[c])
    ptb[c] = pts[c]

    row = tg[...]
    place = lax.broadcasted_iota(jnp.int32, (32, 64), 0)
    at = lax.broadcasted_iota(jnp.int32, (32, 64), 1)
    upper = jnp.sum(jnp.where(at == place, row, 0.0), axis=1, keepdims=True)
    lower = jnp.sum(jnp.where(at == place + 32, row, 0.0), axis=1, keepdims=True)
    noise = jnp.concatenate([nz[0:32, :], nz[32:64, :]], axis=1)
    base = jnp.where(low, upper, lower) - noise

    def line_cands(j):
        tile = xc[:, pl.ds(pl.multiple_of(y_hi * 512 + j * 128, 128), 128)]
        tile = pltpu.roll(tile, lax.rem(128 - core * 32, 128), 1)
        return jnp.where(lane < 32, tile, pltpu.roll(tile, 96, 1))

    for j in range(2):
        atl[512 + j * 128 : 640 + j * 128, :] = left_side(
            pair(line_cands(2 * j), line_cands(2 * j + 1))
        )

    arrived(0, xp)
    for i in range(NH):
        uppers, lowers = [], []
        for j in range(2):
            tiles = [xp[i, :, j * 256 + 128 * g : j * 256 + 128 * g + 128] for g in range(2)]
            uppers.append(pair(*[jnp.where(lane < 32, a, pltpu.roll(a, 96, 1)) for a in tiles]))
            lowers.append(
                pair(*[jnp.where(lane < 32, pltpu.roll(a, 96, 1), swap(a)) for a in tiles])
            )
        for start, tiles in ((i * 256, uppers), (1024 + i * 256, lowers)):
            points = jnp.concatenate(tiles, axis=1)
            ones = jnp.ones((1, 256), F32)
            tail = rows8(ones, ones, ones, *split3(half_norm(points)))
            by[:, start : start + 256] = right_side(points, tail)

    def entries(first, count):
        def one(j, carry):
            columns = pl.ds(pl.multiple_of(j * 256, 256), 256)
            power = jnp.dot(atl[pl.ds(first, count), :], by[:, columns], preferred_element_type=F32)
            km[pl.ds(first, count), columns] = jnp.exp(power).astype(BF16)
            return carry

        lax.fori_loop(0, 8, one, 0)

    arrived(1, xl)
    for j in range(4):
        atl[j * 128 : j * 128 + 128, :] = left_side(pair(xl[2 * j], xl[2 * j + 1]))
    entries(0, 256)

    arrived(3, ptb)
    r0 = base - jnp.sum(ptb[...], axis=0)
    own0[...] = r0
    r0l[z] = r0
    hb0[...] = r0.astype(BF16)
    vb0[q] = r0.astype(BF16)
    push(4, NP, plane_peer, lambda k: hb0, vb0.at[q])
    push(5, NZ, line_peer, lambda k: own0, r0l.at[z])
    rr_own = fold(r0 * r0)

    entries(256, 256)
    entries(512, 256)

    arrived(2, xcb)
    for j in range(2):
        joined = xcb[4 * j]
        for g in range(1, 4):
            joined = jnp.where(lane < 32 * g, joined, pltpu.roll(xcb[4 * j + g], 32 * g, 1))
        atc[j * 128 : j * 128 + 128, :] = left_side(joined)

    def cand_features(i, carry):
        out = feature_rows(atc, pl.multiple_of(i * OWN, OWN), OWN)
        pcs[2 * i] = jnp.where(low, out[0:16], out[16:32])
        pcs[2 * i + 1] = jnp.where(low, out[32:48], out[48:64])
        return carry

    lax.fori_loop(0, 4, cand_features, 0)
    push(6, NC, cand_peer, lambda k: pcs.at[cand_index(k)], pcb.at[c])
    pcb[c] = pcs[c]

    def product(field, pieces, cand_pieces):
        values = field[...].reshape(NP * 32, 128)
        o1[...] = jnp.dot(km[:, 0:1024], values, preferred_element_type=F32)
        o2[...] = jnp.dot(km[:, 1024:2048], values, preferred_element_type=F32)

        def joined(first, size):
            a1, b1 = o1[pl.ds(first, size), :], o1[pl.ds(first + size, size), :]
            a2, b2 = o2[pl.ds(first, size), :], o2[pl.ds(first + size, size), :]
            return jnp.where(low, a1, b2) + swap(jnp.where(low, b1, a2))

        for i in range(NZ):
            pieces[i] = joined(i * 64, 32)
        for i in range(NZ):
            cand_pieces[i] = joined(512 + i * 32, 16)

    arrived(4, vb0)
    product(vb0, kr, ucs)
    push(7, NZ, line_peer, lambda k: kr.at[line_index(k)], krb.at[z])
    krb[z] = kr[z]
    arrived(5, r0l)
    curve = fold(jnp.sum(kr[...] * r0l[...], axis=0))
    part = jnp.where(low, curve, rr_own)
    sa_s[...] = part
    sa[q] = part
    push(8, NP, plane_peer, lambda k: sa_s, sa.at[q])
    push(9, NZ, line_peer, lambda k: ucs.at[line_index(k)], ucb.at[z])
    ucb[z] = ucs[z]
    arrived(8, sa)
    part = jnp.sum(sa[...], axis=0)
    sb_s[...] = part
    sb[z] = part
    push(10, NZ, line_peer, lambda k: sb_s, sb.at[z])
    arrived(7, krb)
    r0 = own0[...]
    image = jnp.sum(krb[...], axis=0) + NOISE_LEVEL * r0
    arrived(10, sb)
    part = jnp.sum(sb[...], axis=0)
    other = swap(part)
    rr0 = jnp.where(low, other, part)
    alpha1 = rr0 / (jnp.where(low, part, other) + NOISE_LEVEL * rr0)
    r1 = r0 - alpha1 * image

    own1[...] = r1
    r1l[z] = r1
    hb1[...] = r1.astype(BF16)
    vb1[q] = r1.astype(BF16)
    push(11, NP, plane_peer, lambda k: hb1, vb1.at[q])
    rr1_own = fold(r1 * r1)
    ra_s[...] = rr1_own
    ra[q] = rr1_own
    push(13, NP, plane_peer, lambda k: ra_s, ra.at[q])
    push(12, NZ, line_peer, lambda k: own1, r1l.at[z])
    arrived(13, ra)
    part = jnp.sum(ra[...], axis=0)
    rb_s[...] = part
    rb[z] = part
    push(14, NZ, line_peer, lambda k: rb_s, rb.at[z])
    arrived(11, vb1)
    product(vb1, kr1, vcs)
    push(15, NZ, line_peer, lambda k: vcs.at[line_index(k)], vcb.at[z])
    vcb[z] = vcs[z]
    arrived(12, r1l)
    arrived(14, rb)
    rr1 = jnp.sum(rb[...], axis=0)
    beta = rr1 / rr0
    curve = fold(jnp.sum((r1l[...] + beta * r0l[...]) * (kr1[...] + beta * kr[...]), axis=0))
    r0, r1 = own0[...], own1[...]
    d1 = r1 + beta * r0
    part = curve + NOISE_LEVEL * fold(d1 * d1)
    qa_s[...] = part
    qa[q] = part
    push(16, NP, plane_peer, lambda k: qa_s, qa.at[q])
    arrived(6, pcb)
    prior = jnp.sum(pcb[...], axis=0)
    arrived(9, ucb)
    first_part = jnp.sum(ucb[...], axis=0)
    arrived(16, qa)
    part = jnp.sum(qa[...], axis=0)
    qb_s[...] = part
    qb[z] = part
    push(17, NZ, line_peer, lambda k: qb_s, qb.at[z])
    arrived(15, vcb)
    second_part = jnp.sum(vcb[...], axis=0)
    arrived(17, qb)
    alpha2 = rr1 / jnp.sum(qb[...], axis=0)

    result = alpha1 * r0 + alpha2 * d1
    sol[0:32, :] = result[:, 0:64]
    sol[32:64, :] = swap(result)[:, 0:64]
    result = prior + (alpha1 + alpha2 * beta) * first_part + alpha2 * second_part
    sam[0:16, :] = result[:, 0:64]
    sam[16:32, :] = swap(result)[:, 0:64]

    for phase, buf in enumerate(
        (xp, xl, xcb, ptb, vb0, r0l, pcb, krb, sa, ucb, sb, vb1, r1l, ra, rb, vcb, qa, qb)
    ):
        settle(phase, ssem, buf)


def body(x_train, x_cand, targets, noise, omega, phase, prior_weights):
    vmem = pltpu.VMEM
    field = lambda n, rows, dtype=F32: vmem((n, rows, 128), dtype)
    tile, row = vmem((8, 128), F32), vmem((1, 128), F32)
    scratch = [
        tile, field(NZ, 8), tile, field(NC, 8), vmem((NH, 8, 512), F32),
        vmem((128, 2048), BF16), vmem((128, FEATS), BF16), vmem((512, 128), BF16),
        vmem((256, 128), BF16), vmem((768, 128), BF16), vmem((768, 2048), BF16),
        vmem((FEATS, 128), BF16),
        field(NC, 32), field(NC, 32), field(NC, 16), field(NC, 16),
        vmem((32, 128), F32), vmem((32, 128), F32),
        field(NP, 32, BF16), field(NP, 32, BF16), field(NZ, 32), field(NZ, 32),
        vmem((768, 128), F32), vmem((768, 128), F32),
        field(NZ, 32), field(NZ, 32), field(NZ, 32),
        field(NZ, 16), field(NZ, 16), field(NZ, 16), field(NZ, 16),
        row, field(NP, 1), row, field(NZ, 1), row, field(NP, 1), row, field(NZ, 1),
        row, field(NP, 1), row, field(NZ, 1),
        vmem((32, 128), BF16), vmem((32, 128), BF16),
        pltpu.SemaphoreType.DMA((18,)), pltpu.SemaphoreType.DMA((18,)),
    ]
    return pl.pallas_call(
        kernel,
        out_shape=(
            jax.ShapeDtypeStruct((CANDS, OWN), F32),
            jax.ShapeDtypeStruct((OWN, OWN), F32),
        ),
        in_specs=[pl.BlockSpec(memory_space=vmem)] * 7,
        out_specs=(pl.BlockSpec(memory_space=vmem),) * 2,
        scratch_shapes=scratch,
        compiler_params=pltpu.CompilerParams(
            collective_id=0, has_side_effects=True, vmem_limit_bytes=32 * 1024 * 1024
        ),
    )(
        x_train, x_cand, targets.reshape(1, OWN), noise, omega,
        phase.reshape(1, TOTAL_FEATS), prior_weights,
    )


def solution(mesh):
    placed = (
        P(None, "train"),
        P(None, "cand"),
        P(("train", "cand")),
        P(("train", "cand"), None),
        P(),
        P(),
        P("cand", None),
    )
    return jax.shard_map(
        body,
        mesh=mesh,
        in_specs=placed,
        out_specs=(P(("cand", "train"), None), P(("train", "cand"), None)),
        check_vma=False,
    )
```

```python
import math

import jax
import jax.numpy as jnp
from jax import lax
from jax.experimental import pallas as pl
from jax.experimental.pallas import tpu as pltpu
from jax.sharding import PartitionSpec as P

MESH = pl.DeviceIdType.MESH
F32, BF16 = jnp.float32, jnp.bfloat16
NZ, NC, NH = 8, 8, 4
NP = NH * NC
OWN = 64
CANDS = 32
FEATS = 512
TOTAL_FEATS = 4096
NOISE_LEVEL = 0.5
COS = (
    0.9999999890590217,
    -19.73920449945381,
    64.93911745989173,
    -85.45013953082398,
    60.16763095051855,
    -25.967599246994247,
    6.528658159389057,
)


def split3(value):
    one = value.astype(BF16).astype(F32)
    two = (value - one).astype(BF16).astype(F32)
    return one, two, value - one - two


def rows8(*rows):
    index = lax.broadcasted_iota(jnp.int32, (8, rows[0].shape[1]), 0)
    out = jnp.zeros((8, rows[0].shape[1]), F32)
    for place, row in enumerate(rows):
        out = jnp.where(index == place, row, out)
    return out


def half_norm(points):
    return -0.5 * jnp.sum(points * points, axis=0, keepdims=True)


def left_side(points):
    one, two, three = split3(points)
    ones = jnp.ones((1, points.shape[1]), F32)
    tail = rows8(*split3(half_norm(points)), ones, ones, ones)
    pad = jnp.zeros((72, points.shape[1]), F32)
    return jnp.concatenate([one, one, two, two, one, three, tail, pad], axis=0).T.astype(BF16)


def right_side(points, tail):
    one, two, three = split3(points)
    pad = jnp.zeros((72, points.shape[1]), F32)
    return jnp.concatenate([one, two, one, two, three, one, tail, pad], axis=0).astype(BF16)


def kernel(
    xt_hbm, xc_hbm, tg_hbm, nz_hbm, om_hbm, ph_hbm, pw_hbm, sam, sol,
    xt, xc, tg, nz, om, ph, pw,
    xls, xl, xcs, xcb, xp, by, bw, atl, km,
    pts, ptb, pcs, pcb, own0, own1, vb0, vb1, r0l, q0l,
    o1, o2, kr, krb, kq, ucs, ucb, wcs, wcb,
    sa_s, sa, sb_s, sb, ra_s, ra, rb_s, rb, qa_s, qa, qb_s, qb,
    hb0, hb1, isem, ssem, rsem,
):
    t, c = lax.axis_index("train"), lax.axis_index("cand")
    y_hi, z, core = t // 16, lax.rem(t, 16) // 2, lax.rem(t, 2)
    h = y_hi * 2 + core
    q = h * NC + c

    def plane_peer(k):
        other = lax.rem(q + k, NP)
        oh, oc = other // NC, lax.rem(other, NC)
        return ((oh // 2) * 16 + z * 2 + lax.rem(oh, 2), oc)

    def line_index(k):
        return lax.rem(z + k, NZ)

    def line_peer(k):
        return (y_hi * 16 + line_index(k) * 2 + core, c)

    def cand_index(k):
        return lax.rem(c + k, NC)

    def cand_peer(k):
        return (t, cand_index(k))

    def block_peer(k):
        oh = lax.rem(h + k, NH)
        return ((oh // 2) * 16 + z * 2 + lax.rem(oh, 2), c)

    feat = pl.ds(pl.multiple_of(c * FEATS, FEATS), FEATS)
    inputs = [
        pltpu.make_async_copy(source, target, isem.at[number])
        for number, (source, target) in enumerate(
            (
                (xt_hbm, xt),
                (om_hbm.at[:, feat], om),
                (ph_hbm.at[:, feat], ph),
                (pw_hbm, pw.at[pl.ds(0, OWN)]),
                (pw_hbm, pw.at[pl.ds(OWN, OWN)]),
                (xc_hbm, xc),
                (tg_hbm, tg),
                (nz_hbm, nz),
            )
        )
    ]
    for copy in inputs:
        copy.start()

    barrier = pltpu.get_barrier_semaphore()

    def greet(peer, count):
        def one(k, carry):
            pl.semaphore_signal(barrier, inc=1, device_id=peer(k), device_id_type=MESH)
            return carry

        lax.fori_loop(1, count, one, 0)

    greet(plane_peer, NP)
    greet(line_peer, NZ)

    def push(phase, count, peer, source, target):
        def one(k, carry):
            pltpu.make_async_remote_copy(
                src_ref=source(k),
                dst_ref=target,
                send_sem=ssem.at[phase],
                recv_sem=rsem.at[phase],
                device_id=peer(k),
                device_id_type=MESH,
            ).start()
            return carry

        lax.fori_loop(1, count, one, 0)

    def settle(phase, sems, buf):
        ref = buf.at[pl.ds(0, buf.shape[0] - 1)]
        pltpu.make_async_copy(ref, ref, sems.at[phase]).wait()

    def arrived(phase, buf):
        settle(phase, rsem, buf)

    lane = lax.broadcasted_iota(jnp.int32, (1, 128), 1)
    low = lane < 64

    def swap(value):
        return pltpu.roll(value, 64, 1)

    def pair(first, second):
        return jnp.where(low, first, swap(second))

    def fold(value):
        row = jnp.sum(value, axis=0, keepdims=True)
        return row + swap(row)

    for copy in inputs[:5]:
        copy.wait()

    turn = 1.0 / (2.0 * math.pi)
    zero = jnp.zeros((1, FEATS), F32)
    bw[...] = right_side(om[...] * turn, rows8(zero, zero, zero, *split3(ph[...] * turn)))
    def prior_share(left):
        turns = jnp.dot(left, bw[...], preferred_element_type=F32)
        part = turns - jnp.floor(turns + 0.5)
        square = part * part
        value = jnp.full(square.shape, COS[-1], F32)
        for coefficient in COS[-2::-1]:
            value = value * square + coefficient
        packed = (value * math.sqrt(2.0 / TOTAL_FEATS)).astype(BF16)
        return lax.dot_general(
            packed, pw[...], (((1,), (1,)), ((), ())), preferred_element_type=F32
        )

    out = prior_share(left_side(xt[...]))
    for i in range(NC):
        pts[i] = jnp.where(low, out[64 * i : 64 * i + 32], out[64 * i + 32 : 64 * i + 64])

    for copy in inputs[5:]:
        copy.wait()

    mine = xt[:, pl.ds(pl.multiple_of((c // 2) * 128, 128), 128)]
    mine = jnp.where(lax.rem(c, 2) == 1, swap(mine), mine)
    xls[...] = mine
    xl[z] = mine
    xp[h] = xt[...]
    cand = xc[:, pl.ds(pl.multiple_of((t // 4) * 128, 128), 128)]
    cand = pltpu.roll(cand, lax.rem(128 - lax.rem(t, 4) * 32, 128), 1)
    xcs[...] = cand
    xcb[c] = cand

    pl.semaphore_wait(barrier, NP - 1 + NZ - 1)
    push(3, NC, cand_peer, lambda k: pts.at[cand_index(k)], ptb.at[c])
    push(0, NH, block_peer, lambda k: xt, xp.at[h])
    push(1, NZ, line_peer, lambda k: xls, xl.at[z])
    push(2, NC, cand_peer, lambda k: xcs, xcb.at[c])
    ptb[c] = pts[c]

    row = tg[...]
    place = lax.broadcasted_iota(jnp.int32, (32, 64), 0)
    at = lax.broadcasted_iota(jnp.int32, (32, 64), 1)
    upper = jnp.sum(jnp.where(at == place, row, 0.0), axis=1, keepdims=True)
    lower = jnp.sum(jnp.where(at == place + 32, row, 0.0), axis=1, keepdims=True)
    noise = jnp.concatenate([nz[0:32, :], nz[32:64, :]], axis=1)
    base = jnp.where(low, upper, lower) - noise

    def line_cands(j):
        tile = xc[:, pl.ds(pl.multiple_of(y_hi * 512 + j * 128, 128), 128)]
        tile = pltpu.roll(tile, lax.rem(128 - core * 32, 128), 1)
        return jnp.where(lane < 32, tile, pltpu.roll(tile, 96, 1))

    for j in range(2):
        atl[512 + j * 128 : 640 + j * 128, :] = left_side(
            pair(line_cands(2 * j), line_cands(2 * j + 1))
        )

    arrived(0, xp)
    for i in range(NH):
        uppers, lowers = [], []
        for j in range(2):
            tiles = [xp[i, :, j * 256 + 128 * g : j * 256 + 128 * g + 128] for g in range(2)]
            uppers.append(pair(*[jnp.where(lane < 32, a, pltpu.roll(a, 96, 1)) for a in tiles]))
            lowers.append(
                pair(*[jnp.where(lane < 32, pltpu.roll(a, 96, 1), swap(a)) for a in tiles])
            )
        for start, tiles in ((i * 256, uppers), (1024 + i * 256, lowers)):
            points = jnp.concatenate(tiles, axis=1)
            ones = jnp.ones((1, 256), F32)
            tail = rows8(ones, ones, ones, *split3(half_norm(points)))
            by[:, start : start + 256] = right_side(points, tail)

    def entries(first, count):
        rows = pl.ds(first, count)
        power = jnp.dot(atl[rows, :], by[...], preferred_element_type=F32)
        km[rows, :] = jnp.exp(power).astype(BF16)

    arrived(3, ptb)
    r0 = base - jnp.sum(ptb[...], axis=0)
    own0[...] = r0
    r0l[z] = r0
    hb0[...] = r0.astype(BF16)
    vb0[q] = r0.astype(BF16)
    push(4, NP, plane_peer, lambda k: hb0, vb0.at[q])
    push(5, NZ, line_peer, lambda k: own0, r0l.at[z])
    rr_own = fold(r0 * r0)

    arrived(1, xl)
    for j in range(4):
        atl[j * 128 : j * 128 + 128, :] = left_side(pair(xl[2 * j], xl[2 * j + 1]))
    entries(0, 512)
    entries(512, 256)

    def multiply(first, count, field):
        rows = pl.ds(first, count)
        values = field[...].reshape(NP * 32, 128)
        o1[rows, :] = jnp.dot(km[rows, 0:1024], values, preferred_element_type=F32)
        o2[rows, :] = jnp.dot(km[rows, 1024:2048], values, preferred_element_type=F32)

    def joined(first, size):
        a1, b1 = o1[pl.ds(first, size), :], o1[pl.ds(first + size, size), :]
        a2, b2 = o2[pl.ds(first, size), :], o2[pl.ds(first + size, size), :]
        return jnp.where(low, a1, b2) + swap(jnp.where(low, b1, a2))

    def train_product(pieces, field):
        multiply(0, 512, field)
        for i in range(NZ):
            pieces[i] = joined(i * 64, 32)

    def cand_product(pieces, field):
        multiply(512, 256, field)
        for i in range(NZ):
            pieces[i] = joined(512 + i * 32, 16)

    def ratio(part):
        other = swap(part)
        norms = jnp.where(low, other, part)
        return norms, jnp.where(low, part, other) / norms + NOISE_LEVEL

    arrived(4, vb0)
    train_product(kr, vb0)
    push(7, NZ, line_peer, lambda k: kr.at[line_index(k)], krb.at[z])
    arrived(5, r0l)
    curve = fold(jnp.sum(kr[...] * r0l[...], axis=0))
    part = jnp.where(low, curve, rr_own)
    sa_s[...] = part
    sa[q] = part
    push(8, NP, plane_peer, lambda k: sa_s, sa.at[q])
    krb[z] = kr[z]
    cand_product(ucs, vb0)

    arrived(2, xcb)
    tiles = []
    for j in range(2):
        tile = xcb[4 * j]
        for g in range(1, 4):
            tile = jnp.where(lane < 32 * g, tile, pltpu.roll(xcb[4 * j + g], 32 * g, 1))
        tiles.append(tile)
    out = prior_share(left_side(jnp.concatenate(tiles, axis=1)))
    for i in range(NC):
        pcs[i] = jnp.where(low, out[32 * i : 32 * i + 16], out[32 * i + 16 : 32 * i + 32])
    pcb[c] = pcs[c]

    arrived(8, sa)
    part = jnp.sum(sa[...], axis=0)
    sb_s[...] = part
    sb[z] = part
    push(10, NZ, line_peer, lambda k: sb_s, sb.at[z])
    share = ratio(part)[1]
    arrived(7, krb)
    r0 = own0[...]
    image = jnp.sum(krb[...], axis=0) + NOISE_LEVEL * r0

    own1[...] = image
    q0l[z] = image
    high = (image - share * r0).astype(BF16)
    hb1[...] = high
    vb1[q] = high
    push(11, NP, plane_peer, lambda k: hb1, vb1.at[q])
    push(12, NZ, line_peer, lambda k: own1, q0l.at[z])
    arrived(10, sb)
    rr0, quotient = ratio(jnp.sum(sb[...], axis=0))
    alpha1 = 1.0 / quotient
    r1 = r0 - alpha1 * image
    rr1_own = fold(r1 * r1)
    ra_s[...] = rr1_own
    ra[q] = rr1_own
    push(13, NP, plane_peer, lambda k: ra_s, ra.at[q])
    push(9, NZ, line_peer, lambda k: ucs.at[line_index(k)], ucb.at[z])
    ucb[z] = ucs[z]
    push(6, NC, cand_peer, lambda k: pcs.at[cand_index(k)], pcb.at[c])
    mixed_own = fold(r0 * r1)
    arrived(11, vb1)
    train_product(kq, vb1)
    arrived(12, q0l)
    r1l = r0l[...] - alpha1 * q0l[...]
    k1 = (1.0 - alpha1 * share) * kr[...] - alpha1 * kq[...]
    curve = fold(jnp.sum(r1l * k1, axis=0)) + NOISE_LEVEL * rr1_own
    mixed = fold(jnp.sum(r0l[...] * k1 + r1l * kr[...], axis=0)) + 2.0 * NOISE_LEVEL * mixed_own
    part = jnp.where(low, curve, mixed)
    qa_s[...] = part
    qa[q] = part
    push(16, NP, plane_peer, lambda k: qa_s, qa.at[q])
    arrived(13, ra)
    part = jnp.sum(ra[...], axis=0)
    rb_s[...] = part
    rb[z] = part
    push(14, NZ, line_peer, lambda k: rb_s, rb.at[z])
    cand_product(wcs, vb1)
    wcs[...] = wcs[...] + share * ucs[...]
    push(15, NZ, line_peer, lambda k: wcs.at[line_index(k)], wcb.at[z])
    wcb[z] = wcs[z]
    arrived(16, qa)
    part = jnp.sum(qa[...], axis=0)
    qb_s[...] = part
    qb[z] = part
    push(17, NZ, line_peer, lambda k: qb_s, qb.at[z])
    arrived(6, pcb)
    prior = jnp.sum(pcb[...], axis=0)
    arrived(9, ucb)
    first_part = jnp.sum(ucb[...], axis=0)
    arrived(14, rb)
    rr1 = jnp.sum(rb[...], axis=0)
    beta = rr1 / rr0
    arrived(15, wcb)
    second_part = first_part - alpha1 * jnp.sum(wcb[...], axis=0)
    r0 = own0[...]
    r1 = r0 - alpha1 * own1[...]
    d1 = r1 + beta * r0
    arrived(17, qb)
    part = jnp.sum(qb[...], axis=0)
    other = swap(part)
    curve, mixed = jnp.where(low, part, other), jnp.where(low, other, part)
    alpha2 = rr1 / (curve + beta * (mixed + beta * (rr0 / alpha1)))

    result = alpha1 * r0 + alpha2 * d1
    sol[0:32, :] = result[:, 0:64]
    sol[32:64, :] = swap(result)[:, 0:64]
    result = prior + (alpha1 + alpha2 * beta) * first_part + alpha2 * second_part
    sam[0:16, :] = result[:, 0:64]
    sam[16:32, :] = swap(result)[:, 0:64]

    for phase, buf in enumerate(
        (xp, xl, xcb, ptb, vb0, r0l, pcb, krb, sa, ucb, sb, vb1, q0l, ra, rb, wcb, qa, qb)
    ):
        settle(phase, ssem, buf)


def body(x_train, x_cand, targets, noise, omega, phase, prior_weights):
    vmem = pltpu.VMEM
    field = lambda n, rows, dtype=F32: vmem((n, rows, 128), dtype)
    tile, row = vmem((8, 128), F32), vmem((1, 128), F32)
    scratch = [
        vmem((8, 512), F32), vmem((8, 1024), F32), vmem((1, OWN), F32), vmem((OWN, OWN), F32),
        vmem((8, FEATS), F32), vmem((1, FEATS), F32), vmem((2 * OWN, FEATS), BF16),
        tile, field(NZ, 8), tile, field(NC, 8), vmem((NH, 8, 512), F32),
        vmem((128, 2048), BF16), vmem((128, FEATS), BF16), vmem((768, 128), BF16), vmem((768, 2048), BF16),
        field(NC, 32), field(NC, 32), field(NC, 16), field(NC, 16),
        vmem((32, 128), F32), vmem((32, 128), F32),
        field(NP, 32, BF16), field(NP, 32, BF16),
        field(NZ, 32), field(NZ, 32),
        vmem((768, 128), F32), vmem((768, 128), F32),
        field(NZ, 32), field(NZ, 32), field(NZ, 32),
        field(NZ, 16), field(NZ, 16), field(NZ, 16), field(NZ, 16),
        row, field(NP, 1), row, field(NZ, 1), row, field(NP, 1), row, field(NZ, 1),
        row, field(NP, 1), row, field(NZ, 1),
        vmem((32, 128), BF16), vmem((32, 128), BF16),
        pltpu.SemaphoreType.DMA((8,)), pltpu.SemaphoreType.DMA((18,)),
        pltpu.SemaphoreType.DMA((18,)),
    ]
    return pl.pallas_call(
        kernel,
        out_shape=(
            jax.ShapeDtypeStruct((CANDS, OWN), F32),
            jax.ShapeDtypeStruct((OWN, OWN), F32),
        ),
        in_specs=[pl.BlockSpec(memory_space=pltpu.HBM)] * 7,
        out_specs=(pl.BlockSpec(memory_space=vmem),) * 2,
        scratch_shapes=scratch,
        compiler_params=pltpu.CompilerParams(
            collective_id=0, has_side_effects=True, vmem_limit_bytes=64 * 1024 * 1024
        ),
    )(
        x_train, x_cand, targets.reshape(1, OWN), noise, omega,
        phase.reshape(1, TOTAL_FEATS), prior_weights.T,
    )


def solution(mesh):
    placed = (
        P(None, "train"),
        P(None, "cand"),
        P(("train", "cand")),
        P(("train", "cand"), None),
        P(),
        P(),
        P("cand", None),
    )
    return jax.shard_map(
        body,
        mesh=mesh,
        in_specs=placed,
        out_specs=(P(("cand", "train"), None), P(("train", "cand"), None)),
        check_vma=False,
    )
```

```python
import math

import jax
import jax.numpy as jnp
from jax import lax
from jax.experimental import pallas as pl
from jax.experimental.pallas import tpu as pltpu
from jax.sharding import PartitionSpec as P

MESH = pl.DeviceIdType.MESH
F32, BF16 = jnp.float32, jnp.bfloat16
NZ, NC, NH = 8, 8, 4
NP = NH * NC
OWN = 64
CANDS = 32
FEATS = 512
TOTAL_FEATS = 4096
NOISE_LEVEL = 0.5
COS = (
    0.9999999890590217,
    -19.73920449945381,
    64.93911745989173,
    -85.45013953082398,
    60.16763095051855,
    -25.967599246994247,
    6.528658159389057,
)


def split3(value):
    one = value.astype(BF16).astype(F32)
    two = (value - one).astype(BF16).astype(F32)
    return one, two, value - one - two


def rows8(*rows):
    index = lax.broadcasted_iota(jnp.int32, (8, rows[0].shape[1]), 0)
    out = jnp.zeros((8, rows[0].shape[1]), F32)
    for place, row in enumerate(rows):
        out = jnp.where(index == place, row, out)
    return out


def half_norm(points):
    return -0.5 * jnp.sum(points * points, axis=0, keepdims=True)


def left_side(points):
    one, two, three = split3(points)
    ones = jnp.ones((1, points.shape[1]), F32)
    tail = rows8(*split3(half_norm(points)), ones, ones, ones)
    pad = jnp.zeros((72, points.shape[1]), F32)
    return jnp.concatenate([one, one, two, two, one, three, tail, pad], axis=0).T.astype(BF16)


def right_side(points, tail):
    one, two, three = split3(points)
    pad = jnp.zeros((72, points.shape[1]), F32)
    return jnp.concatenate([one, two, one, two, three, one, tail, pad], axis=0).astype(BF16)


def kernel(
    xt_hbm, xc_hbm, tg_hbm, nz_hbm, om_hbm, ph_hbm, pw_hbm, sam, sol,
    xt, xc, tg, nz, om, ph, pw,
    xls, xl, xcs, xcb, xp, by, bw, atl, km,
    pts, ptb, pcs, pcb, own0, own1, vb0, vb1, r0l, q0l,
    o1, o2, kr, krb, kq, ucs, ucb, wcs, wcb,
    sa_s, sa, sb_s, sb, ra_s, ra, rb_s, rb, qa_s, qa, qb_s, qb,
    hb0, hb1, isem, ssem, rsem,
):
    t, c = lax.axis_index("train"), lax.axis_index("cand")
    y_hi, z, core = t // 16, lax.rem(t, 16) // 2, lax.rem(t, 2)
    h = y_hi * 2 + core
    q = h * NC + c

    x, y = c // 2, y_hi * 2 + lax.rem(c, 2)

    ys = [lax.rem(y + k, 4) for k in range(4)]
    xs = [lax.rem(x + k, 4) for k in range(4)]
    cores = [core, 1 - core]
    hops = lambda k, n: min(k, n - k)

    def device(dx, dy, dz, dcore):
        other_z = z if dz == 0 else lax.rem(z + dz, NZ)
        return (
            (ys[dy] // 2) * 16 + other_z * 2 + cores[dcore],
            xs[dx] * 2 + lax.rem(ys[dy], 2),
        )

    def ranked(group):
        return sorted(group, key=lambda d: -(hops(d[0], 4) + hops(d[1], 4) + hops(d[2], NZ)))

    plane = [
        device(*d)
        for d in ranked((i, j, 0, k) for i in range(4) for j in range(4) for k in range(2))
        if d != (0, 0, 0, 0)
    ]
    plane = [(peer, None) for peer in plane]
    line = [
        (device(0, 0, k, 0), lax.rem(z + k, NZ)) for k in (4, 3, 5, 2, 6, 1, 7)
    ]
    cands = [
        ((t, xs[i] * 2 + lax.rem(y + j, 2)), xs[i] * 2 + lax.rem(y + j, 2))
        for i, j in ((2, 1), (2, 0), (1, 1), (3, 1), (1, 0), (3, 0), (0, 1))
    ]
    blocks = [(device(0, j, 0, k), None) for j, k in ((2, 1), (2, 0), (0, 1))]

    feat = pl.ds(pl.multiple_of(c * FEATS, FEATS), FEATS)
    inputs = [
        pltpu.make_async_copy(source, target, isem.at[number])
        for number, (source, target) in enumerate(
            (
                (xt_hbm, xt),
                (om_hbm.at[:, feat], om),
                (ph_hbm.at[:, feat], ph),
                (pw_hbm, pw.at[pl.ds(0, OWN)]),
                (pw_hbm, pw.at[pl.ds(OWN, OWN)]),
                (xc_hbm, xc),
                (tg_hbm, tg),
                (nz_hbm, nz),
            )
        )
    ]
    for copy in inputs:
        copy.start()

    barrier = pltpu.get_barrier_semaphore()

    for peer, _ in plane + line:
        pl.semaphore_signal(barrier, inc=1, device_id=peer, device_id_type=MESH)

    def push(phase, peers, source, target):
        for peer, index in peers:
            pltpu.make_async_remote_copy(
                src_ref=source if index is None else source(index),
                dst_ref=target,
                send_sem=ssem.at[phase],
                recv_sem=rsem.at[phase],
                device_id=peer,
                device_id_type=MESH,
            ).start()

    def settle(phase, sems, buf):
        ref = buf.at[pl.ds(0, buf.shape[0] - 1)]
        pltpu.make_async_copy(ref, ref, sems.at[phase]).wait()

    def arrived(phase, buf):
        settle(phase, rsem, buf)

    lane = lax.broadcasted_iota(jnp.int32, (1, 128), 1)
    low = lane < 64

    def swap(value):
        return pltpu.roll(value, 64, 1)

    def pair(first, second):
        return jnp.where(low, first, swap(second))

    def fold(value):
        row = jnp.sum(value, axis=0, keepdims=True)
        return row + swap(row)

    for copy in inputs[:5]:
        copy.wait()

    turn = 1.0 / (2.0 * math.pi)
    zero = jnp.zeros((1, FEATS), F32)
    bw[...] = right_side(om[...] * turn, rows8(zero, zero, zero, *split3(ph[...] * turn)))
    def prior_share(left):
        turns = jnp.dot(left, bw[...], preferred_element_type=F32)
        part = turns - jnp.floor(turns + 0.5)
        square = part * part
        value = jnp.full(square.shape, COS[-1], F32)
        for coefficient in COS[-2::-1]:
            value = value * square + coefficient
        packed = (value * math.sqrt(2.0 / TOTAL_FEATS)).astype(BF16)
        return lax.dot_general(
            packed, pw[...], (((1,), (1,)), ((), ())), preferred_element_type=F32
        )

    out = prior_share(left_side(xt[...]))
    for i in range(NC):
        pts[i] = jnp.where(low, out[64 * i : 64 * i + 32], out[64 * i + 32 : 64 * i + 64])

    pl.semaphore_wait(barrier, NP - 1 + NZ - 1)
    push(3, cands, lambda i: pts.at[i], ptb.at[c])
    for copy in inputs[5:]:
        copy.wait()

    mine = xt[:, pl.ds(pl.multiple_of((c // 2) * 128, 128), 128)]
    mine = jnp.where(lax.rem(c, 2) == 1, swap(mine), mine)
    xls[...] = mine
    xl[z] = mine
    xp[h] = xt[...]
    cand = xc[:, pl.ds(pl.multiple_of((t // 4) * 128, 128), 128)]
    cand = pltpu.roll(cand, lax.rem(128 - lax.rem(t, 4) * 32, 128), 1)
    xcs[...] = cand
    xcb[c] = cand
    push(0, blocks, xt, xp.at[h])
    push(1, line, lambda i: xls, xl.at[z])
    push(2, cands, lambda i: xcs, xcb.at[c])
    ptb[c] = pts[c]

    row = tg[...]
    place = lax.broadcasted_iota(jnp.int32, (32, 64), 0)
    at = lax.broadcasted_iota(jnp.int32, (32, 64), 1)
    upper = jnp.sum(jnp.where(at == place, row, 0.0), axis=1, keepdims=True)
    lower = jnp.sum(jnp.where(at == place + 32, row, 0.0), axis=1, keepdims=True)
    noise = jnp.concatenate([nz[0:32, :], nz[32:64, :]], axis=1)
    base = jnp.where(low, upper, lower) - noise

    def line_cands(j):
        tile = xc[:, pl.ds(pl.multiple_of(y_hi * 512 + j * 128, 128), 128)]
        tile = pltpu.roll(tile, lax.rem(128 - core * 32, 128), 1)
        return jnp.where(lane < 32, tile, pltpu.roll(tile, 96, 1))

    for j in range(2):
        atl[512 + j * 128 : 640 + j * 128, :] = left_side(
            pair(line_cands(2 * j), line_cands(2 * j + 1))
        )

    arrived(0, xp)
    for i in range(NH):
        uppers, lowers = [], []
        for j in range(2):
            tiles = [xp[i, :, j * 256 + 128 * g : j * 256 + 128 * g + 128] for g in range(2)]
            uppers.append(pair(*[jnp.where(lane < 32, a, pltpu.roll(a, 96, 1)) for a in tiles]))
            lowers.append(
                pair(*[jnp.where(lane < 32, pltpu.roll(a, 96, 1), swap(a)) for a in tiles])
            )
        for start, tiles in ((i * 256, uppers), (1024 + i * 256, lowers)):
            points = jnp.concatenate(tiles, axis=1)
            ones = jnp.ones((1, 256), F32)
            tail = rows8(ones, ones, ones, *split3(half_norm(points)))
            by[:, start : start + 256] = right_side(points, tail)

    def entries(first, count):
        rows = pl.ds(first, count)
        power = jnp.dot(atl[rows, :], by[...], preferred_element_type=F32)
        km[rows, :] = jnp.exp(power).astype(BF16)

    arrived(3, ptb)
    r0 = base - jnp.sum(ptb[...], axis=0)
    own0[...] = r0
    r0l[z] = r0
    hb0[...] = r0.astype(BF16)
    vb0[q] = r0.astype(BF16)
    push(4, plane, hb0, vb0.at[q])
    push(5, line, lambda i: own0, r0l.at[z])
    rr_own = fold(r0 * r0)

    arrived(1, xl)
    for j in range(4):
        atl[j * 128 : j * 128 + 128, :] = left_side(pair(xl[2 * j], xl[2 * j + 1]))
    entries(0, 512)
    entries(512, 256)

    def multiply(first, count, field):
        rows = pl.ds(first, count)
        values = field[...].reshape(NP * 32, 128)
        o1[rows, :] = jnp.dot(km[rows, 0:1024], values, preferred_element_type=F32)
        o2[rows, :] = jnp.dot(km[rows, 1024:2048], values, preferred_element_type=F32)

    def joined(first, size):
        a1, b1 = o1[pl.ds(first, size), :], o1[pl.ds(first + size, size), :]
        a2, b2 = o2[pl.ds(first, size), :], o2[pl.ds(first + size, size), :]
        return jnp.where(low, a1, b2) + swap(jnp.where(low, b1, a2))

    def train_product(pieces, field):
        multiply(0, 512, field)
        for i in range(NZ):
            pieces[i] = joined(i * 64, 32)

    def cand_product(pieces, field):
        multiply(512, 256, field)
        for i in range(NZ):
            pieces[i] = joined(512 + i * 32, 16)

    def ratio(part):
        other = swap(part)
        norms = jnp.where(low, other, part)
        return norms, jnp.where(low, part, other) / norms + NOISE_LEVEL

    arrived(4, vb0)
    train_product(kr, vb0)
    push(7, line, lambda i: kr.at[i], krb.at[z])
    arrived(5, r0l)
    curve = fold(jnp.sum(kr[...] * r0l[...], axis=0))
    part = jnp.where(low, curve, rr_own)
    sa_s[...] = part
    sa[q] = part
    push(8, plane, sa_s, sa.at[q])
    krb[z] = kr[z]
    cand_product(ucs, vb0)

    arrived(2, xcb)
    tiles = []
    for j in range(2):
        tile = xcb[4 * j]
        for g in range(1, 4):
            tile = jnp.where(lane < 32 * g, tile, pltpu.roll(xcb[4 * j + g], 32 * g, 1))
        tiles.append(tile)
    out = prior_share(left_side(jnp.concatenate(tiles, axis=1)))
    for i in range(NC):
        pcs[i] = jnp.where(low, out[32 * i : 32 * i + 16], out[32 * i + 16 : 32 * i + 32])
    pcb[c] = pcs[c]

    arrived(8, sa)
    part = jnp.sum(sa[...], axis=0)
    sb_s[...] = part
    sb[z] = part
    push(10, line, lambda i: sb_s, sb.at[z])
    norms, quotient = ratio(part)
    share = jnp.where(norms > 0.0, quotient, 0.0)
    arrived(7, krb)
    r0 = own0[...]
    image = jnp.sum(krb[...], axis=0) + NOISE_LEVEL * r0

    own1[...] = image
    q0l[z] = image
    high = (image - share * r0).astype(BF16)
    hb1[...] = high
    vb1[q] = high
    push(11, plane, hb1, vb1.at[q])
    push(12, line, lambda i: own1, q0l.at[z])
    arrived(10, sb)
    rr0, quotient = ratio(jnp.sum(sb[...], axis=0))
    alpha1 = 1.0 / quotient
    r1 = r0 - alpha1 * image
    rr1_own = fold(r1 * r1)
    ra_s[...] = rr1_own
    ra[q] = rr1_own
    push(13, plane, ra_s, ra.at[q])
    push(9, line, lambda i: ucs.at[i], ucb.at[z])
    ucb[z] = ucs[z]
    push(6, cands, lambda i: pcs.at[i], pcb.at[c])
    mixed_own = fold(r0 * r1)
    arrived(11, vb1)
    train_product(kq, vb1)
    arrived(12, q0l)
    r1l = r0l[...] - alpha1 * q0l[...]
    k1 = (1.0 - alpha1 * share) * kr[...] - alpha1 * kq[...]
    curve = fold(jnp.sum(r1l * k1, axis=0)) + NOISE_LEVEL * rr1_own
    mixed = fold(jnp.sum(r0l[...] * k1 + r1l * kr[...], axis=0)) + 2.0 * NOISE_LEVEL * mixed_own
    part = jnp.where(low, curve, mixed)
    qa_s[...] = part
    qa[q] = part
    push(16, plane, qa_s, qa.at[q])
    arrived(13, ra)
    part = jnp.sum(ra[...], axis=0)
    rb_s[...] = part
    rb[z] = part
    push(14, line, lambda i: rb_s, rb.at[z])
    cand_product(wcs, vb1)
    wcs[...] = wcs[...] + share * ucs[...]
    push(15, line, lambda i: wcs.at[i], wcb.at[z])
    wcb[z] = wcs[z]
    arrived(16, qa)
    part = jnp.sum(qa[...], axis=0)
    qb_s[...] = part
    qb[z] = part
    push(17, line, lambda i: qb_s, qb.at[z])
    arrived(6, pcb)
    prior = jnp.sum(pcb[...], axis=0)
    arrived(9, ucb)
    first_part = jnp.sum(ucb[...], axis=0)
    arrived(14, rb)
    rr1 = jnp.sum(rb[...], axis=0)
    beta = rr1 / rr0
    arrived(15, wcb)
    second_part = first_part - alpha1 * jnp.sum(wcb[...], axis=0)
    r0 = own0[...]
    r1 = r0 - alpha1 * own1[...]
    d1 = r1 + beta * r0
    arrived(17, qb)
    part = jnp.sum(qb[...], axis=0)
    other = swap(part)
    curve, mixed = jnp.where(low, part, other), jnp.where(low, other, part)
    alpha2 = rr1 / (curve + beta * (mixed + beta * (rr0 / alpha1)))

    result = alpha1 * r0 + alpha2 * d1
    sol[0:32, :] = result[:, 0:64]
    sol[32:64, :] = swap(result)[:, 0:64]
    result = prior + (alpha1 + alpha2 * beta) * first_part + alpha2 * second_part
    sam[0:16, :] = result[:, 0:64]
    sam[16:32, :] = swap(result)[:, 0:64]

    for phase, buf in enumerate(
        (xp, xl, xcb, ptb, vb0, r0l, pcb, krb, sa, ucb, sb, vb1, q0l, ra, rb, wcb, qa, qb)
    ):
        settle(phase, ssem, buf)


def body(x_train, x_cand, targets, noise, omega, phase, prior_weights):
    vmem = pltpu.VMEM
    field = lambda n, rows, dtype=F32: vmem((n, rows, 128), dtype)
    tile, row = vmem((8, 128), F32), vmem((1, 128), F32)
    scratch = [
        vmem((8, 512), F32), vmem((8, 1024), F32), vmem((1, OWN), F32), vmem((OWN, OWN), F32),
        vmem((8, FEATS), F32), vmem((1, FEATS), F32), vmem((2 * OWN, FEATS), BF16),
        tile, field(NZ, 8), tile, field(NC, 8), vmem((NH, 8, 512), F32),
        vmem((128, 2048), BF16), vmem((128, FEATS), BF16), vmem((768, 128), BF16), vmem((768, 2048), BF16),
        field(NC, 32), field(NC, 32), field(NC, 16), field(NC, 16),
        vmem((32, 128), F32), vmem((32, 128), F32),
        field(NP, 32, BF16), field(NP, 32, BF16),
        field(NZ, 32), field(NZ, 32),
        vmem((768, 128), F32), vmem((768, 128), F32),
        field(NZ, 32), field(NZ, 32), field(NZ, 32),
        field(NZ, 16), field(NZ, 16), field(NZ, 16), field(NZ, 16),
        row, field(NP, 1), row, field(NZ, 1), row, field(NP, 1), row, field(NZ, 1),
        row, field(NP, 1), row, field(NZ, 1),
        vmem((32, 128), BF16), vmem((32, 128), BF16),
        pltpu.SemaphoreType.DMA((8,)), pltpu.SemaphoreType.DMA((18,)),
        pltpu.SemaphoreType.DMA((18,)),
    ]
    operands = (
        x_train, x_cand, targets.reshape(1, OWN), noise, omega,
        phase.reshape(1, TOTAL_FEATS), prior_weights.T,
    )
    return pl.pallas_call(
        kernel,
        out_shape=(
            jax.ShapeDtypeStruct((CANDS, OWN), F32),
            jax.ShapeDtypeStruct((OWN, OWN), F32),
        ),
        in_specs=[pl.BlockSpec(memory_space=pltpu.HBM)] * 7,
        out_specs=(pl.BlockSpec(memory_space=vmem),) * 2,
        scratch_shapes=scratch,
        compiler_params=pltpu.CompilerParams(
            collective_id=0, has_side_effects=True, vmem_limit_bytes=32 * 1024 * 1024
        ),
    )(*(pltpu.with_memory_space_constraint(value, pltpu.HBM) for value in operands))


def solution(mesh):
    placed = (
        P(None, "train"),
        P(None, "cand"),
        P(("train", "cand")),
        P(("train", "cand"), None),
        P(),
        P(),
        P("cand", None),
    )
    return jax.shard_map(
        body,
        mesh=mesh,
        in_specs=placed,
        out_specs=(P(("cand", "train"), None), P(("train", "cand"), None)),
        check_vma=False,
    )
```

```python
import math

import jax
import jax.numpy as jnp
from jax import lax
from jax.experimental import pallas as pl
from jax.experimental.pallas import tpu as pltpu
from jax.sharding import PartitionSpec as P

MESH = pl.DeviceIdType.MESH
F32, BF16 = jnp.float32, jnp.bfloat16
NZ, NC, NH = 8, 8, 4
NP = NH * NC
OWN = 64
CANDS = 32
FEATS = 512
TOTAL_FEATS = 4096
NOISE_LEVEL = 0.5
PLANE_ORDER = sorted(
    ((i, j, k) for i in range(4) for j in range(4) for k in range(2) if i + j + k),
    key=lambda d: -(min(d[0], 4 - d[0]) + min(d[1], 4 - d[1])),
)
LINE_ORDER = (4, 3, 5, 2, 6, 1, 7, 0)


def place_of(k):
    return LINE_ORDER.index(k % NZ)
SIN = (
    6.283185159611151,
    -41.3416549293423,
    81.60099819256979,
    -76.5496568198889,
    39.53581370662112,
)


def split3(value):
    one = value.astype(BF16).astype(F32)
    two = (value - one).astype(BF16).astype(F32)
    return one, two, value - one - two


def rows8(*rows):
    index = lax.broadcasted_iota(jnp.int32, (8, rows[0].shape[1]), 0)
    out = jnp.zeros((8, rows[0].shape[1]), F32)
    for place, row in enumerate(rows):
        out = jnp.where(index == place, row, out)
    return out


def half_norm(points):
    return -0.5 * jnp.sum(points * points, axis=0, keepdims=True)


def left_side(points):
    one, two, three = split3(points)
    ones = jnp.ones((1, points.shape[1]), F32)
    tail = rows8(*split3(half_norm(points)), ones, ones, ones)
    pad = jnp.zeros((72, points.shape[1]), F32)
    return jnp.concatenate([one, one, two, two, one, three, tail, pad], axis=0).T.astype(BF16)


def right_side(points, tail):
    one, two, three = split3(points)
    pad = jnp.zeros((72, points.shape[1]), F32)
    return jnp.concatenate([one, two, one, two, three, one, tail, pad], axis=0).astype(BF16)


def kernel(
    xt_hbm, xc_hbm, tg_hbm, nz_hbm, om_hbm, ph_hbm, pw_hbm, packed,
    xt, xc, tg, nz, om, ph, pw,
    xls, xl, xcs, xcb, xp, by, bw, atl, km,
    pts, ptb, pcs, pcb, own0, own1, vb0, vb1, r0l, q0l,
    o1, o2, kr, krb, kq, ucs, ucb, wcs, wcb,
    sa_s, sa, sb_s, sb, ra_s, ra, rb_s, rb, qa_s, qa, qb_s, qb,
    hb0, hb1, isem, ssem, rsem,
):
    t, c = lax.axis_index("train"), lax.axis_index("cand")
    y_hi, z, core = t // 16, lax.rem(t, 16) // 2, lax.rem(t, 2)
    h = y_hi * 2 + core
    q = h * NC + c

    x, y = c // 2, y_hi * 2 + lax.rem(c, 2)

    y_lo = lax.rem(c, 2)
    ys = [lax.rem(y + k, 4) for k in range(4)]
    xs = [lax.rem(x + k, 4) for k in range(4)]
    zs = [lax.rem(z + k, NZ) for k in range(NZ)]
    cores = [core, 1 - core]

    def device(dx, dy, dz, dcore):
        return (
            (ys[dy] // 2) * 16 + zs[dz] * 2 + cores[dcore],
            xs[dx] * 2 + lax.rem(ys[dy], 2),
        )

    plane = [(device(i, j, 0, k), i) for i, j, k in PLANE_ORDER]
    line = [(device(0, 0, k, 0), k) for k in LINE_ORDER[:-1]]
    blocks = [(device(0, j, 0, k), None) for j, k in ((2, 1), (2, 0), (0, 1))]
    near = 1 - y_lo
    cands = [
        ((t, xs[i] * 2 + j), (i, j))
        for i, j in ((2, 0), (2, 1), (1, 0), (1, 1), (3, 0), (3, 1), (0, near))
    ]
    sub = h * 2 + y_lo

    feat = pl.ds(pl.multiple_of(c * FEATS, FEATS), FEATS)
    inputs = [
        pltpu.make_async_copy(source, target, isem.at[number])
        for number, (source, target) in enumerate(
            (
                (xt_hbm, xt),
                (om_hbm.at[:, feat], om),
                (ph_hbm.at[:, feat], ph),
                (pw_hbm, pw.at[pl.ds(0, OWN)]),
                (pw_hbm, pw.at[pl.ds(OWN, OWN)]),
                (xc_hbm, xc),
                (tg_hbm, tg),
                (nz_hbm, nz),
            )
        )
    ]
    barrier = pltpu.get_barrier_semaphore()
    for copy in inputs[:5]:
        copy.start()
    for peer, _ in plane + line:
        pl.semaphore_signal(barrier, inc=1, device_id=peer, device_id_type=MESH)
    for copy in inputs[5:]:
        copy.start()

    def push(phase, peers, source, target):
        for peer, tag in peers:
            number = phase(tag) if callable(phase) else phase
            pltpu.make_async_remote_copy(
                src_ref=source(tag) if callable(source) else source,
                dst_ref=target(tag) if callable(target) else target,
                send_sem=ssem.at[number],
                recv_sem=rsem.at[number],
                device_id=peer,
                device_id_type=MESH,
            ).start()

    def settle(phase, sems, buf, count=None):
        ref = buf.at[pl.ds(0, count or buf.shape[0] - 1)]
        pltpu.make_async_copy(ref, ref, sems.at[phase]).wait()

    def arrived(phase, buf, count=None):
        settle(phase, rsem, buf, count)

    def gather(base, source, target):
        push(lambda i: base + -i % 4, plane, source, lambda i: target.at[(-i % 4) * 8 + sub])

    lane = lax.broadcasted_iota(jnp.int32, (1, 128), 1)
    low = lane < 64

    def swap(value):
        return pltpu.roll(value, 64, 1)

    def pair(first, second):
        return jnp.where(low, first, swap(second))

    def fold(value):
        row = jnp.sum(value, axis=0, keepdims=True)
        return row + swap(row)

    for copy in inputs[:5]:
        copy.wait()

    turn = 1.0 / (2.0 * math.pi)
    zero = jnp.zeros((1, FEATS), F32)
    bw[...] = right_side(om[...] * turn, rows8(zero, zero, zero, *split3(ph[...] * turn)))
    def prior_share(left):
        turns = jnp.dot(left, bw[...], preferred_element_type=F32)
        wave = jnp.abs(turns - jnp.floor(turns) - 0.5) - 0.25
        square = wave * wave
        scale = math.sqrt(2.0 / TOTAL_FEATS)
        value = square * (SIN[-1] * scale) + SIN[-2] * scale
        for coefficient in SIN[-3::-1]:
            value = value * square + coefficient * scale
        packed = (value * wave).astype(BF16)
        return lax.dot_general(
            packed, pw[...], (((1,), (1,)), ((), ())), preferred_element_type=F32
        )

    out = prior_share(left_side(xt[...]))
    for i in range(NC):
        pts[i] = jnp.where(low, out[64 * i : 64 * i + 32], out[64 * i + 32 : 64 * i + 64])
    pl.semaphore_wait(barrier, NP - 1 + NZ - 1)
    push(3, cands, lambda tag: pts.at[xs[tag[0]] * 2 + tag[1]], ptb.at[c])
    for copy in inputs[5:]:
        copy.wait()

    mine = xt[:, pl.ds(pl.multiple_of((c // 2) * 128, 128), 128)]
    mine = jnp.where(lax.rem(c, 2) == 1, swap(mine), mine)
    xls[...] = mine
    xl[place_of(0)] = mine
    xp[h] = xt[...]
    cand = xc[:, pl.ds(pl.multiple_of((t // 4) * 128, 128), 128)]
    cand = pltpu.roll(cand, lax.rem(128 - lax.rem(t, 4) * 32, 128), 1)
    xcs[...] = cand
    xcb[c] = cand
    push(0, blocks, xt, xp.at[h])
    push(1, line, xls, lambda k: xl.at[place_of(-k)])
    push(2, cands, xcs, xcb.at[c])
    ptb[c] = pts[c]

    row = tg[...]
    place = lax.broadcasted_iota(jnp.int32, (32, 64), 0)
    at = lax.broadcasted_iota(jnp.int32, (32, 64), 1)
    upper = jnp.sum(jnp.where(at == place, row, 0.0), axis=1, keepdims=True)
    lower = jnp.sum(jnp.where(at == place + 32, row, 0.0), axis=1, keepdims=True)
    noise = jnp.concatenate([nz[0:32, :], nz[32:64, :]], axis=1)
    base = jnp.where(low, upper, lower) - noise

    def line_cands(j):
        tile = xc[:, pl.ds(pl.multiple_of(y_hi * 512 + j * 128, 128), 128)]
        tile = pltpu.roll(tile, lax.rem(128 - core * 32, 128), 1)
        return jnp.where(lane < 32, tile, pltpu.roll(tile, 96, 1))

    for j in range(2):
        atl[512 + j * 128 : 640 + j * 128, :] = left_side(
            pair(line_cands(2 * j), line_cands(2 * j + 1))
        )

    arrived(0, xp)
    for i in range(4):
        tiles = [xp[g, :, pl.ds(pl.multiple_of(xs[i] * 128, 128), 128)] for g in range(NH)]
        uppers = [jnp.where(lane < 32, a, pltpu.roll(a, 96, 1)) for a in tiles]
        lowers = [jnp.where(lane < 32, pltpu.roll(a, 96, 1), swap(a)) for a in tiles]
        for start, halves in ((i * 256, uppers), (1024 + i * 256, lowers)):
            points = jnp.concatenate([pair(*halves[:2]), pair(*halves[2:])], axis=1)
            ones = jnp.ones((1, 256), F32)
            tail = rows8(ones, ones, ones, *split3(half_norm(points)))
            by[:, start : start + 256] = right_side(points, tail)

    def entries(first, count):
        rows = pl.ds(first, count)
        power = jnp.dot(atl[rows, :], by[...], preferred_element_type=F32)
        km[rows, :] = jnp.exp(power).astype(BF16)

    arrived(3, ptb)
    r0 = base - jnp.sum(ptb[...], axis=0)
    own0[...] = r0
    r0l[place_of(0)] = r0
    hb0[...] = r0.astype(BF16)
    vb0[sub] = r0.astype(BF16)
    gather(18, hb0, vb0)
    push(5, line, own0, lambda k: r0l.at[place_of(-k)])
    rr_own = fold(r0 * r0)

    arrived(1, xl)
    for j in range(4):
        atl[j * 128 : j * 128 + 128, :] = left_side(pair(xl[2 * j], xl[2 * j + 1]))
    entries(0, 512)
    entries(512, 256)

    def group_product(first, count, field, i, fresh):
        rows = pl.ds(first, count)
        values = field[8 * i : 8 * i + 8].reshape(256, 128)
        for start, out in ((0, o1), (1024, o2)):
            term = jnp.dot(
                km[rows, start + 256 * i : start + 256 * i + 256],
                values,
                preferred_element_type=F32,
            )
            out[rows, :] = term if fresh else out[rows, :] + term

    def joined(first, size):
        a1, b1 = o1[pl.ds(first, size), :], o1[pl.ds(first + size, size), :]
        a2, b2 = o2[pl.ds(first, size), :], o2[pl.ds(first + size, size), :]
        return jnp.where(low, a1, b2) + swap(jnp.where(low, b1, a2))

    def train_product(pieces, base, field, ready):
        for i in range(4):
            arrived(base + i, field, 7 if i == 0 else 8)
        values = field[...].reshape(NP * 32, 128)
        for first in (0, 4):
            rows = pl.ds(64 * first, 256)
            o1[rows, :] = jnp.dot(km[rows, 0:1024], values, preferred_element_type=F32)
            o2[rows, :] = jnp.dot(km[rows, 1024:2048], values, preferred_element_type=F32)
            for k in range(first, first + 4):
                pieces[k] = joined(64 * k, 32)
            ready(first)

    def cand_product(pieces, field):
        values = field[...].reshape(NP * 32, 128)
        o1[512:768, :] = jnp.dot(km[512:768, 0:1024], values, preferred_element_type=F32)
        o2[512:768, :] = jnp.dot(km[512:768, 1024:2048], values, preferred_element_type=F32)
        for i in range(NZ):
            pieces[i] = joined(512 + i * 32, 16)

    def ratio(part):
        other = swap(part)
        norms = jnp.where(low, other, part)
        return norms, jnp.where(low, part, other) / norms + NOISE_LEVEL

    train_product(
        kr,
        18,
        vb0,
        lambda first: push(
            7, line[first : first + 4], lambda k: kr.at[place_of(k)], krb.at[z]
        ),
    )
    arrived(5, r0l)
    curve = fold(jnp.sum(kr[...] * r0l[...], axis=0))
    part = jnp.where(low, curve, rr_own)
    sa_s[...] = part
    sa[q] = part
    push(8, plane, sa_s, sa.at[q])
    krb[z] = kr[place_of(0)]
    cand_product(ucs, vb0)

    arrived(2, xcb)
    tiles = []
    for j in range(2):
        tile = xcb[4 * j]
        for g in range(1, 4):
            tile = jnp.where(lane < 32 * g, tile, pltpu.roll(xcb[4 * j + g], 32 * g, 1))
        tiles.append(tile)
    out = prior_share(left_side(jnp.concatenate(tiles, axis=1)))
    for i in range(NC):
        pcs[i] = jnp.where(low, out[32 * i : 32 * i + 16], out[32 * i + 16 : 32 * i + 32])
    pcb[c] = pcs[c]

    arrived(8, sa)
    part = jnp.sum(sa[...], axis=0)
    sb_s[...] = part
    sb[z] = part
    push(10, line, sb_s, sb.at[z])
    norms, quotient = ratio(part)
    share = jnp.where(norms > 0.0, quotient, 0.0)
    arrived(7, krb)
    r0 = own0[...]
    image = jnp.sum(krb[...], axis=0) + NOISE_LEVEL * r0

    own1[...] = image
    q0l[place_of(0)] = image
    high = (image - share * r0).astype(BF16)
    hb1[...] = high
    vb1[sub] = high
    gather(22, hb1, vb1)
    push(12, line, own1, lambda k: q0l.at[place_of(-k)])
    arrived(10, sb)
    rr0, quotient = ratio(jnp.sum(sb[...], axis=0))
    alpha1 = 1.0 / quotient
    r1 = r0 - alpha1 * image
    rr1_own = fold(r1 * r1)
    ra_s[...] = rr1_own
    ra[q] = rr1_own
    push(13, plane, ra_s, ra.at[q])
    push(9, line, lambda k: ucs.at[zs[k]], ucb.at[z])
    ucb[z] = ucs[z]
    push(6, cands, lambda tag: pcs.at[xs[tag[0]] * 2 + tag[1]], pcb.at[c])
    mixed_own = fold(r0 * r1)
    train_product(kq, 22, vb1, lambda first: None)
    arrived(12, q0l)
    r1l = r0l[...] - alpha1 * q0l[...]
    k1 = (1.0 - alpha1 * share) * kr[...] - alpha1 * kq[...]
    curve = fold(jnp.sum(r1l * k1, axis=0)) + NOISE_LEVEL * rr1_own
    mixed = fold(jnp.sum(r0l[...] * k1 + r1l * kr[...], axis=0)) + 2.0 * NOISE_LEVEL * mixed_own
    part = jnp.where(low, curve, mixed)
    qa_s[...] = part
    qa[q] = part
    push(16, plane, qa_s, qa.at[q])
    arrived(13, ra)
    part = jnp.sum(ra[...], axis=0)
    rb_s[...] = part
    rb[z] = part
    push(14, line, rb_s, rb.at[z])
    cand_product(wcs, vb1)
    wcs[...] = wcs[...] + share * ucs[...]
    push(15, line, lambda k: wcs.at[zs[k]], wcb.at[z])
    wcb[z] = wcs[z]
    arrived(16, qa)
    part = jnp.sum(qa[...], axis=0)
    qb_s[...] = part
    qb[z] = part
    push(17, line, qb_s, qb.at[z])
    arrived(6, pcb)
    prior = jnp.sum(pcb[...], axis=0)
    arrived(9, ucb)
    first_part = jnp.sum(ucb[...], axis=0)
    arrived(14, rb)
    rr1 = jnp.sum(rb[...], axis=0)
    beta = rr1 / rr0
    arrived(15, wcb)
    second_part = first_part - alpha1 * jnp.sum(wcb[...], axis=0)
    r0 = own0[...]
    r1 = r0 - alpha1 * own1[...]
    d1 = r1 + beta * r0
    arrived(17, qb)
    part = jnp.sum(qb[...], axis=0)
    other = swap(part)
    curve, mixed = jnp.where(low, part, other), jnp.where(low, other, part)
    alpha2 = rr1 / (curve + beta * (mixed + beta * (rr0 / alpha1)))

    packed[0:32, :] = alpha1 * r0 + alpha2 * d1
    packed[32:48, :] = prior + (alpha1 + alpha2 * beta) * first_part + alpha2 * second_part

    whole = {
        0: xp, 1: xl, 2: xcb, 3: ptb, 5: r0l, 6: pcb, 7: krb, 8: sa, 9: ucb, 10: sb,
        12: q0l, 13: ra, 14: rb, 15: wcb, 16: qa, 17: qb,
    }
    for phase, buf in whole.items():
        settle(phase, ssem, buf)
    for base, buf in ((18, vb0), (22, vb1)):
        for i in range(4):
            settle(base + i, ssem, buf, 7 if i == 0 else 8)


def unpack(packed, sam, sol):
    sol[0:32, :] = packed[0:32, 0:64]
    sol[32:64, :] = pltpu.roll(packed[0:32, :], 64, 1)[:, 0:64]
    sam[0:16, :] = packed[32:48, 0:64]
    sam[16:32, :] = pltpu.roll(packed[32:48, :], 64, 1)[:, 0:64]


def body(x_train, x_cand, targets, noise, omega, phase, prior_weights):
    vmem = pltpu.VMEM
    field = lambda n, rows, dtype=F32: vmem((n, rows, 128), dtype)
    tile, row = vmem((8, 128), F32), vmem((1, 128), F32)
    scratch = [
        vmem((8, 512), F32), vmem((8, 1024), F32), vmem((1, OWN), F32), vmem((OWN, OWN), F32),
        vmem((8, FEATS), F32), vmem((1, FEATS), F32), vmem((2 * OWN, FEATS), BF16),
        tile, field(NZ, 8), tile, field(NC, 8), vmem((NH, 8, 512), F32),
        vmem((128, 2048), BF16), vmem((128, FEATS), BF16), vmem((768, 128), BF16), vmem((768, 2048), BF16),
        field(NC, 32), field(NC, 32), field(NC, 16), field(NC, 16),
        vmem((32, 128), F32), vmem((32, 128), F32),
        field(NP, 32, BF16), field(NP, 32, BF16),
        field(NZ, 32), field(NZ, 32),
        vmem((768, 128), F32), vmem((768, 128), F32),
        field(NZ, 32), field(NZ, 32), field(NZ, 32),
        field(NZ, 16), field(NZ, 16), field(NZ, 16), field(NZ, 16),
        row, field(NP, 1), row, field(NZ, 1), row, field(NP, 1), row, field(NZ, 1),
        row, field(NP, 1), row, field(NZ, 1),
        vmem((32, 128), BF16), vmem((32, 128), BF16),
        pltpu.SemaphoreType.DMA((8,)), pltpu.SemaphoreType.DMA((26,)),
        pltpu.SemaphoreType.DMA((26,)),
    ]
    operands = (
        x_train, x_cand, targets.reshape(1, OWN), noise, omega,
        phase.reshape(1, TOTAL_FEATS), prior_weights.T,
    )
    packed = pl.pallas_call(
        kernel,
        out_shape=jax.ShapeDtypeStruct((48, 128), F32),
        in_specs=[pl.BlockSpec(memory_space=pltpu.HBM)] * 7,
        out_specs=pl.BlockSpec(memory_space=vmem),
        scratch_shapes=scratch,
        compiler_params=pltpu.CompilerParams(
            collective_id=0, has_side_effects=True, vmem_limit_bytes=32 * 1024 * 1024
        ),
    )(*(pltpu.with_memory_space_constraint(value, pltpu.HBM) for value in operands))
    return pl.pallas_call(
        unpack,
        out_shape=(
            jax.ShapeDtypeStruct((CANDS, OWN), F32),
            jax.ShapeDtypeStruct((OWN, OWN), F32),
        ),
        in_specs=[pl.BlockSpec(memory_space=vmem)],
        out_specs=(pl.BlockSpec(memory_space=vmem),) * 2,
        compiler_params=pltpu.CompilerParams(vmem_limit_bytes=4 * 1024 * 1024),
    )(packed)


def solution(mesh):
    placed = (
        P(None, "train"),
        P(None, "cand"),
        P(("train", "cand")),
        P(("train", "cand"), None),
        P(),
        P(),
        P("cand", None),
    )
    return jax.shard_map(
        body,
        mesh=mesh,
        in_specs=placed,
        out_specs=(P(("cand", "train"), None), P(("train", "cand"), None)),
        check_vma=False,
    )
```

```python
import math

import jax
import jax.numpy as jnp
from jax import lax
from jax.experimental import pallas as pl
from jax.experimental.pallas import tpu as pltpu
from jax.sharding import PartitionSpec as P

MESH = pl.DeviceIdType.MESH
F32, BF16 = jnp.float32, jnp.bfloat16
NZ, NC, NH = 8, 8, 4
NP = NH * NC
OWN = 64
CANDS = 32
FEATS = 512
TOTAL_FEATS = 4096
NOISE_LEVEL = 0.5
def hops(offset):
    dx, dy, dz, _ = offset
    return min(dx, 4 - dx) + min(dy, 4 - dy) + min(dz, NZ - dz)


PLANE_ORDER = sorted(
    ((i, j, 0, k) for i in range(4) for j in range(4) for k in range(2) if i + j + k),
    key=lambda offset: -hops(offset),
)
LINE_ORDER = (4, 3, 5, 2, 6, 1, 7, 0)
GREETING = sorted(
    [(0, 0, k, 0) for k in LINE_ORDER[:-1]] + PLANE_ORDER, key=lambda offset: -hops(offset)
)


def place_of(k):
    return LINE_ORDER.index(k % NZ)
SIN = (
    6.283185159611151,
    -41.3416549293423,
    81.60099819256979,
    -76.5496568198889,
    39.53581370662112,
)


def split3(value):
    one = value.astype(BF16).astype(F32)
    two = (value - one).astype(BF16).astype(F32)
    return one, two, value - one - two


def rows8(*rows):
    index = lax.broadcasted_iota(jnp.int32, (8, rows[0].shape[1]), 0)
    out = jnp.zeros((8, rows[0].shape[1]), F32)
    for place, row in enumerate(rows):
        out = jnp.where(index == place, row, out)
    return out


def half_norm(points):
    return -0.5 * jnp.sum(points * points, axis=0, keepdims=True)


def left_side(points):
    one, two, three = split3(points)
    ones = jnp.ones((1, points.shape[1]), F32)
    tail = rows8(*split3(half_norm(points)), ones, ones, ones)
    pad = jnp.zeros((72, points.shape[1]), F32)
    return jnp.concatenate([one, one, two, two, one, three, tail, pad], axis=0).T.astype(BF16)


def right_side(points, tail):
    one, two, three = split3(points)
    pad = jnp.zeros((72, points.shape[1]), F32)
    return jnp.concatenate([one, two, one, two, three, one, tail, pad], axis=0).astype(BF16)


def kernel(
    xt_hbm, xc_hbm, tg_hbm, nz_hbm, om_hbm, ph_hbm, pw_hbm, packed,
    xt, xc, tg, nz, om, ph, pw,
    xls, xl, xcs, xcb, xp, by, bw, atl, km,
    pts, ptb, pcs, pcb, own0, own1, vb0, vb1, r0l, q0l,
    o1, o2, kr, krb, kq, ucs, ucb, wcs, wcb,
    sa_s, sa, sb_s, sb, ra_s, ra, rb_s, rb, qa_s, qa, qb_s, qb,
    isem, ssem, rsem,
):
    t, c = lax.axis_index("train"), lax.axis_index("cand")
    y_hi, z, core = t // 16, lax.rem(t, 16) // 2, lax.rem(t, 2)
    h = y_hi * 2 + core
    q = h * NC + c

    x, y = c // 2, y_hi * 2 + lax.rem(c, 2)

    y_lo = lax.rem(c, 2)
    ys = [lax.rem(y + k, 4) for k in range(4)]
    xs = [lax.rem(x + k, 4) for k in range(4)]
    zs = [lax.rem(z + k, NZ) for k in range(NZ)]
    cores = [core, 1 - core]

    def device(dx, dy, dz, dcore):
        return (
            (ys[dy] // 2) * 16 + zs[dz] * 2 + cores[dcore],
            xs[dx] * 2 + lax.rem(ys[dy], 2),
        )

    plane = [(device(*offset), offset[0]) for offset in PLANE_ORDER]
    line = [(device(0, 0, k, 0), k) for k in LINE_ORDER[:-1]]
    blocks = [(device(0, j, 0, k), None) for j, k in ((2, 1), (2, 0), (0, 1))]
    near = 1 - y_lo
    cands = [
        ((t, xs[i] * 2 + j), (i, j))
        for i, j in ((2, 0), (2, 1), (1, 0), (1, 1), (3, 0), (3, 1), (0, near))
    ]
    sub = h * 2 + y_lo

    feat = pl.ds(pl.multiple_of(c * FEATS, FEATS), FEATS)
    inputs = [
        pltpu.make_async_copy(source, target, isem.at[number])
        for number, (source, target) in enumerate(
            (
                (xt_hbm, xt),
                (om_hbm.at[:, feat], om),
                (ph_hbm.at[:, feat], ph),
                (pw_hbm, pw.at[pl.ds(0, OWN)]),
                (pw_hbm, pw.at[pl.ds(OWN, OWN)]),
                (xc_hbm, xc),
                (tg_hbm, tg),
                (nz_hbm, nz),
            )
        )
    ]
    barrier = pltpu.get_barrier_semaphore()
    for copy in inputs[:5]:
        copy.start()
    for offset in GREETING:
        peer = device(*offset)
        pl.semaphore_signal(barrier, inc=1, device_id=peer, device_id_type=MESH)
    for copy in inputs[5:]:
        copy.start()

    def push(phase, peers, source, target):
        for peer, tag in peers:
            number = phase(tag) if callable(phase) else phase
            pltpu.make_async_remote_copy(
                src_ref=source(tag) if callable(source) else source,
                dst_ref=target(tag) if callable(target) else target,
                send_sem=ssem.at[number],
                recv_sem=rsem.at[number],
                device_id=peer,
                device_id_type=MESH,
            ).start()

    def settle(phase, sems, buf, count=None):
        ref = buf.at[pl.ds(0, count or buf.shape[0] - 1)]
        pltpu.make_async_copy(ref, ref, sems.at[phase]).wait()

    def arrived(phase, buf, count=None):
        settle(phase, rsem, buf, count)

    def gather(base, field):
        push(
            lambda i: base + -i % 4,
            plane,
            field.at[sub],
            lambda i: field.at[(-i % 4) * 8 + sub],
        )

    lane = lax.broadcasted_iota(jnp.int32, (1, 128), 1)
    low = lane < 64

    def swap(value):
        return pltpu.roll(value, 64, 1)

    def pair(first, second):
        return jnp.where(low, first, swap(second))

    def fold(value):
        row = jnp.sum(value, axis=0, keepdims=True)
        return row + swap(row)

    for copy in inputs[:5]:
        copy.wait()

    turn = 1.0 / (2.0 * math.pi)
    zero = jnp.zeros((1, FEATS), F32)
    bw[...] = right_side(om[...] * turn, rows8(zero, zero, zero, *split3(ph[...] * turn)))
    def prior_share(left):
        turns = jnp.dot(left, bw[...], preferred_element_type=F32)
        wave = jnp.abs(turns - jnp.floor(turns) - 0.5) - 0.25
        square = wave * wave
        scale = math.sqrt(2.0 / TOTAL_FEATS)
        value = square * (SIN[-1] * scale) + SIN[-2] * scale
        for coefficient in SIN[-3::-1]:
            value = value * square + coefficient * scale
        packed = (value * wave).astype(BF16)
        return lax.dot_general(
            packed, pw[...], (((1,), (1,)), ((), ())), preferred_element_type=F32
        )

    out = prior_share(left_side(xt[...]))
    for i in range(NC):
        pts[i] = jnp.where(low, out[64 * i : 64 * i + 32], out[64 * i + 32 : 64 * i + 64])
    pl.semaphore_wait(barrier, NP - 1 + NZ - 1)
    push(3, cands, lambda tag: pts.at[xs[tag[0]] * 2 + tag[1]], ptb.at[c])
    for copy in inputs[5:]:
        copy.wait()

    mine = xt[:, pl.ds(pl.multiple_of((c // 2) * 128, 128), 128)]
    mine = jnp.where(lax.rem(c, 2) == 1, swap(mine), mine)
    xls[...] = mine
    xl[place_of(0)] = mine
    xp[h] = xt[...]
    cand = xc[:, pl.ds(pl.multiple_of((t // 4) * 128, 128), 128)]
    cand = pltpu.roll(cand, lax.rem(128 - lax.rem(t, 4) * 32, 128), 1)
    xcs[...] = cand
    xcb[c] = cand
    push(0, blocks, xt, xp.at[h])
    push(1, line, xls, lambda k: xl.at[place_of(-k)])
    push(2, cands, xcs, xcb.at[c])
    ptb[c] = pts[c]

    row = tg[...]
    place = lax.broadcasted_iota(jnp.int32, (32, 64), 0)
    at = lax.broadcasted_iota(jnp.int32, (32, 64), 1)
    upper = jnp.sum(jnp.where(at == place, row, 0.0), axis=1, keepdims=True)
    lower = jnp.sum(jnp.where(at == place + 32, row, 0.0), axis=1, keepdims=True)
    noise = jnp.concatenate([nz[0:32, :], nz[32:64, :]], axis=1)
    base = jnp.where(low, upper, lower) - noise

    def line_cands(j):
        tile = xc[:, pl.ds(pl.multiple_of(y_hi * 512 + j * 128, 128), 128)]
        tile = pltpu.roll(tile, lax.rem(128 - core * 32, 128), 1)
        return jnp.where(lane < 32, tile, pltpu.roll(tile, 96, 1))

    for j in range(2):
        atl[512 + j * 128 : 640 + j * 128, :] = left_side(
            pair(line_cands(2 * j), line_cands(2 * j + 1))
        )

    def entries(first, count):
        rows = pl.ds(first, count)
        power = jnp.dot(atl[rows, :], by[...], preferred_element_type=F32)
        km[rows, :] = jnp.exp(power).astype(BF16)

    arrived(3, ptb)
    r0 = base - jnp.sum(ptb[...], axis=0)
    own0[...] = r0
    r0l[place_of(0)] = r0
    vb0[sub] = r0.astype(BF16)
    gather(18, vb0)
    push(5, line, own0, lambda k: r0l.at[place_of(-k)])
    rr_own = fold(r0 * r0)

    arrived(0, xp)
    for i in range(4):
        tiles = [xp[g, :, pl.ds(pl.multiple_of(xs[i] * 128, 128), 128)] for g in range(NH)]
        uppers = [jnp.where(lane < 32, a, pltpu.roll(a, 96, 1)) for a in tiles]
        lowers = [jnp.where(lane < 32, pltpu.roll(a, 96, 1), swap(a)) for a in tiles]
        for start, halves in ((i * 256, uppers), (1024 + i * 256, lowers)):
            points = jnp.concatenate([pair(*halves[:2]), pair(*halves[2:])], axis=1)
            ones = jnp.ones((1, 256), F32)
            tail = rows8(ones, ones, ones, *split3(half_norm(points)))
            by[:, start : start + 256] = right_side(points, tail)

    arrived(1, xl)
    for j in range(4):
        atl[j * 128 : j * 128 + 128, :] = left_side(pair(xl[2 * j], xl[2 * j + 1]))
    entries(0, 512)
    entries(512, 256)

    def multiply(first, count, field):
        rows = pl.ds(first, count)
        values = field[...].reshape(NP * 32, 128)
        o1[rows, :] = jnp.dot(km[rows, 0:1024], values, preferred_element_type=F32)
        o2[rows, :] = jnp.dot(km[rows, 1024:2048], values, preferred_element_type=F32)

    def joined(first, size):
        a1, b1 = o1[pl.ds(first, size), :], o1[pl.ds(first + size, size), :]
        a2, b2 = o2[pl.ds(first, size), :], o2[pl.ds(first + size, size), :]
        return jnp.where(low, a1, b2) + swap(jnp.where(low, b1, a2))

    def gathered(base, field):
        for i in range(4):
            arrived(base + i, field, 7 if i == 0 else 8)

    def train_product(first, count, pieces, field):
        multiply(64 * first, 64 * count, field)
        for k in range(first, first + count):
            pieces[k] = joined(64 * k, 32)

    def cand_product(pieces, field):
        multiply(512, 256, field)
        for i in range(NZ):
            pieces[i] = joined(512 + i * 32, 16)

    def ratio(part):
        other = swap(part)
        norms = jnp.where(low, other, part)
        return norms, jnp.where(low, part, other) / norms + NOISE_LEVEL

    gathered(18, vb0)
    for first in (0, 4):
        train_product(first, 4, kr, vb0)
        push(7, line[first : first + 4], lambda k: kr.at[place_of(k)], krb.at[z])
    arrived(5, r0l)
    curve = fold(jnp.sum(kr[...] * r0l[...], axis=0))
    part = jnp.where(low, curve, rr_own)
    sa_s[...] = part
    sa[q] = part
    push(8, plane, sa_s, sa.at[q])
    krb[z] = kr[place_of(0)]
    cand_product(ucs, vb0)

    arrived(2, xcb)
    tiles = []
    for j in range(2):
        tile = xcb[4 * j]
        for g in range(1, 4):
            tile = jnp.where(lane < 32 * g, tile, pltpu.roll(xcb[4 * j + g], 32 * g, 1))
        tiles.append(tile)
    out = prior_share(left_side(jnp.concatenate(tiles, axis=1)))
    for i in range(NC):
        pcs[i] = jnp.where(low, out[32 * i : 32 * i + 16], out[32 * i + 16 : 32 * i + 32])
    pcb[c] = pcs[c]

    arrived(8, sa)
    part = jnp.sum(sa[...], axis=0)
    sb_s[...] = part
    sb[z] = part
    push(10, line, sb_s, sb.at[z])
    norms, quotient = ratio(part)
    share = jnp.where(norms > 0.0, quotient, 0.0)
    arrived(7, krb)
    r0 = own0[...]
    image = jnp.sum(krb[...], axis=0) + NOISE_LEVEL * r0

    own1[...] = image
    q0l[place_of(0)] = image
    vb1[sub] = (image - share * r0).astype(BF16)
    gather(22, vb1)
    push(12, line, own1, lambda k: q0l.at[place_of(-k)])
    arrived(10, sb)
    rr0, quotient = ratio(jnp.sum(sb[...], axis=0))
    alpha1 = 1.0 / quotient
    r1 = r0 - alpha1 * image
    rr1_own = fold(r1 * r1)
    ra_s[...] = rr1_own
    ra[q] = rr1_own
    push(13, plane, ra_s, ra.at[q])
    push(9, line, lambda k: ucs.at[zs[k]], ucb.at[z])
    ucb[z] = ucs[z]
    push(6, cands, lambda tag: pcs.at[xs[tag[0]] * 2 + tag[1]], pcb.at[c])
    mixed_own = fold(r0 * r1)
    gathered(22, vb1)
    train_product(0, NZ, kq, vb1)
    arrived(12, q0l)
    r1l = r0l[...] - alpha1 * q0l[...]
    k1 = (1.0 - alpha1 * share) * kr[...] - alpha1 * kq[...]
    curve = fold(jnp.sum(r1l * k1, axis=0)) + NOISE_LEVEL * rr1_own
    mixed = fold(jnp.sum(r0l[...] * k1 + r1l * kr[...], axis=0)) + 2.0 * NOISE_LEVEL * mixed_own
    part = jnp.where(low, curve, mixed)
    qa_s[...] = part
    qa[q] = part
    push(16, plane, qa_s, qa.at[q])
    arrived(13, ra)
    part = jnp.sum(ra[...], axis=0)
    rb_s[...] = part
    rb[z] = part
    push(14, line, rb_s, rb.at[z])
    cand_product(wcs, vb1)
    wcs[...] = wcs[...] + share * ucs[...]
    push(15, line, lambda k: wcs.at[zs[k]], wcb.at[z])
    wcb[z] = wcs[z]
    arrived(16, qa)
    part = jnp.sum(qa[...], axis=0)
    qb_s[...] = part
    qb[z] = part
    push(17, line, qb_s, qb.at[z])
    arrived(6, pcb)
    prior = jnp.sum(pcb[...], axis=0)
    arrived(9, ucb)
    first_part = jnp.sum(ucb[...], axis=0)
    arrived(14, rb)
    rr1 = jnp.sum(rb[...], axis=0)
    beta = rr1 / rr0
    arrived(15, wcb)
    second_part = first_part - alpha1 * jnp.sum(wcb[...], axis=0)
    r0 = own0[...]
    r1 = r0 - alpha1 * own1[...]
    d1 = r1 + beta * r0
    arrived(17, qb)
    part = jnp.sum(qb[...], axis=0)
    other = swap(part)
    curve, mixed = jnp.where(low, part, other), jnp.where(low, other, part)
    alpha2 = rr1 / (curve + beta * (mixed + beta * (rr0 / alpha1)))

    packed[0:32, :] = alpha1 * r0 + alpha2 * d1
    packed[32:48, :] = prior + (alpha1 + alpha2 * beta) * first_part + alpha2 * second_part

    whole = {
        0: xp, 1: xl, 2: xcb, 3: ptb, 5: r0l, 6: pcb, 7: krb, 8: sa, 9: ucb, 10: sb,
        12: q0l, 13: ra, 14: rb, 15: wcb, 16: qa, 17: qb,
    }
    for phase, buf in whole.items():
        settle(phase, ssem, buf)
    for base, buf in ((18, vb0), (22, vb1)):
        for i in range(4):
            settle(base + i, ssem, buf, 7 if i == 0 else 8)


def unpack(packed, sam, sol):
    sol[0:32, :] = packed[0:32, 0:64]
    sol[32:64, :] = pltpu.roll(packed[0:32, :], 64, 1)[:, 0:64]
    sam[0:16, :] = packed[32:48, 0:64]
    sam[16:32, :] = pltpu.roll(packed[32:48, :], 64, 1)[:, 0:64]


def body(x_train, x_cand, targets, noise, omega, phase, prior_weights):
    vmem = pltpu.VMEM
    field = lambda n, rows, dtype=F32: vmem((n, rows, 128), dtype)
    tile, row = vmem((8, 128), F32), vmem((1, 128), F32)
    scratch = [
        vmem((8, 512), F32), vmem((8, 1024), F32), vmem((1, OWN), F32), vmem((OWN, OWN), F32),
        vmem((8, FEATS), F32), vmem((1, FEATS), F32), vmem((2 * OWN, FEATS), BF16),
        tile, field(NZ, 8), tile, field(NC, 8), vmem((NH, 8, 512), F32),
        vmem((128, 2048), BF16), vmem((128, FEATS), BF16), vmem((768, 128), BF16), vmem((768, 2048), BF16),
        field(NC, 32), field(NC, 32), field(NC, 16), field(NC, 16),
        vmem((32, 128), F32), vmem((32, 128), F32),
        field(NP, 32, BF16), field(NP, 32, BF16),
        field(NZ, 32), field(NZ, 32),
        vmem((768, 128), F32), vmem((768, 128), F32),
        field(NZ, 32), field(NZ, 32), field(NZ, 32),
        field(NZ, 16), field(NZ, 16), field(NZ, 16), field(NZ, 16),
        row, field(NP, 1), row, field(NZ, 1), row, field(NP, 1), row, field(NZ, 1),
        row, field(NP, 1), row, field(NZ, 1),
        pltpu.SemaphoreType.DMA((8,)), pltpu.SemaphoreType.DMA((26,)),
        pltpu.SemaphoreType.DMA((26,)),
    ]
    operands = (
        x_train, x_cand, targets.reshape(1, OWN), noise, omega,
        phase.reshape(1, TOTAL_FEATS), prior_weights.T,
    )
    packed = pl.pallas_call(
        kernel,
        out_shape=jax.ShapeDtypeStruct((48, 128), F32),
        in_specs=[pl.BlockSpec(memory_space=pltpu.HBM)] * 7,
        out_specs=pl.BlockSpec(memory_space=vmem),
        scratch_shapes=scratch,
        compiler_params=pltpu.CompilerParams(
            collective_id=0, has_side_effects=True, vmem_limit_bytes=32 * 1024 * 1024
        ),
    )(*(pltpu.with_memory_space_constraint(value, pltpu.HBM) for value in operands))
    return pl.pallas_call(
        unpack,
        out_shape=(
            jax.ShapeDtypeStruct((CANDS, OWN), F32),
            jax.ShapeDtypeStruct((OWN, OWN), F32),
        ),
        in_specs=[pl.BlockSpec(memory_space=vmem)],
        out_specs=(pl.BlockSpec(memory_space=vmem),) * 2,
        compiler_params=pltpu.CompilerParams(vmem_limit_bytes=4 * 1024 * 1024),
    )(packed)


def solution(mesh):
    placed = (
        P(None, "train"),
        P(None, "cand"),
        P(("train", "cand")),
        P(("train", "cand"), None),
        P(),
        P(),
        P("cand", None),
    )
    return jax.shard_map(
        body,
        mesh=mesh,
        in_specs=placed,
        out_specs=(P(("cand", "train"), None), P(("train", "cand"), None)),
        check_vma=False,
    )
```

```python
import math

import jax
import jax.numpy as jnp
from jax import lax
from jax.experimental import pallas as pl
from jax.experimental.pallas import tpu as pltpu
from jax.sharding import PartitionSpec as P

MESH = pl.DeviceIdType.MESH
F32, BF16 = jnp.float32, jnp.bfloat16
NZ, NC, NH = 8, 8, 4
NP = NH * NC
OWN = 64
CANDS = 32
FEATS = 512
TOTAL_FEATS = 4096
NOISE_LEVEL = 0.5
def hops(offset):
    dx, dy, dz, _ = offset
    return min(dx, 4 - dx) + min(dy, 4 - dy) + min(dz, NZ - dz)


PLANE_ORDER = sorted(
    ((i, j, 0, k) for i in range(4) for j in range(4) for k in range(2) if i + j + k),
    key=lambda offset: -hops(offset),
)
EVERYONE = sorted(
    (
        (i, j, k, core)
        for i in range(4)
        for j in range(4)
        for k in range(NZ)
        for core in range(2)
        if i + j + k + core
    ),
    key=lambda offset: -hops(offset),
)
LINE_ORDER = (4, 3, 5, 2, 6, 1, 7, 0)
GREETING = sorted(
    [(0, 0, k, 0) for k in LINE_ORDER[:-1]] + PLANE_ORDER, key=lambda offset: -hops(offset)
)


def place_of(k):
    return LINE_ORDER.index(k % NZ)
SIN = (
    6.283185159611151,
    -41.3416549293423,
    81.60099819256979,
    -76.5496568198889,
    39.53581370662112,
)


def split3(value):
    one = value.astype(BF16).astype(F32)
    two = (value - one).astype(BF16).astype(F32)
    return one, two, value - one - two


def rows8(*rows):
    index = lax.broadcasted_iota(jnp.int32, (8, rows[0].shape[1]), 0)
    out = jnp.zeros((8, rows[0].shape[1]), F32)
    for place, row in enumerate(rows):
        out = jnp.where(index == place, row, out)
    return out


def half_norm(points):
    return -0.5 * jnp.sum(points * points, axis=0, keepdims=True)


def left_side(points):
    one, two, three = split3(points)
    ones = jnp.ones((1, points.shape[1]), F32)
    tail = rows8(*split3(half_norm(points)), ones, ones, ones)
    pad = jnp.zeros((72, points.shape[1]), F32)
    return jnp.concatenate([one, one, two, two, one, three, tail, pad], axis=0).T.astype(BF16)


def right_side(points, tail):
    one, two, three = split3(points)
    pad = jnp.zeros((72, points.shape[1]), F32)
    return jnp.concatenate([one, two, one, two, three, one, tail, pad], axis=0).astype(BF16)


def kernel(
    xt_hbm, xc_hbm, tg_hbm, nz_hbm, om_hbm, ph_hbm, pw_hbm, packed,
    xt, xc, tg, nz, om, ph, pw,
    xls, xl, xcs, xcb, xp, by, bw, atl, km,
    pts, ptb, pcs, pcb, own0, own1, vb0, vb1, r0l, q0l,
    o1, o2, kr, krb, kq, ucs, ucb, wcs, wcb,
    sa_s, sa, sb_s, sb, ra_s, ra, rb_s, rb, qa_s, qa,
    isem, ssem, rsem,
):
    t, c = lax.axis_index("train"), lax.axis_index("cand")
    y_hi, z, core = t // 16, lax.rem(t, 16) // 2, lax.rem(t, 2)
    h = y_hi * 2 + core
    q = h * NC + c

    x, y = c // 2, y_hi * 2 + lax.rem(c, 2)

    y_lo = lax.rem(c, 2)
    ys = [lax.rem(y + k, 4) for k in range(4)]
    xs = [lax.rem(x + k, 4) for k in range(4)]
    zs = [lax.rem(z + k, NZ) for k in range(NZ)]
    cores = [core, 1 - core]

    def device(dx, dy, dz, dcore):
        return (
            (ys[dy] // 2) * 16 + zs[dz] * 2 + cores[dcore],
            xs[dx] * 2 + lax.rem(ys[dy], 2),
        )

    plane = [(device(*offset), offset[0]) for offset in PLANE_ORDER]
    everyone = [(device(*offset), None) for offset in EVERYONE]
    line = [(device(0, 0, k, 0), k) for k in LINE_ORDER[:-1]]
    blocks = [(device(0, j, 0, k), None) for j, k in ((2, 1), (2, 0), (0, 1))]
    near = 1 - y_lo
    cands = [
        ((t, xs[i] * 2 + j), (i, j))
        for i, j in ((2, 0), (2, 1), (1, 0), (1, 1), (3, 0), (3, 1), (0, near))
    ]
    sub = h * 2 + y_lo

    feat = pl.ds(pl.multiple_of(c * FEATS, FEATS), FEATS)
    inputs = [
        pltpu.make_async_copy(source, target, isem.at[number])
        for number, (source, target) in enumerate(
            (
                (xt_hbm, xt),
                (om_hbm.at[:, feat], om),
                (ph_hbm.at[:, feat], ph),
                (pw_hbm, pw.at[pl.ds(0, OWN)]),
                (pw_hbm, pw.at[pl.ds(OWN, OWN)]),
                (xc_hbm, xc),
                (tg_hbm, tg),
                (nz_hbm, nz),
            )
        )
    ]
    barrier = pltpu.get_barrier_semaphore()
    for copy in inputs[:5]:
        copy.start()
    for offset in GREETING:
        peer = device(*offset)
        pl.semaphore_signal(barrier, inc=1, device_id=peer, device_id_type=MESH)
    for copy in inputs[5:]:
        copy.start()

    def push(phase, peers, source, target):
        for peer, tag in peers:
            number = phase(tag) if callable(phase) else phase
            pltpu.make_async_remote_copy(
                src_ref=source(tag) if callable(source) else source,
                dst_ref=target(tag) if callable(target) else target,
                send_sem=ssem.at[number],
                recv_sem=rsem.at[number],
                device_id=peer,
                device_id_type=MESH,
            ).start()

    def settle(phase, sems, buf, count=None):
        ref = buf.at[pl.ds(0, count or buf.shape[0] - 1)]
        pltpu.make_async_copy(ref, ref, sems.at[phase]).wait()

    def arrived(phase, buf, count=None):
        settle(phase, rsem, buf, count)

    def gather(base, field):
        push(
            lambda i: base + -i % 4,
            plane,
            field.at[sub],
            lambda i: field.at[(-i % 4) * 8 + sub],
        )

    lane = lax.broadcasted_iota(jnp.int32, (1, 128), 1)
    low = lane < 64

    def swap(value):
        return pltpu.roll(value, 64, 1)

    def pair(first, second):
        return jnp.where(low, first, swap(second))

    def fold(value):
        row = jnp.sum(value, axis=0, keepdims=True)
        return row + swap(row)

    for copy in inputs[:5]:
        copy.wait()

    turn = 1.0 / (2.0 * math.pi)
    zero = jnp.zeros((1, FEATS), F32)
    bw[...] = right_side(om[...] * turn, rows8(zero, zero, zero, *split3(ph[...] * turn)))
    def prior_share(left):
        turns = jnp.dot(left, bw[...], preferred_element_type=F32)
        wave = jnp.abs(turns - jnp.floor(turns) - 0.5) - 0.25
        square = wave * wave
        scale = math.sqrt(2.0 / TOTAL_FEATS)
        value = square * (SIN[-1] * scale) + SIN[-2] * scale
        for coefficient in SIN[-3::-1]:
            value = value * square + coefficient * scale
        packed = (value * wave).astype(BF16)
        return lax.dot_general(
            packed, pw[...], (((1,), (1,)), ((), ())), preferred_element_type=F32
        )

    out = prior_share(left_side(xt[...]))
    for i in range(NC):
        pts[i] = jnp.where(low, out[64 * i : 64 * i + 32], out[64 * i + 32 : 64 * i + 64])
    pl.semaphore_wait(barrier, NP - 1 + NZ - 1)
    push(3, cands, lambda tag: pts.at[xs[tag[0]] * 2 + tag[1]], ptb.at[c])
    for copy in inputs[5:]:
        copy.wait()

    mine = xt[:, pl.ds(pl.multiple_of((c // 2) * 128, 128), 128)]
    mine = jnp.where(lax.rem(c, 2) == 1, swap(mine), mine)
    xls[...] = mine
    xl[place_of(0)] = mine
    xp[h] = xt[...]
    cand = xc[:, pl.ds(pl.multiple_of((t // 4) * 128, 128), 128)]
    cand = pltpu.roll(cand, lax.rem(128 - lax.rem(t, 4) * 32, 128), 1)
    xcs[...] = cand
    xcb[c] = cand
    push(0, blocks, xt, xp.at[h])
    push(1, line, xls, lambda k: xl.at[place_of(-k)])
    push(2, cands, xcs, xcb.at[c])
    ptb[c] = pts[c]

    row = tg[...]
    place = lax.broadcasted_iota(jnp.int32, (32, 64), 0)
    at = lax.broadcasted_iota(jnp.int32, (32, 64), 1)
    upper = jnp.sum(jnp.where(at == place, row, 0.0), axis=1, keepdims=True)
    lower = jnp.sum(jnp.where(at == place + 32, row, 0.0), axis=1, keepdims=True)
    noise = jnp.concatenate([nz[0:32, :], nz[32:64, :]], axis=1)
    base = jnp.where(low, upper, lower) - noise

    def line_cands(j):
        tile = xc[:, pl.ds(pl.multiple_of(y_hi * 512 + j * 128, 128), 128)]
        tile = pltpu.roll(tile, lax.rem(128 - core * 32, 128), 1)
        return jnp.where(lane < 32, tile, pltpu.roll(tile, 96, 1))

    for j in range(2):
        atl[512 + j * 128 : 640 + j * 128, :] = left_side(
            pair(line_cands(2 * j), line_cands(2 * j + 1))
        )

    def entries(first, count):
        rows = pl.ds(first, count)
        power = jnp.dot(atl[rows, :], by[...], preferred_element_type=F32)
        km[rows, :] = jnp.exp(power).astype(BF16)

    arrived(3, ptb)
    r0 = base - jnp.sum(ptb[...], axis=0)
    own0[...] = r0
    r0l[place_of(0)] = r0
    vb0[sub] = r0.astype(BF16)
    gather(18, vb0)
    push(5, line, own0, lambda k: r0l.at[place_of(-k)])
    rr_own = fold(r0 * r0)

    arrived(0, xp)
    for i in range(4):
        tiles = [xp[g, :, pl.ds(pl.multiple_of(xs[i] * 128, 128), 128)] for g in range(NH)]
        uppers = [jnp.where(lane < 32, a, pltpu.roll(a, 96, 1)) for a in tiles]
        lowers = [jnp.where(lane < 32, pltpu.roll(a, 96, 1), swap(a)) for a in tiles]
        for start, halves in ((i * 256, uppers), (1024 + i * 256, lowers)):
            points = jnp.concatenate([pair(*halves[:2]), pair(*halves[2:])], axis=1)
            ones = jnp.ones((1, 256), F32)
            tail = rows8(ones, ones, ones, *split3(half_norm(points)))
            by[:, start : start + 256] = right_side(points, tail)

    arrived(1, xl)
    for j in range(4):
        atl[j * 128 : j * 128 + 128, :] = left_side(pair(xl[2 * j], xl[2 * j + 1]))
    entries(0, 512)
    entries(512, 256)

    def multiply(first, count, field):
        rows = pl.ds(first, count)
        values = field[...].reshape(NP * 32, 128)
        o1[rows, :] = jnp.dot(km[rows, 0:1024], values, preferred_element_type=F32)
        o2[rows, :] = jnp.dot(km[rows, 1024:2048], values, preferred_element_type=F32)

    def joined(first, size):
        a1, b1 = o1[pl.ds(first, size), :], o1[pl.ds(first + size, size), :]
        a2, b2 = o2[pl.ds(first, size), :], o2[pl.ds(first + size, size), :]
        return jnp.where(low, a1, b2) + swap(jnp.where(low, b1, a2))

    def gathered(base, field):
        for i in range(4):
            arrived(base + i, field, 7 if i == 0 else 8)

    def train_product(first, count, pieces, field):
        multiply(64 * first, 64 * count, field)
        for k in range(first, first + count):
            pieces[k] = joined(64 * k, 32)

    def cand_product(pieces, field):
        multiply(512, 256, field)
        for i in range(NZ):
            pieces[i] = joined(512 + i * 32, 16)

    def ratio(part):
        other = swap(part)
        norms = jnp.where(low, other, part)
        return norms, jnp.where(low, part, other) / norms + NOISE_LEVEL

    gathered(18, vb0)
    for first in (0, 4):
        train_product(first, 4, kr, vb0)
        push(7, line[first : first + 4], lambda k: kr.at[place_of(k)], krb.at[z])
    arrived(5, r0l)
    curve = fold(jnp.sum(kr[...] * r0l[...], axis=0))
    part = jnp.where(low, curve, rr_own)
    sa_s[...] = part
    sa[q] = part
    push(8, plane, sa_s, sa.at[q])
    krb[z] = kr[place_of(0)]
    cand_product(ucs, vb0)

    arrived(2, xcb)
    tiles = []
    for j in range(2):
        tile = xcb[4 * j]
        for g in range(1, 4):
            tile = jnp.where(lane < 32 * g, tile, pltpu.roll(xcb[4 * j + g], 32 * g, 1))
        tiles.append(tile)
    out = prior_share(left_side(jnp.concatenate(tiles, axis=1)))
    for i in range(NC):
        pcs[i] = jnp.where(low, out[32 * i : 32 * i + 16], out[32 * i + 16 : 32 * i + 32])
    pcb[c] = pcs[c]

    arrived(8, sa)
    part = jnp.sum(sa[...], axis=0)
    sb_s[...] = part
    sb[z] = part
    push(10, line, sb_s, sb.at[z])
    norms, quotient = ratio(part)
    share = jnp.where(norms > 0.0, quotient, 0.0)
    arrived(7, krb)
    r0 = own0[...]
    image = jnp.sum(krb[...], axis=0) + NOISE_LEVEL * r0

    own1[...] = image
    q0l[place_of(0)] = image
    vb1[sub] = (image - share * r0).astype(BF16)
    gather(22, vb1)
    push(12, line, own1, lambda k: q0l.at[place_of(-k)])
    arrived(10, sb)
    rr0, quotient = ratio(jnp.sum(sb[...], axis=0))
    alpha1 = 1.0 / quotient
    r1 = r0 - alpha1 * image
    rr1_own = fold(r1 * r1)
    ra_s[...] = rr1_own
    ra[q] = rr1_own
    push(13, plane, ra_s, ra.at[q])
    push(9, line, lambda k: ucs.at[zs[k]], ucb.at[z])
    ucb[z] = ucs[z]
    push(6, cands, lambda tag: pcs.at[xs[tag[0]] * 2 + tag[1]], pcb.at[c])
    mixed_own = fold(r0 * r1)
    gathered(22, vb1)
    train_product(0, NZ, kq, vb1)
    arrived(12, q0l)
    r1l = r0l[...] - alpha1 * q0l[...]
    k1 = (1.0 - alpha1 * share) * kr[...] - alpha1 * kq[...]
    curve = fold(jnp.sum(r1l * k1, axis=0)) + NOISE_LEVEL * rr1_own
    mixed = fold(jnp.sum(r0l[...] * k1 + r1l * kr[...], axis=0)) + 2.0 * NOISE_LEVEL * mixed_own
    part = jnp.where(low, curve, mixed)
    qa_s[...] = part
    qa[z * NP + q] = part
    push(16, everyone, qa_s, qa.at[z * NP + q])
    arrived(13, ra)
    part = jnp.sum(ra[...], axis=0)
    rb_s[...] = part
    rb[z] = part
    push(14, line, rb_s, rb.at[z])
    cand_product(wcs, vb1)
    wcs[...] = wcs[...] + share * ucs[...]
    push(15, line, lambda k: wcs.at[zs[k]], wcb.at[z])
    wcb[z] = wcs[z]
    arrived(6, pcb)
    prior = jnp.sum(pcb[...], axis=0)
    arrived(9, ucb)
    first_part = jnp.sum(ucb[...], axis=0)
    arrived(14, rb)
    rr1 = jnp.sum(rb[...], axis=0)
    beta = rr1 / rr0
    arrived(15, wcb)
    second_part = first_part - alpha1 * jnp.sum(wcb[...], axis=0)
    r0 = own0[...]
    r1 = r0 - alpha1 * own1[...]
    d1 = r1 + beta * r0
    arrived(16, qa)
    part = jnp.sum(qa[...], axis=0)
    other = swap(part)
    curve, mixed = jnp.where(low, part, other), jnp.where(low, other, part)
    alpha2 = rr1 / (curve + beta * (mixed + beta * (rr0 / alpha1)))

    packed[0:32, :] = alpha1 * r0 + alpha2 * d1
    packed[32:48, :] = prior + (alpha1 + alpha2 * beta) * first_part + alpha2 * second_part

    whole = {
        0: xp, 1: xl, 2: xcb, 3: ptb, 5: r0l, 6: pcb, 7: krb, 8: sa, 9: ucb, 10: sb,
        12: q0l, 13: ra, 14: rb, 15: wcb, 16: qa,
    }
    for phase, buf in whole.items():
        settle(phase, ssem, buf)
    for base, buf in ((18, vb0), (22, vb1)):
        for i in range(4):
            settle(base + i, ssem, buf, 7 if i == 0 else 8)


def unpack(packed, sam, sol):
    sol[0:32, :] = packed[0:32, 0:64]
    sol[32:64, :] = pltpu.roll(packed[0:32, :], 64, 1)[:, 0:64]
    sam[0:16, :] = packed[32:48, 0:64]
    sam[16:32, :] = pltpu.roll(packed[32:48, :], 64, 1)[:, 0:64]


def body(x_train, x_cand, targets, noise, omega, phase, prior_weights):
    vmem = pltpu.VMEM
    field = lambda n, rows, dtype=F32: vmem((n, rows, 128), dtype)
    tile, row = vmem((8, 128), F32), vmem((1, 128), F32)
    scratch = [
        vmem((8, 512), F32), vmem((8, 1024), F32), vmem((1, OWN), F32), vmem((OWN, OWN), F32),
        vmem((8, FEATS), F32), vmem((1, FEATS), F32), vmem((2 * OWN, FEATS), BF16),
        tile, field(NZ, 8), tile, field(NC, 8), vmem((NH, 8, 512), F32),
        vmem((128, 2048), BF16), vmem((128, FEATS), BF16), vmem((768, 128), BF16), vmem((768, 2048), BF16),
        field(NC, 32), field(NC, 32), field(NC, 16), field(NC, 16),
        vmem((32, 128), F32), vmem((32, 128), F32),
        field(NP, 32, BF16), field(NP, 32, BF16),
        field(NZ, 32), field(NZ, 32),
        vmem((768, 128), F32), vmem((768, 128), F32),
        field(NZ, 32), field(NZ, 32), field(NZ, 32),
        field(NZ, 16), field(NZ, 16), field(NZ, 16), field(NZ, 16),
        row, field(NP, 1), row, field(NZ, 1), row, field(NP, 1), row, field(NZ, 1),
        row, field(NZ * NP, 1),
        pltpu.SemaphoreType.DMA((8,)), pltpu.SemaphoreType.DMA((26,)),
        pltpu.SemaphoreType.DMA((26,)),
    ]
    operands = (
        x_train, x_cand, targets.reshape(1, OWN), noise, omega,
        phase.reshape(1, TOTAL_FEATS), prior_weights.T,
    )
    packed = pl.pallas_call(
        kernel,
        out_shape=jax.ShapeDtypeStruct((48, 128), F32),
        in_specs=[pl.BlockSpec(memory_space=pltpu.HBM)] * 7,
        out_specs=pl.BlockSpec(memory_space=vmem),
        scratch_shapes=scratch,
        compiler_params=pltpu.CompilerParams(
            collective_id=0, has_side_effects=True, vmem_limit_bytes=32 * 1024 * 1024
        ),
    )(*(pltpu.with_memory_space_constraint(value, pltpu.HBM) for value in operands))
    return pl.pallas_call(
        unpack,
        out_shape=(
            jax.ShapeDtypeStruct((CANDS, OWN), F32),
            jax.ShapeDtypeStruct((OWN, OWN), F32),
        ),
        in_specs=[pl.BlockSpec(memory_space=vmem)],
        out_specs=(pl.BlockSpec(memory_space=vmem),) * 2,
        compiler_params=pltpu.CompilerParams(vmem_limit_bytes=4 * 1024 * 1024),
    )(packed)


def solution(mesh):
    placed = (
        P(None, "train"),
        P(None, "cand"),
        P(("train", "cand")),
        P(("train", "cand"), None),
        P(),
        P(),
        P("cand", None),
    )
    return jax.shard_map(
        body,
        mesh=mesh,
        in_specs=placed,
        out_specs=(P(("cand", "train"), None), P(("train", "cand"), None)),
        check_vma=False,
    )
```

```python
import math

import jax
import jax.numpy as jnp
from jax import lax
from jax.experimental import pallas as pl
from jax.experimental.pallas import tpu as pltpu
from jax.sharding import PartitionSpec as P

MESH = pl.DeviceIdType.MESH
F32, BF16 = jnp.float32, jnp.bfloat16
NZ, NC, NH = 8, 8, 4
NP = NH * NC
OWN = 64
CANDS = 32
FEATS = 512
TOTAL_FEATS = 4096
NOISE_LEVEL = 0.5
def hops(offset):
    dx, dy, dz, _ = offset
    return min(dx, 4 - dx) + min(dy, 4 - dy) + min(dz, NZ - dz)


PLANE_ORDER = sorted(
    ((i, j, 0, k) for i in range(4) for j in range(4) for k in range(2) if i + j + k),
    key=lambda offset: -hops(offset),
)
EVERYONE = sorted(
    (
        (i, j, k, core)
        for i in range(4)
        for j in range(4)
        for k in range(NZ)
        for core in range(2)
        if i + j + k + core
    ),
    key=lambda offset: -hops(offset),
)
LINE_ORDER = (4, 3, 5, 2, 6, 1, 7, 0)


def place_of(k):
    return LINE_ORDER.index(k % NZ)
SIN = (
    6.283185159611151,
    -41.3416549293423,
    81.60099819256979,
    -76.5496568198889,
    39.53581370662112,
)


def split3(value):
    one = value.astype(BF16).astype(F32)
    two = (value - one).astype(BF16).astype(F32)
    return one, two, value - one - two


def rows8(*rows):
    index = lax.broadcasted_iota(jnp.int32, (8, rows[0].shape[1]), 0)
    out = jnp.zeros((8, rows[0].shape[1]), F32)
    for place, row in enumerate(rows):
        out = jnp.where(index == place, row, out)
    return out


def half_norm(points):
    return -0.5 * jnp.sum(points * points, axis=0, keepdims=True)


def left_side(points):
    one, two, three = split3(points)
    ones = jnp.ones((1, points.shape[1]), F32)
    tail = rows8(*split3(half_norm(points)), ones, ones, ones)
    pad = jnp.zeros((72, points.shape[1]), F32)
    return jnp.concatenate([one, one, two, two, one, three, tail, pad], axis=0).T.astype(BF16)


def right_side(points, tail):
    one, two, three = split3(points)
    pad = jnp.zeros((72, points.shape[1]), F32)
    return jnp.concatenate([one, two, one, two, three, one, tail, pad], axis=0).astype(BF16)


def kernel(
    xt_hbm, xc_hbm, tg_hbm, nz_hbm, om_hbm, ph_hbm, pw_hbm, packed,
    xt, xc, tg, nz, om, ph, pw,
    xls, xl, xcs, xcb, xp, by, bw, atl, km,
    pts, ptb, pcs, pcb, own0, own1, vb0, vb1, r0l, q0l,
    o1, o2, kr, krb, kq, ucs, ucb, wcs, wcb,
    sa_s, sa, sb_s, sb, ra_s, ra, rb_s, rb, qa_s, qa,
    isem, ssem, rsem,
):
    t, c = lax.axis_index("train"), lax.axis_index("cand")
    y_hi, z, core = t // 16, lax.rem(t, 16) // 2, lax.rem(t, 2)
    h = y_hi * 2 + core
    q = h * NC + c

    x, y = c // 2, y_hi * 2 + lax.rem(c, 2)

    y_lo = lax.rem(c, 2)
    ys = [lax.rem(y + k, 4) for k in range(4)]
    xs = [lax.rem(x + k, 4) for k in range(4)]
    zs = [lax.rem(z + k, NZ) for k in range(NZ)]
    cores = [core, 1 - core]

    def device(dx, dy, dz, dcore):
        return (
            (ys[dy] // 2) * 16 + zs[dz] * 2 + cores[dcore],
            xs[dx] * 2 + lax.rem(ys[dy], 2),
        )

    plane = [(device(*offset), offset[0]) for offset in PLANE_ORDER]
    everyone = [(device(*offset), None) for offset in EVERYONE]
    line = [(device(0, 0, k, 0), k) for k in LINE_ORDER[:-1]]
    blocks = [(device(0, j, 0, k), None) for j, k in ((2, 1), (2, 0), (0, 1))]
    near = 1 - y_lo
    cands = [
        ((t, xs[i] * 2 + j), (i, j))
        for i, j in ((2, 0), (2, 1), (1, 0), (1, 1), (3, 0), (3, 1), (0, near))
    ]
    sub = h * 2 + y_lo

    feat = pl.ds(pl.multiple_of(c * FEATS, FEATS), FEATS)
    inputs = [
        pltpu.make_async_copy(source, target, isem.at[number])
        for number, (source, target) in enumerate(
            (
                (xt_hbm, xt),
                (om_hbm.at[:, feat], om),
                (ph_hbm.at[:, feat], ph),
                (pw_hbm, pw.at[pl.ds(0, OWN)]),
                (pw_hbm, pw.at[pl.ds(OWN, OWN)]),
                (xc_hbm, xc),
                (tg_hbm, tg),
                (nz_hbm, nz),
            )
        )
    ]
    barrier = pltpu.get_barrier_semaphore()
    for copy in inputs[:5]:
        copy.start()
    greeted = line[:3] + cands[:2] + line[3:5] + cands[2:6] + blocks + line[5:] + cands[6:]
    for peer, _ in greeted:
        pl.semaphore_signal(barrier, inc=1, device_id=peer, device_id_type=MESH)
    for copy in inputs[5:]:
        copy.start()

    def push(phase, peers, source, target):
        for peer, tag in peers:
            number = phase(tag) if callable(phase) else phase
            pltpu.make_async_remote_copy(
                src_ref=source(tag) if callable(source) else source,
                dst_ref=target(tag) if callable(target) else target,
                send_sem=ssem.at[number],
                recv_sem=rsem.at[number],
                device_id=peer,
                device_id_type=MESH,
            ).start()

    def settle(phase, sems, buf, count=None):
        ref = buf.at[pl.ds(0, count or buf.shape[0] - 1)]
        pltpu.make_async_copy(ref, ref, sems.at[phase]).wait()

    def arrived(phase, buf, count=None):
        settle(phase, rsem, buf, count)

    def gather(base, field):
        push(
            lambda i: base + -i % 4,
            plane,
            field.at[sub],
            lambda i: field.at[(-i % 4) * 8 + sub],
        )

    lane = lax.broadcasted_iota(jnp.int32, (1, 128), 1)
    low = lane < 64

    def swap(value):
        return pltpu.roll(value, 64, 1)

    def pair(first, second):
        return jnp.where(low, first, swap(second))

    def fold(value):
        row = jnp.sum(value, axis=0, keepdims=True)
        return row + swap(row)

    for copy in inputs[:5]:
        copy.wait()

    turn = 1.0 / (2.0 * math.pi)
    zero = jnp.zeros((1, FEATS), F32)
    bw[...] = right_side(om[...] * turn, rows8(zero, zero, zero, *split3(ph[...] * turn)))
    def prior_share(left):
        turns = jnp.dot(left, bw[...], preferred_element_type=F32)
        wave = jnp.abs(turns - jnp.floor(turns) - 0.5) - 0.25
        square = wave * wave
        scale = math.sqrt(2.0 / TOTAL_FEATS)
        value = square * (SIN[-1] * scale) + SIN[-2] * scale
        for coefficient in SIN[-3::-1]:
            value = value * square + coefficient * scale
        packed = (value * wave).astype(BF16)
        return lax.dot_general(
            packed, pw[...], (((1,), (1,)), ((), ())), preferred_element_type=F32
        )

    out = prior_share(left_side(xt[...]))
    for i in range(NC):
        pts[i] = jnp.where(low, out[64 * i : 64 * i + 32], out[64 * i + 32 : 64 * i + 64])
    pl.semaphore_wait(barrier, len(greeted))
    push(3, cands, lambda tag: pts.at[xs[tag[0]] * 2 + tag[1]], ptb.at[c])
    for copy in inputs[5:]:
        copy.wait()

    mine = xt[:, pl.ds(pl.multiple_of((c // 2) * 128, 128), 128)]
    mine = jnp.where(lax.rem(c, 2) == 1, swap(mine), mine)
    xls[...] = mine
    xl[place_of(0)] = mine
    xp[h] = xt[...]
    cand = xc[:, pl.ds(pl.multiple_of((t // 4) * 128, 128), 128)]
    cand = pltpu.roll(cand, lax.rem(128 - lax.rem(t, 4) * 32, 128), 1)
    xcs[...] = cand
    xcb[c] = cand
    push(0, blocks, xt, xp.at[h])
    push(1, line, xls, lambda k: xl.at[place_of(-k)])
    push(2, cands, xcs, xcb.at[c])
    ptb[c] = pts[c]

    row = tg[...]
    place = lax.broadcasted_iota(jnp.int32, (32, 64), 0)
    at = lax.broadcasted_iota(jnp.int32, (32, 64), 1)
    upper = jnp.sum(jnp.where(at == place, row, 0.0), axis=1, keepdims=True)
    lower = jnp.sum(jnp.where(at == place + 32, row, 0.0), axis=1, keepdims=True)
    noise = jnp.concatenate([nz[0:32, :], nz[32:64, :]], axis=1)
    base = jnp.where(low, upper, lower) - noise

    def line_cands(j):
        tile = xc[:, pl.ds(pl.multiple_of(y_hi * 512 + j * 128, 128), 128)]
        tile = pltpu.roll(tile, lax.rem(128 - core * 32, 128), 1)
        return jnp.where(lane < 32, tile, pltpu.roll(tile, 96, 1))

    for j in range(2):
        atl[512 + j * 128 : 640 + j * 128, :] = left_side(
            pair(line_cands(2 * j), line_cands(2 * j + 1))
        )

    def entries(first, count):
        rows = pl.ds(first, count)
        power = jnp.dot(atl[rows, :], by[...], preferred_element_type=F32)
        km[rows, :] = jnp.exp(power).astype(BF16)

    arrived(3, ptb)
    r0 = base - jnp.sum(ptb[...], axis=0)
    own0[...] = r0
    r0l[place_of(0)] = r0
    vb0[sub] = r0.astype(BF16)
    gather(18, vb0)
    push(5, line, own0, lambda k: r0l.at[place_of(-k)])
    rr_own = fold(r0 * r0)

    arrived(0, xp)
    for i in range(4):
        tiles = [xp[g, :, pl.ds(pl.multiple_of(xs[i] * 128, 128), 128)] for g in range(NH)]
        uppers = [jnp.where(lane < 32, a, pltpu.roll(a, 96, 1)) for a in tiles]
        lowers = [jnp.where(lane < 32, pltpu.roll(a, 96, 1), swap(a)) for a in tiles]
        for start, halves in ((i * 256, uppers), (1024 + i * 256, lowers)):
            points = jnp.concatenate([pair(*halves[:2]), pair(*halves[2:])], axis=1)
            ones = jnp.ones((1, 256), F32)
            tail = rows8(ones, ones, ones, *split3(half_norm(points)))
            by[:, start : start + 256] = right_side(points, tail)

    arrived(1, xl)
    for j in range(4):
        atl[j * 128 : j * 128 + 128, :] = left_side(pair(xl[2 * j], xl[2 * j + 1]))
    entries(0, 512)
    entries(512, 256)

    def multiply(first, count, field):
        rows = pl.ds(first, count)
        values = field[...].reshape(NP * 32, 128)
        o1[rows, :] = jnp.dot(km[rows, 0:1024], values, preferred_element_type=F32)
        o2[rows, :] = jnp.dot(km[rows, 1024:2048], values, preferred_element_type=F32)

    def joined(first, size):
        a1, b1 = o1[pl.ds(first, size), :], o1[pl.ds(first + size, size), :]
        a2, b2 = o2[pl.ds(first, size), :], o2[pl.ds(first + size, size), :]
        return jnp.where(low, a1, b2) + swap(jnp.where(low, b1, a2))

    def gathered(base, field):
        for i in range(4):
            arrived(base + i, field, 7 if i == 0 else 8)

    def train_product(first, count, pieces, field):
        multiply(64 * first, 64 * count, field)
        for k in range(first, first + count):
            pieces[k] = joined(64 * k, 32)

    def cand_product(pieces, field):
        multiply(512, 256, field)
        for i in range(NZ):
            pieces[i] = joined(512 + i * 32, 16)

    def ratio(part):
        other = swap(part)
        norms = jnp.where(low, other, part)
        return norms, jnp.where(low, part, other) / norms + NOISE_LEVEL

    gathered(18, vb0)
    for first in (0, 4):
        train_product(first, 4, kr, vb0)
        push(7, line[first : first + 4], lambda k: kr.at[place_of(k)], krb.at[z])
    arrived(5, r0l)
    curve = fold(jnp.sum(kr[...] * r0l[...], axis=0))
    part = jnp.where(low, curve, rr_own)
    sa_s[...] = part
    sa[q] = part
    push(8, plane, sa_s, sa.at[q])
    krb[z] = kr[place_of(0)]
    cand_product(ucs, vb0)

    arrived(2, xcb)
    tiles = []
    for j in range(2):
        tile = xcb[4 * j]
        for g in range(1, 4):
            tile = jnp.where(lane < 32 * g, tile, pltpu.roll(xcb[4 * j + g], 32 * g, 1))
        tiles.append(tile)
    out = prior_share(left_side(jnp.concatenate(tiles, axis=1)))
    for i in range(NC):
        pcs[i] = jnp.where(low, out[32 * i : 32 * i + 16], out[32 * i + 16 : 32 * i + 32])
    pcb[c] = pcs[c]

    arrived(8, sa)
    part = jnp.sum(sa[...], axis=0)
    sb_s[...] = part
    sb[z] = part
    push(10, line, sb_s, sb.at[z])
    norms, quotient = ratio(part)
    share = jnp.where(norms > 0.0, quotient, 0.0)
    arrived(7, krb)
    r0 = own0[...]
    image = jnp.sum(krb[...], axis=0) + NOISE_LEVEL * r0

    own1[...] = image
    q0l[place_of(0)] = image
    vb1[sub] = (image - share * r0).astype(BF16)
    gather(22, vb1)
    push(12, line, own1, lambda k: q0l.at[place_of(-k)])
    arrived(10, sb)
    rr0, quotient = ratio(jnp.sum(sb[...], axis=0))
    alpha1 = 1.0 / quotient
    r1 = r0 - alpha1 * image
    rr1_own = fold(r1 * r1)
    ra_s[...] = rr1_own
    ra[q] = rr1_own
    push(13, plane, ra_s, ra.at[q])
    push(9, line, lambda k: ucs.at[zs[k]], ucb.at[z])
    ucb[z] = ucs[z]
    push(6, cands, lambda tag: pcs.at[xs[tag[0]] * 2 + tag[1]], pcb.at[c])
    mixed_own = fold(r0 * r1)
    gathered(22, vb1)
    train_product(0, NZ, kq, vb1)
    arrived(12, q0l)
    r1l = r0l[...] - alpha1 * q0l[...]
    k1 = (1.0 - alpha1 * share) * kr[...] - alpha1 * kq[...]
    curve = fold(jnp.sum(r1l * k1, axis=0)) + NOISE_LEVEL * rr1_own
    mixed = fold(jnp.sum(r0l[...] * k1 + r1l * kr[...], axis=0)) + 2.0 * NOISE_LEVEL * mixed_own
    part = jnp.where(low, curve, mixed)
    qa_s[...] = part
    qa[z * NP + q] = part
    push(16, everyone, qa_s, qa.at[z * NP + q])
    cand_product(wcs, vb1)
    wcs[...] = wcs[...] + share * ucs[...]
    push(15, line, lambda k: wcs.at[zs[k]], wcb.at[z])
    wcb[z] = wcs[z]
    arrived(13, ra)
    part = jnp.sum(ra[...], axis=0)
    rb_s[...] = part
    rb[z] = part
    push(14, line, rb_s, rb.at[z])
    arrived(6, pcb)
    prior = jnp.sum(pcb[...], axis=0)
    arrived(9, ucb)
    first_part = jnp.sum(ucb[...], axis=0)
    arrived(14, rb)
    rr1 = jnp.sum(rb[...], axis=0)
    beta = rr1 / rr0
    arrived(15, wcb)
    second_part = first_part - alpha1 * jnp.sum(wcb[...], axis=0)
    r0 = own0[...]
    r1 = r0 - alpha1 * own1[...]
    d1 = r1 + beta * r0
    arrived(16, qa)
    part = jnp.sum(qa[...], axis=0)
    other = swap(part)
    curve, mixed = jnp.where(low, part, other), jnp.where(low, other, part)
    alpha2 = rr1 / (curve + beta * (mixed + beta * (rr0 / alpha1)))

    packed[0:32, :] = alpha1 * r0 + alpha2 * d1
    packed[32:48, :] = prior + (alpha1 + alpha2 * beta) * first_part + alpha2 * second_part

    whole = {
        0: xp, 1: xl, 2: xcb, 3: ptb, 5: r0l, 6: pcb, 7: krb, 8: sa, 9: ucb, 10: sb,
        12: q0l, 13: ra, 14: rb, 15: wcb, 16: qa,
    }
    for phase, buf in whole.items():
        settle(phase, ssem, buf)
    for base, buf in ((18, vb0), (22, vb1)):
        for i in range(4):
            settle(base + i, ssem, buf, 7 if i == 0 else 8)


def unpack(packed, sam, sol):
    sol[0:32, :] = packed[0:32, 0:64]
    sol[32:64, :] = pltpu.roll(packed[0:32, :], 64, 1)[:, 0:64]
    sam[0:16, :] = packed[32:48, 0:64]
    sam[16:32, :] = pltpu.roll(packed[32:48, :], 64, 1)[:, 0:64]


def body(x_train, x_cand, targets, noise, omega, phase, prior_weights):
    vmem = pltpu.VMEM
    field = lambda n, rows, dtype=F32: vmem((n, rows, 128), dtype)
    tile, row = vmem((8, 128), F32), vmem((1, 128), F32)
    scratch = [
        vmem((8, 512), F32), vmem((8, 1024), F32), vmem((1, OWN), F32), vmem((OWN, OWN), F32),
        vmem((8, FEATS), F32), vmem((1, FEATS), F32), vmem((2 * OWN, FEATS), BF16),
        tile, field(NZ, 8), tile, field(NC, 8), vmem((NH, 8, 512), F32),
        vmem((128, 2048), BF16), vmem((128, FEATS), BF16), vmem((768, 128), BF16), vmem((768, 2048), BF16),
        field(NC, 32), field(NC, 32), field(NC, 16), field(NC, 16),
        vmem((32, 128), F32), vmem((32, 128), F32),
        field(NP, 32, BF16), field(NP, 32, BF16),
        field(NZ, 32), field(NZ, 32),
        vmem((768, 128), F32), vmem((768, 128), F32),
        field(NZ, 32), field(NZ, 32), field(NZ, 32),
        field(NZ, 16), field(NZ, 16), field(NZ, 16), field(NZ, 16),
        row, field(NP, 1), row, field(NZ, 1), row, field(NP, 1), row, field(NZ, 1),
        row, field(NZ * NP, 1),
        pltpu.SemaphoreType.DMA((8,)), pltpu.SemaphoreType.DMA((26,)),
        pltpu.SemaphoreType.DMA((26,)),
    ]
    operands = (
        x_train, x_cand, targets.reshape(1, OWN), noise, omega,
        phase.reshape(1, TOTAL_FEATS), prior_weights.T,
    )
    packed = pl.pallas_call(
        kernel,
        out_shape=jax.ShapeDtypeStruct((48, 128), F32),
        in_specs=[pl.BlockSpec(memory_space=pltpu.HBM)] * 7,
        out_specs=pl.BlockSpec(memory_space=vmem),
        scratch_shapes=scratch,
        compiler_params=pltpu.CompilerParams(
            collective_id=0, has_side_effects=True, vmem_limit_bytes=32 * 1024 * 1024
        ),
    )(*(pltpu.with_memory_space_constraint(value, pltpu.HBM) for value in operands))
    return pl.pallas_call(
        unpack,
        out_shape=(
            jax.ShapeDtypeStruct((CANDS, OWN), F32),
            jax.ShapeDtypeStruct((OWN, OWN), F32),
        ),
        in_specs=[pl.BlockSpec(memory_space=vmem)],
        out_specs=(pl.BlockSpec(memory_space=vmem),) * 2,
        compiler_params=pltpu.CompilerParams(vmem_limit_bytes=4 * 1024 * 1024),
    )(packed)


def solution(mesh):
    placed = (
        P(None, "train"),
        P(None, "cand"),
        P(("train", "cand")),
        P(("train", "cand"), None),
        P(),
        P(),
        P("cand", None),
    )
    return jax.shard_map(
        body,
        mesh=mesh,
        in_specs=placed,
        out_specs=(P(("cand", "train"), None), P(("train", "cand"), None)),
        check_vma=False,
    )
```

```python
import math

import jax
import jax.numpy as jnp
from jax import lax
from jax.experimental import pallas as pl
from jax.experimental.pallas import tpu as pltpu
from jax.sharding import PartitionSpec as P

MESH = pl.DeviceIdType.MESH
F32, BF16 = jnp.float32, jnp.bfloat16
NZ, NC, NH = 8, 8, 4
NP = NH * NC
OWN = 64
CANDS = 32
FEATS = 512
TOTAL_FEATS = 4096
NOISE_LEVEL = 0.5
def hops(offset):
    dx, dy, dz, _ = offset
    return min(dx, 4 - dx) + min(dy, 4 - dy) + min(dz, NZ - dz)


PLANE_ORDER = sorted(
    ((i, j, 0, k) for i in range(4) for j in range(4) for k in range(2) if i + j + k),
    key=lambda offset: -hops(offset),
)
EVERYONE = sorted(
    (
        (i, j, k, core)
        for i in range(4)
        for j in range(4)
        for k in range(NZ)
        for core in range(2)
        if i + j + k + core
    ),
    key=lambda offset: -hops(offset),
)
LINE_ORDER = (4, 3, 5, 2, 6, 1, 7, 0)


def place_of(k):
    return LINE_ORDER.index(k % NZ)
SIN = (
    6.283185159611151,
    -41.3416549293423,
    81.60099819256979,
    -76.5496568198889,
    39.53581370662112,
)


def split3(value):
    one = value.astype(BF16).astype(F32)
    two = (value - one).astype(BF16).astype(F32)
    return one, two, value - one - two


def rows8(*rows):
    index = lax.broadcasted_iota(jnp.int32, (8, rows[0].shape[1]), 0)
    out = jnp.zeros((8, rows[0].shape[1]), F32)
    for place, row in enumerate(rows):
        out = jnp.where(index == place, row, out)
    return out


def half_norm(points):
    return -0.5 * jnp.sum(points * points, axis=0, keepdims=True)


def left_side(points):
    one, two, three = split3(points)
    ones = jnp.ones((1, points.shape[1]), F32)
    tail = rows8(*split3(half_norm(points)), ones, ones, ones)
    pad = jnp.zeros((72, points.shape[1]), F32)
    return jnp.concatenate([one, one, two, two, one, three, tail, pad], axis=0).T.astype(BF16)


def right_side(points, tail):
    one, two, three = split3(points)
    pad = jnp.zeros((72, points.shape[1]), F32)
    return jnp.concatenate([one, two, one, two, three, one, tail, pad], axis=0).astype(BF16)


def kernel(
    xt_hbm, xc_hbm, tg_hbm, nz_hbm, om_hbm, ph_hbm, pw_hbm, packed,
    xt, xc, tg, nz, om, ph, pw,
    xls, xl, xcs, xcb, xp, by, bw, atl, km,
    pts, ptb, pcs, pcb, own0, own1, vb0, vb1, r0l, q0l,
    o1, o2, kr, krb, kq, ucs, ucb, wcs, wcb,
    sa_s, sa, sb_s, sb, ra_s, ra, rb_s, rb, qa_s, qa,
    isem, ssem, rsem,
):
    t, c = lax.axis_index("train"), lax.axis_index("cand")
    y_hi, z, core = t // 16, lax.rem(t, 16) // 2, lax.rem(t, 2)
    h = y_hi * 2 + core
    q = h * NC + c

    x, y = c // 2, y_hi * 2 + lax.rem(c, 2)

    y_lo = lax.rem(c, 2)
    ys = [lax.rem(y + k, 4) for k in range(4)]
    xs = [lax.rem(x + k, 4) for k in range(4)]
    zs = [lax.rem(z + k, NZ) for k in range(NZ)]
    cores = [core, 1 - core]

    def device(dx, dy, dz, dcore):
        return (
            (ys[dy] // 2) * 16 + zs[dz] * 2 + cores[dcore],
            xs[dx] * 2 + lax.rem(ys[dy], 2),
        )

    plane = [(device(*offset), offset[0]) for offset in PLANE_ORDER]
    everyone = [(device(*offset), None) for offset in EVERYONE]
    line = [(device(0, 0, k, 0), k) for k in LINE_ORDER[:-1]]
    blocks = [(device(0, j, 0, k), None) for j, k in ((2, 1), (2, 0), (0, 1))]
    near = 1 - y_lo
    cands = [
        ((t, xs[i] * 2 + j), (i, j))
        for i, j in (
            (2, near), (1, near), (3, near), (2, y_lo), (1, y_lo), (3, y_lo), (0, near),
        )
    ]
    sub = h * 2 + y_lo

    feat = pl.ds(pl.multiple_of(c * FEATS, FEATS), FEATS)
    inputs = [
        pltpu.make_async_copy(source, target, isem.at[number])
        for number, (source, target) in enumerate(
            (
                (xt_hbm, xt),
                (om_hbm.at[:, feat], om),
                (ph_hbm.at[:, feat], ph),
                (pw_hbm, pw.at[pl.ds(0, OWN)]),
                (pw_hbm, pw.at[pl.ds(OWN, OWN)]),
                (xc_hbm, xc),
                (tg_hbm, tg),
                (nz_hbm, nz),
            )
        )
    ]
    barrier = pltpu.get_barrier_semaphore()
    for copy in inputs[:5]:
        copy.start()
    greeted = line[:3] + cands[:2] + line[3:5] + cands[2:6] + blocks + line[5:] + cands[6:]
    for peer, _ in greeted:
        pl.semaphore_signal(barrier, inc=1, device_id=peer, device_id_type=MESH)
    for copy in inputs[5:]:
        copy.start()

    def push(phase, peers, source, target):
        for peer, tag in peers:
            number = phase(tag) if callable(phase) else phase
            pltpu.make_async_remote_copy(
                src_ref=source(tag) if callable(source) else source,
                dst_ref=target(tag) if callable(target) else target,
                send_sem=ssem.at[number],
                recv_sem=rsem.at[number],
                device_id=peer,
                device_id_type=MESH,
            ).start()

    def settle(phase, sems, buf, count=None):
        ref = buf.at[pl.ds(0, count or buf.shape[0] - 1)]
        pltpu.make_async_copy(ref, ref, sems.at[phase]).wait()

    def arrived(phase, buf, count=None):
        settle(phase, rsem, buf, count)

    def gather(base, field):
        push(
            lambda i: base + -i % 4,
            plane,
            field.at[sub],
            lambda i: field.at[(-i % 4) * 8 + sub],
        )

    lane = lax.broadcasted_iota(jnp.int32, (1, 128), 1)
    low = lane < 64

    def swap(value):
        return pltpu.roll(value, 64, 1)

    def pair(first, second):
        return jnp.where(low, first, swap(second))

    def fold(value):
        row = jnp.sum(value, axis=0, keepdims=True)
        return row + swap(row)

    for copy in inputs[:5]:
        copy.wait()

    turn = 1.0 / (2.0 * math.pi)
    zero = jnp.zeros((1, FEATS), F32)
    bw[...] = right_side(om[...] * turn, rows8(zero, zero, zero, *split3(ph[...] * turn)))
    def prior_share(left):
        turns = jnp.dot(left, bw[...], preferred_element_type=F32)
        wave = jnp.abs(turns - jnp.floor(turns) - 0.5) - 0.25
        square = wave * wave
        scale = math.sqrt(2.0 / TOTAL_FEATS)
        value = square * (SIN[-1] * scale) + SIN[-2] * scale
        for coefficient in SIN[-3::-1]:
            value = value * square + coefficient * scale
        packed = (value * wave).astype(BF16)
        return lax.dot_general(
            packed, pw[...], (((1,), (1,)), ((), ())), preferred_element_type=F32
        )

    out = prior_share(left_side(xt[...]))
    for i in range(NC):
        pts[i] = jnp.where(low, out[64 * i : 64 * i + 32], out[64 * i + 32 : 64 * i + 64])
    pl.semaphore_wait(barrier, len(greeted))
    push(3, cands, lambda tag: pts.at[xs[tag[0]] * 2 + tag[1]], ptb.at[c])
    for copy in inputs[5:]:
        copy.wait()

    mine = xt[:, pl.ds(pl.multiple_of((c // 2) * 128, 128), 128)]
    mine = jnp.where(lax.rem(c, 2) == 1, swap(mine), mine)
    xls[...] = mine
    xl[place_of(0)] = mine
    xp[h] = xt[...]
    cand = xc[:, pl.ds(pl.multiple_of((t // 4) * 128, 128), 128)]
    cand = pltpu.roll(cand, lax.rem(128 - lax.rem(t, 4) * 32, 128), 1)
    xcs[...] = cand
    xcb[c] = cand
    push(0, blocks, xt, xp.at[h])
    push(1, line, xls, lambda k: xl.at[place_of(-k)])
    push(2, cands, xcs, xcb.at[c])
    ptb[c] = pts[c]

    row = tg[...]
    place = lax.broadcasted_iota(jnp.int32, (32, 64), 0)
    at = lax.broadcasted_iota(jnp.int32, (32, 64), 1)
    upper = jnp.sum(jnp.where(at == place, row, 0.0), axis=1, keepdims=True)
    lower = jnp.sum(jnp.where(at == place + 32, row, 0.0), axis=1, keepdims=True)
    noise = jnp.concatenate([nz[0:32, :], nz[32:64, :]], axis=1)
    base = jnp.where(low, upper, lower) - noise

    def line_cands(j):
        tile = xc[:, pl.ds(pl.multiple_of(y_hi * 512 + j * 128, 128), 128)]
        tile = pltpu.roll(tile, lax.rem(128 - core * 32, 128), 1)
        return jnp.where(lane < 32, tile, pltpu.roll(tile, 96, 1))

    for j in range(2):
        atl[512 + j * 128 : 640 + j * 128, :] = left_side(
            pair(line_cands(2 * j), line_cands(2 * j + 1))
        )

    def entries(first, count):
        rows = pl.ds(first, count)
        power = jnp.dot(atl[rows, :], by[...], preferred_element_type=F32)
        km[rows, :] = jnp.exp(power).astype(BF16)

    arrived(3, ptb)
    r0 = base - jnp.sum(ptb[...], axis=0)
    own0[...] = r0
    r0l[place_of(0)] = r0
    vb0[sub] = r0.astype(BF16)
    gather(18, vb0)
    push(5, line, own0, lambda k: r0l.at[place_of(-k)])
    rr_own = fold(r0 * r0)

    arrived(0, xp)
    for i in range(4):
        tiles = [xp[g, :, pl.ds(pl.multiple_of(xs[i] * 128, 128), 128)] for g in range(NH)]
        uppers = [jnp.where(lane < 32, a, pltpu.roll(a, 96, 1)) for a in tiles]
        lowers = [jnp.where(lane < 32, pltpu.roll(a, 96, 1), swap(a)) for a in tiles]
        for start, halves in ((i * 256, uppers), (1024 + i * 256, lowers)):
            points = jnp.concatenate([pair(*halves[:2]), pair(*halves[2:])], axis=1)
            ones = jnp.ones((1, 256), F32)
            tail = rows8(ones, ones, ones, *split3(half_norm(points)))
            by[:, start : start + 256] = right_side(points, tail)

    arrived(1, xl)
    for j in range(4):
        atl[j * 128 : j * 128 + 128, :] = left_side(pair(xl[2 * j], xl[2 * j + 1]))
    entries(0, 512)
    entries(512, 256)

    def multiply(first, count, field):
        rows = pl.ds(first, count)
        values = field[...].reshape(NP * 32, 128)
        o1[rows, :] = jnp.dot(km[rows, 0:1024], values, preferred_element_type=F32)
        o2[rows, :] = jnp.dot(km[rows, 1024:2048], values, preferred_element_type=F32)

    def joined(first, size):
        a1, b1 = o1[pl.ds(first, size), :], o1[pl.ds(first + size, size), :]
        a2, b2 = o2[pl.ds(first, size), :], o2[pl.ds(first + size, size), :]
        return jnp.where(low, a1, b2) + swap(jnp.where(low, b1, a2))

    def gathered(base, field):
        for i in range(4):
            arrived(base + i, field, 7 if i == 0 else 8)

    def train_product(first, count, pieces, field):
        multiply(64 * first, 64 * count, field)
        for k in range(first, first + count):
            pieces[k] = joined(64 * k, 32)

    def cand_product(pieces, field):
        multiply(512, 256, field)
        for i in range(NZ):
            pieces[i] = joined(512 + i * 32, 16)

    def ratio(part):
        other = swap(part)
        norms = jnp.where(low, other, part)
        return norms, jnp.where(low, part, other) / norms + NOISE_LEVEL

    gathered(18, vb0)
    for first in (0, 4):
        train_product(first, 4, kr, vb0)
        push(7, line[first : first + 4], lambda k: kr.at[place_of(k)], krb.at[z])
    arrived(5, r0l)
    curve = fold(jnp.sum(kr[...] * r0l[...], axis=0))
    part = jnp.where(low, curve, rr_own)
    sa_s[...] = part
    sa[q] = part
    push(8, plane, sa_s, sa.at[q])
    krb[z] = kr[place_of(0)]
    cand_product(ucs, vb0)

    arrived(2, xcb)
    tiles = []
    for j in range(2):
        tile = xcb[4 * j]
        for g in range(1, 4):
            tile = jnp.where(lane < 32 * g, tile, pltpu.roll(xcb[4 * j + g], 32 * g, 1))
        tiles.append(tile)
    out = prior_share(left_side(jnp.concatenate(tiles, axis=1)))
    for i in range(NC):
        pcs[i] = jnp.where(low, out[32 * i : 32 * i + 16], out[32 * i + 16 : 32 * i + 32])
    pcb[c] = pcs[c]

    arrived(8, sa)
    part = jnp.sum(sa[...], axis=0)
    sb_s[...] = part
    sb[z] = part
    push(10, line, sb_s, sb.at[z])
    norms, quotient = ratio(part)
    share = jnp.where(norms > 0.0, quotient, 0.0)
    arrived(7, krb)
    r0 = own0[...]
    image = jnp.sum(krb[...], axis=0) + NOISE_LEVEL * r0

    own1[...] = image
    q0l[place_of(0)] = image
    vb1[sub] = (image - share * r0).astype(BF16)
    gather(22, vb1)
    push(12, line, own1, lambda k: q0l.at[place_of(-k)])
    arrived(10, sb)
    rr0, quotient = ratio(jnp.sum(sb[...], axis=0))
    alpha1 = 1.0 / quotient
    r1 = r0 - alpha1 * image
    rr1_own = fold(r1 * r1)
    ra_s[...] = rr1_own
    ra[q] = rr1_own
    push(13, plane, ra_s, ra.at[q])
    push(9, line, lambda k: ucs.at[zs[k]], ucb.at[z])
    ucb[z] = ucs[z]
    push(6, cands, lambda tag: pcs.at[xs[tag[0]] * 2 + tag[1]], pcb.at[c])
    mixed_own = fold(r0 * r1)
    gathered(22, vb1)
    train_product(0, NZ, kq, vb1)
    arrived(12, q0l)
    r1l = r0l[...] - alpha1 * q0l[...]
    k1 = (1.0 - alpha1 * share) * kr[...] - alpha1 * kq[...]
    curve = fold(jnp.sum(r1l * k1, axis=0)) + NOISE_LEVEL * rr1_own
    mixed = fold(jnp.sum(r0l[...] * k1 + r1l * kr[...], axis=0)) + 2.0 * NOISE_LEVEL * mixed_own
    part = jnp.where(low, curve, mixed)
    qa_s[...] = part
    qa[z * NP + q] = part
    push(16, everyone, qa_s, qa.at[z * NP + q])
    cand_product(wcs, vb1)
    wcs[...] = wcs[...] + share * ucs[...]
    push(15, line, lambda k: wcs.at[zs[k]], wcb.at[z])
    wcb[z] = wcs[z]
    arrived(13, ra)
    part = jnp.sum(ra[...], axis=0)
    rb_s[...] = part
    rb[z] = part
    push(14, line, rb_s, rb.at[z])
    arrived(6, pcb)
    prior = jnp.sum(pcb[...], axis=0)
    arrived(9, ucb)
    first_part = jnp.sum(ucb[...], axis=0)
    arrived(14, rb)
    rr1 = jnp.sum(rb[...], axis=0)
    beta = rr1 / rr0
    arrived(15, wcb)
    second_part = first_part - alpha1 * jnp.sum(wcb[...], axis=0)
    r0 = own0[...]
    r1 = r0 - alpha1 * own1[...]
    d1 = r1 + beta * r0
    arrived(16, qa)
    part = jnp.sum(qa[...], axis=0)
    other = swap(part)
    curve, mixed = jnp.where(low, part, other), jnp.where(low, other, part)
    alpha2 = rr1 / (curve + beta * (mixed + beta * (rr0 / alpha1)))

    packed[0:32, :] = alpha1 * r0 + alpha2 * d1
    packed[32:48, :] = prior + (alpha1 + alpha2 * beta) * first_part + alpha2 * second_part

    whole = {
        0: xp, 1: xl, 2: xcb, 3: ptb, 5: r0l, 6: pcb, 7: krb, 8: sa, 9: ucb, 10: sb,
        12: q0l, 13: ra, 14: rb, 15: wcb, 16: qa,
    }
    for phase, buf in whole.items():
        settle(phase, ssem, buf)
    for base, buf in ((18, vb0), (22, vb1)):
        for i in range(4):
            settle(base + i, ssem, buf, 7 if i == 0 else 8)


def unpack(packed, sam, sol):
    sol[0:32, :] = packed[0:32, 0:64]
    sol[32:64, :] = pltpu.roll(packed[0:32, :], 64, 1)[:, 0:64]
    sam[0:16, :] = packed[32:48, 0:64]
    sam[16:32, :] = pltpu.roll(packed[32:48, :], 64, 1)[:, 0:64]


def body(x_train, x_cand, targets, noise, omega, phase, prior_weights):
    vmem = pltpu.VMEM
    field = lambda n, rows, dtype=F32: vmem((n, rows, 128), dtype)
    tile, row = vmem((8, 128), F32), vmem((1, 128), F32)
    scratch = [
        vmem((8, 512), F32), vmem((8, 1024), F32), vmem((1, OWN), F32), vmem((OWN, OWN), F32),
        vmem((8, FEATS), F32), vmem((1, FEATS), F32), vmem((2 * OWN, FEATS), BF16),
        tile, field(NZ, 8), tile, field(NC, 8), vmem((NH, 8, 512), F32),
        vmem((128, 2048), BF16), vmem((128, FEATS), BF16), vmem((768, 128), BF16), vmem((768, 2048), BF16),
        field(NC, 32), field(NC, 32), field(NC, 16), field(NC, 16),
        vmem((32, 128), F32), vmem((32, 128), F32),
        field(NP, 32, BF16), field(NP, 32, BF16),
        field(NZ, 32), field(NZ, 32),
        vmem((768, 128), F32), vmem((768, 128), F32),
        field(NZ, 32), field(NZ, 32), field(NZ, 32),
        field(NZ, 16), field(NZ, 16), field(NZ, 16), field(NZ, 16),
        row, field(NP, 1), row, field(NZ, 1), row, field(NP, 1), row, field(NZ, 1),
        row, field(NZ * NP, 1),
        pltpu.SemaphoreType.DMA((8,)), pltpu.SemaphoreType.DMA((26,)),
        pltpu.SemaphoreType.DMA((26,)),
    ]
    operands = (
        x_train, x_cand, targets.reshape(1, OWN), noise, omega,
        phase.reshape(1, TOTAL_FEATS), prior_weights.T,
    )
    packed = pl.pallas_call(
        kernel,
        out_shape=jax.ShapeDtypeStruct((48, 128), F32),
        in_specs=[pl.BlockSpec(memory_space=pltpu.HBM)] * 7,
        out_specs=pl.BlockSpec(memory_space=vmem),
        scratch_shapes=scratch,
        compiler_params=pltpu.CompilerParams(
            collective_id=0, has_side_effects=True, vmem_limit_bytes=32 * 1024 * 1024
        ),
    )(*(pltpu.with_memory_space_constraint(value, pltpu.HBM) for value in operands))
    return pl.pallas_call(
        unpack,
        out_shape=(
            jax.ShapeDtypeStruct((CANDS, OWN), F32),
            jax.ShapeDtypeStruct((OWN, OWN), F32),
        ),
        in_specs=[pl.BlockSpec(memory_space=vmem)],
        out_specs=(pl.BlockSpec(memory_space=vmem),) * 2,
        compiler_params=pltpu.CompilerParams(vmem_limit_bytes=4 * 1024 * 1024),
    )(packed)


def solution(mesh):
    placed = (
        P(None, "train"),
        P(None, "cand"),
        P(("train", "cand")),
        P(("train", "cand"), None),
        P(),
        P(),
        P("cand", None),
    )
    return jax.shard_map(
        body,
        mesh=mesh,
        in_specs=placed,
        out_specs=(P(("cand", "train"), None), P(("train", "cand"), None)),
        check_vma=False,
    )
```

```python
import math

import jax
import jax.numpy as jnp
from jax import lax
from jax.experimental import pallas as pl
from jax.experimental.pallas import tpu as pltpu
from jax.sharding import PartitionSpec as P

MESH = pl.DeviceIdType.MESH
F32, BF16 = jnp.float32, jnp.bfloat16
NZ, NC, NH = 8, 8, 4
NP = NH * NC
OWN = 64
CANDS = 32
FEATS = 512
TOTAL_FEATS = 4096
NOISE_LEVEL = 0.5
def hops(offset):
    dx, dy, dz, _ = offset
    return min(dx, 4 - dx) + min(dy, 4 - dy) + min(dz, NZ - dz)


PLANE_ORDER = sorted(
    ((i, j, 0, k) for i in range(4) for j in range(4) for k in range(2) if i + j + k),
    key=lambda offset: -hops(offset),
)
EVERYONE = sorted(
    (
        (i, j, k, core)
        for i in range(4)
        for j in range(4)
        for k in range(NZ)
        for core in range(2)
        if i + j + k + core
    ),
    key=lambda offset: -hops(offset),
)
LINE_ORDER = (4, 3, 5, 2, 6, 1, 7, 0)


def place_of(k):
    return LINE_ORDER.index(k % NZ)
SIN = (
    6.283185159611151,
    -41.3416549293423,
    81.60099819256979,
    -76.5496568198889,
    39.53581370662112,
)


def split3(value):
    one = value.astype(BF16).astype(F32)
    two = (value - one).astype(BF16).astype(F32)
    return one, two, value - one - two


def rows8(*rows):
    index = lax.broadcasted_iota(jnp.int32, (8, rows[0].shape[1]), 0)
    out = jnp.zeros((8, rows[0].shape[1]), F32)
    for place, row in enumerate(rows):
        out = jnp.where(index == place, row, out)
    return out


def half_norm(points):
    return -0.5 * jnp.sum(points * points, axis=0, keepdims=True)


def left_side(points):
    one, two, three = split3(points)
    ones = jnp.ones((1, points.shape[1]), F32)
    tail = rows8(*split3(half_norm(points)), ones, ones, ones)
    pad = jnp.zeros((72, points.shape[1]), F32)
    return jnp.concatenate([one, one, two, two, one, three, tail, pad], axis=0).T.astype(BF16)


def right_side(points, tail):
    one, two, three = split3(points)
    pad = jnp.zeros((72, points.shape[1]), F32)
    return jnp.concatenate([one, two, one, two, three, one, tail, pad], axis=0).astype(BF16)


def kernel(
    xt_hbm, xc_hbm, tg_hbm, nz_hbm, om_hbm, ph_hbm, pw_hbm, packed,
    xt, xc, tg, nz, om, ph, pw,
    xls, xl, xcs, xcb, xp, by, bw, atl, km,
    pts, ptb, pcs, pcb, own0, own1, vb0, vb1, r0l, q0l,
    o1, o2, kr, krb, kq, ucs, ucb, wcs, wcb,
    sa_s, sa, sb_s, sb, ra_s, ra, rb_s, rb, qa_s, qa,
    isem, ssem, rsem,
):
    t, c = lax.axis_index("train"), lax.axis_index("cand")
    y_hi, z, core = t // 16, lax.rem(t, 16) // 2, lax.rem(t, 2)
    h = y_hi * 2 + core
    q = h * NC + c

    x, y = c // 2, y_hi * 2 + lax.rem(c, 2)

    y_lo = lax.rem(c, 2)
    ys = [lax.rem(y + k, 4) for k in range(4)]
    xs = [lax.rem(x + k, 4) for k in range(4)]
    zs = [lax.rem(z + k, NZ) for k in range(NZ)]
    cores = [core, 1 - core]

    def device(dx, dy, dz, dcore):
        return (
            (ys[dy] // 2) * 16 + zs[dz] * 2 + cores[dcore],
            xs[dx] * 2 + lax.rem(ys[dy], 2),
        )

    plane = [(device(*offset), offset[0]) for offset in PLANE_ORDER]
    everyone = [(device(*offset), None) for offset in EVERYONE]
    line = [(device(0, 0, k, 0), k) for k in LINE_ORDER[:-1]]
    blocks = [(device(0, j, 0, k), None) for j, k in ((2, 1), (2, 0), (0, 1))]
    near = 1 - y_lo
    cands = [
        ((t, xs[i] * 2 + j), (i, j))
        for i, j in (
            (2, near), (1, near), (3, near), (2, y_lo), (1, y_lo), (3, y_lo), (0, near),
        )
    ]
    sub = h * 2 + y_lo

    feat = pl.ds(pl.multiple_of(c * FEATS, FEATS), FEATS)
    inputs = [
        pltpu.make_async_copy(source, target, isem.at[number])
        for number, (source, target) in enumerate(
            (
                (xt_hbm, xt),
                (om_hbm.at[:, feat], om),
                (ph_hbm.at[:, feat], ph),
                (pw_hbm, pw.at[pl.ds(0, OWN)]),
                (pw_hbm, pw.at[pl.ds(OWN, OWN)]),
                (xc_hbm, xc),
                (tg_hbm, tg),
                (nz_hbm, nz),
            )
        )
    ]
    barrier = pltpu.get_barrier_semaphore()
    for copy in inputs[:5]:
        copy.start()
    greeted = line[:3] + cands[:2] + line[3:5] + cands[2:6] + blocks + line[5:] + cands[6:]
    for peer, _ in greeted:
        pl.semaphore_signal(barrier, inc=1, device_id=peer, device_id_type=MESH)
    for copy in inputs[5:]:
        copy.start()

    def push(phase, peers, source, target):
        for peer, tag in peers:
            number = phase(tag) if callable(phase) else phase
            pltpu.make_async_remote_copy(
                src_ref=source(tag) if callable(source) else source,
                dst_ref=target(tag) if callable(target) else target,
                send_sem=ssem.at[number],
                recv_sem=rsem.at[number],
                device_id=peer,
                device_id_type=MESH,
            ).start()

    def settle(phase, sems, buf, count=None):
        ref = buf.at[pl.ds(0, count or buf.shape[0] - 1)]
        pltpu.make_async_copy(ref, ref, sems.at[phase]).wait()

    def arrived(phase, buf, count=None):
        settle(phase, rsem, buf, count)

    def gather(base, field):
        push(
            lambda i: base + -i % 4,
            plane,
            field.at[sub],
            lambda i: field.at[(-i % 4) * 8 + sub],
        )

    lane = lax.broadcasted_iota(jnp.int32, (1, 128), 1)
    low = lane < 64

    def swap(value):
        return pltpu.roll(value, 64, 1)

    def pair(first, second):
        return jnp.where(low, first, swap(second))

    def fold(value):
        row = jnp.sum(value, axis=0, keepdims=True)
        return row + swap(row)

    for copy in inputs[:5]:
        copy.wait()

    turn = 1.0 / (2.0 * math.pi)
    zero = jnp.zeros((1, FEATS), F32)
    bw[...] = right_side(om[...] * turn, rows8(zero, zero, zero, *split3(ph[...] * turn)))
    def prior_share(left):
        turns = jnp.dot(left, bw[...], preferred_element_type=F32)
        wave = jnp.abs(turns - jnp.floor(turns) - 0.5) - 0.25
        square = wave * wave
        scale = math.sqrt(2.0 / TOTAL_FEATS)
        value = square * (SIN[-1] * scale) + SIN[-2] * scale
        for coefficient in SIN[-3::-1]:
            value = value * square + coefficient * scale
        packed = (value * wave).astype(BF16)
        return lax.dot_general(
            packed, pw[...], (((1,), (1,)), ((), ())), preferred_element_type=F32
        )

    out = prior_share(left_side(xt[...]))
    for i in range(NC):
        pts[i] = jnp.where(low, out[64 * i : 64 * i + 32], out[64 * i + 32 : 64 * i + 64])
    pl.semaphore_wait(barrier, len(greeted))
    push(3, cands, lambda tag: pts.at[xs[tag[0]] * 2 + tag[1]], ptb.at[c])
    for copy in inputs[5:]:
        copy.wait()

    mine = xt[:, pl.ds(pl.multiple_of((c // 2) * 128, 128), 128)]
    mine = jnp.where(lax.rem(c, 2) == 1, swap(mine), mine)
    xls[...] = mine
    xl[place_of(0)] = mine
    xp[h] = xt[...]
    cand = xc[:, pl.ds(pl.multiple_of((t // 4) * 128, 128), 128)]
    cand = pltpu.roll(cand, lax.rem(128 - lax.rem(t, 4) * 32, 128), 1)
    xcs[...] = cand
    xcb[c] = cand
    push(0, blocks, xt, xp.at[h])
    push(1, line, xls, lambda k: xl.at[place_of(-k)])
    push(2, cands, xcs, xcb.at[c])
    ptb[c] = pts[c]

    row = tg[...]
    place = lax.broadcasted_iota(jnp.int32, (32, 64), 0)
    at = lax.broadcasted_iota(jnp.int32, (32, 64), 1)
    upper = jnp.sum(jnp.where(at == place, row, 0.0), axis=1, keepdims=True)
    lower = jnp.sum(jnp.where(at == place + 32, row, 0.0), axis=1, keepdims=True)
    noise = jnp.concatenate([nz[0:32, :], nz[32:64, :]], axis=1)
    base = jnp.where(low, upper, lower) - noise

    def line_cands(j):
        tile = xc[:, pl.ds(pl.multiple_of(y_hi * 512 + j * 128, 128), 128)]
        tile = pltpu.roll(tile, lax.rem(128 - core * 32, 128), 1)
        return jnp.where(lane < 32, tile, pltpu.roll(tile, 96, 1))

    for j in range(2):
        atl[512 + j * 128 : 640 + j * 128, :] = left_side(
            pair(line_cands(2 * j), line_cands(2 * j + 1))
        )

    def entries(first, count):
        rows = pl.ds(first, count)
        power = jnp.dot(atl[rows, :], by[...], preferred_element_type=F32)
        km[rows, :] = jnp.exp(power).astype(BF16)

    arrived(3, ptb)
    r0 = base - jnp.sum(ptb[...], axis=0)
    own0[...] = r0
    r0l[place_of(0)] = r0
    vb0[sub] = r0.astype(BF16)
    gather(18, vb0)
    push(5, line, own0, lambda k: r0l.at[place_of(-k)])
    rr_own = fold(r0 * r0)

    arrived(0, xp)
    for i in range(4):
        tiles = [xp[g, :, pl.ds(pl.multiple_of(xs[i] * 128, 128), 128)] for g in range(NH)]
        uppers = [jnp.where(lane < 32, a, pltpu.roll(a, 96, 1)) for a in tiles]
        lowers = [jnp.where(lane < 32, pltpu.roll(a, 96, 1), swap(a)) for a in tiles]
        for start, halves in ((i * 256, uppers), (1024 + i * 256, lowers)):
            points = jnp.concatenate([pair(*halves[:2]), pair(*halves[2:])], axis=1)
            ones = jnp.ones((1, 256), F32)
            tail = rows8(ones, ones, ones, *split3(half_norm(points)))
            by[:, start : start + 256] = right_side(points, tail)

    arrived(1, xl)
    for j in range(4):
        atl[j * 128 : j * 128 + 128, :] = left_side(pair(xl[2 * j], xl[2 * j + 1]))
    entries(0, 512)
    entries(512, 256)

    def multiply(first, count, field):
        rows = pl.ds(first, count)
        values = field[...].reshape(NP * 32, 128)
        o1[rows, :] = jnp.dot(km[rows, 0:1024], values, preferred_element_type=F32)
        o2[rows, :] = jnp.dot(km[rows, 1024:2048], values, preferred_element_type=F32)

    def joined(first, size):
        a1, b1 = o1[pl.ds(first, size), :], o1[pl.ds(first + size, size), :]
        a2, b2 = o2[pl.ds(first, size), :], o2[pl.ds(first + size, size), :]
        return jnp.where(low, a1, b2) + swap(jnp.where(low, b1, a2))

    def gathered(base, field):
        for i in range(4):
            arrived(base + i, field, 7 if i == 0 else 8)

    def train_product(first, count, pieces, field):
        multiply(64 * first, 64 * count, field)
        for k in range(first, first + count):
            pieces[k] = joined(64 * k, 32)

    def cand_product(pieces, field):
        multiply(512, 256, field)
        for i in range(NZ):
            pieces[i] = joined(512 + i * 32, 16)

    def ratio(part):
        other = swap(part)
        norms = jnp.where(low, other, part)
        return norms, jnp.where(low, part, other) / norms + NOISE_LEVEL

    gathered(18, vb0)
    for first in (0, 4):
        train_product(first, 4, kr, vb0)
        push(7, line[first : first + 4], lambda k: kr.at[place_of(k)], krb.at[z])
    arrived(5, r0l)
    curve = fold(jnp.sum(kr[...] * r0l[...], axis=0))
    part = jnp.where(low, curve, rr_own)
    sa_s[...] = part
    sa[q] = part
    push(8, plane, sa_s, sa.at[q])
    krb[z] = kr[place_of(0)]
    cand_product(ucs, vb0)

    arrived(2, xcb)
    tiles = []
    for j in range(2):
        tile = xcb[4 * j]
        for g in range(1, 4):
            tile = jnp.where(lane < 32 * g, tile, pltpu.roll(xcb[4 * j + g], 32 * g, 1))
        tiles.append(tile)
    out = prior_share(left_side(jnp.concatenate(tiles, axis=1)))
    for i in range(NC):
        pcs[i] = jnp.where(low, out[32 * i : 32 * i + 16], out[32 * i + 16 : 32 * i + 32])
    pcb[c] = pcs[c]

    arrived(8, sa)
    part = jnp.sum(sa[...], axis=0)
    sb_s[...] = part
    sb[z] = part
    push(10, line, sb_s, sb.at[z])
    norms, quotient = ratio(part)
    share = jnp.where(norms > 0.0, quotient, 0.0)
    arrived(7, krb)
    r0 = own0[...]
    image = jnp.sum(krb[...], axis=0) + NOISE_LEVEL * r0

    own1[...] = image
    q0l[place_of(0)] = image
    vb1[sub] = (image - share * r0).astype(BF16)
    gather(22, vb1)
    push(12, line, own1, lambda k: q0l.at[place_of(-k)])
    arrived(10, sb)
    rr0, quotient = ratio(jnp.sum(sb[...], axis=0))
    alpha1 = 1.0 / quotient
    r1 = r0 - alpha1 * image
    rr1_own = fold(r1 * r1)
    ra_s[...] = rr1_own
    ra[q] = rr1_own
    push(13, plane, ra_s, ra.at[q])
    push(9, line, lambda k: ucs.at[zs[k]], ucb.at[z])
    ucb[z] = ucs[z]
    push(6, cands, lambda tag: pcs.at[xs[tag[0]] * 2 + tag[1]], pcb.at[c])
    mixed_own = fold(r0 * r1)
    gathered(22, vb1)
    train_product(0, NZ, kq, vb1)
    arrived(12, q0l)
    r1l = r0l[...] - alpha1 * q0l[...]
    k1 = (1.0 - alpha1 * share) * kr[...] - alpha1 * kq[...]
    curve = fold(jnp.sum(r1l * k1, axis=0)) + NOISE_LEVEL * rr1_own
    mixed = fold(jnp.sum(r0l[...] * k1 + r1l * kr[...], axis=0)) + 2.0 * NOISE_LEVEL * mixed_own
    part = jnp.where(low, curve, mixed)
    qa_s[...] = part
    qa[z * NP + q] = part
    push(16, everyone, qa_s, qa.at[z * NP + q])
    cand_product(wcs, vb1)
    wcs[...] = wcs[...] + share * ucs[...]
    push(15, line, lambda k: wcs.at[zs[k]], wcb.at[z])
    wcb[z] = wcs[z]
    arrived(13, ra)
    part = jnp.sum(ra[...], axis=0)
    rb_s[...] = part
    rb[z] = part
    push(14, line, rb_s, rb.at[z])
    arrived(6, pcb)
    prior = jnp.sum(pcb[...], axis=0)
    arrived(9, ucb)
    first_part = jnp.sum(ucb[...], axis=0)
    arrived(14, rb)
    rr1 = jnp.sum(rb[...], axis=0)
    beta = rr1 / rr0
    arrived(15, wcb)
    second_part = first_part - alpha1 * jnp.sum(wcb[...], axis=0)
    r0 = own0[...]
    r1 = r0 - alpha1 * own1[...]
    d1 = r1 + beta * r0
    first_step = alpha1 * r0
    first_sample = prior + alpha1 * first_part
    sample_step = beta * first_part + second_part
    first_square = beta * beta * (rr0 / alpha1)

    whole = {
        0: xp, 1: xl, 2: xcb, 3: ptb, 5: r0l, 6: pcb, 7: krb, 8: sa, 9: ucb, 10: sb,
        12: q0l, 13: ra, 14: rb, 15: wcb, 16: qa,
    }
    for phase, buf in whole.items():
        settle(phase, ssem, buf)
    for base, buf in ((18, vb0), (22, vb1)):
        for i in range(4):
            settle(base + i, ssem, buf, 7 if i == 0 else 8)

    arrived(16, qa)
    part = jnp.sum(qa[...], axis=0)
    other = swap(part)
    curve, mixed = jnp.where(low, part, other), jnp.where(low, other, part)
    alpha2 = rr1 / (curve + beta * mixed + first_square)
    packed[0:32, :] = first_step + alpha2 * d1
    packed[32:48, :] = first_sample + alpha2 * sample_step


def unpack(packed, sam, sol):
    sol[0:32, :] = packed[0:32, 0:64]
    sol[32:64, :] = pltpu.roll(packed[0:32, :], 64, 1)[:, 0:64]
    sam[0:16, :] = packed[32:48, 0:64]
    sam[16:32, :] = pltpu.roll(packed[32:48, :], 64, 1)[:, 0:64]


def body(x_train, x_cand, targets, noise, omega, phase, prior_weights):
    vmem = pltpu.VMEM
    field = lambda n, rows, dtype=F32: vmem((n, rows, 128), dtype)
    tile, row = vmem((8, 128), F32), vmem((1, 128), F32)
    scratch = [
        vmem((8, 512), F32), vmem((8, 1024), F32), vmem((1, OWN), F32), vmem((OWN, OWN), F32),
        vmem((8, FEATS), F32), vmem((1, FEATS), F32), vmem((2 * OWN, FEATS), BF16),
        tile, field(NZ, 8), tile, field(NC, 8), vmem((NH, 8, 512), F32),
        vmem((128, 2048), BF16), vmem((128, FEATS), BF16), vmem((768, 128), BF16), vmem((768, 2048), BF16),
        field(NC, 32), field(NC, 32), field(NC, 16), field(NC, 16),
        vmem((32, 128), F32), vmem((32, 128), F32),
        field(NP, 32, BF16), field(NP, 32, BF16),
        field(NZ, 32), field(NZ, 32),
        vmem((768, 128), F32), vmem((768, 128), F32),
        field(NZ, 32), field(NZ, 32), field(NZ, 32),
        field(NZ, 16), field(NZ, 16), field(NZ, 16), field(NZ, 16),
        row, field(NP, 1), row, field(NZ, 1), row, field(NP, 1), row, field(NZ, 1),
        row, field(NZ * NP, 1),
        pltpu.SemaphoreType.DMA((8,)), pltpu.SemaphoreType.DMA((26,)),
        pltpu.SemaphoreType.DMA((26,)),
    ]
    operands = (
        x_train, x_cand, targets.reshape(1, OWN), noise, omega,
        phase.reshape(1, TOTAL_FEATS), prior_weights.T,
    )
    packed = pl.pallas_call(
        kernel,
        out_shape=jax.ShapeDtypeStruct((48, 128), F32),
        in_specs=[pl.BlockSpec(memory_space=pltpu.HBM)] * 7,
        out_specs=pl.BlockSpec(memory_space=vmem),
        scratch_shapes=scratch,
        compiler_params=pltpu.CompilerParams(
            collective_id=0, has_side_effects=True, vmem_limit_bytes=32 * 1024 * 1024
        ),
    )(*(pltpu.with_memory_space_constraint(value, pltpu.HBM) for value in operands))
    return pl.pallas_call(
        unpack,
        out_shape=(
            jax.ShapeDtypeStruct((CANDS, OWN), F32),
            jax.ShapeDtypeStruct((OWN, OWN), F32),
        ),
        in_specs=[pl.BlockSpec(memory_space=vmem)],
        out_specs=(pl.BlockSpec(memory_space=vmem),) * 2,
        compiler_params=pltpu.CompilerParams(vmem_limit_bytes=4 * 1024 * 1024),
    )(packed)


def solution(mesh):
    placed = (
        P(None, "train"),
        P(None, "cand"),
        P(("train", "cand")),
        P(("train", "cand"), None),
        P(),
        P(),
        P("cand", None),
    )
    return jax.shard_map(
        body,
        mesh=mesh,
        in_specs=placed,
        out_specs=(P(("cand", "train"), None), P(("train", "cand"), None)),
        check_vma=False,
    )
```

```python
import math

import jax
import jax.numpy as jnp
from jax import lax
from jax.experimental import pallas as pl
from jax.experimental.pallas import tpu as pltpu
from jax.sharding import PartitionSpec as P

MESH = pl.DeviceIdType.MESH
F32, BF16 = jnp.float32, jnp.bfloat16
NZ, NC, NH = 8, 8, 4
NP = NH * NC
OWN = 64
CANDS = 32
FEATS = 512
TOTAL_FEATS = 4096
NOISE_LEVEL = 0.5
def hops(offset):
    dx, dy, dz, _ = offset
    return min(dx, 4 - dx) + min(dy, 4 - dy) + min(dz, NZ - dz)


PLANE_ORDER = sorted(
    ((i, j, 0, k) for i in range(4) for j in range(4) for k in range(2) if i + j + k),
    key=lambda offset: -hops(offset),
)
EVERYONE = sorted(
    (
        (i, j, k, core)
        for i in range(4)
        for j in range(4)
        for k in range(NZ)
        for core in range(2)
        if i + j + k + core
    ),
    key=lambda offset: -hops(offset),
)
LINE_ORDER = (4, 3, 5, 2, 6, 1, 7, 0)


def place_of(k):
    return LINE_ORDER.index(k % NZ)
SIN = (
    6.283185159611151,
    -41.3416549293423,
    81.60099819256979,
    -76.5496568198889,
    39.53581370662112,
)


def split3(value):
    one = value.astype(BF16).astype(F32)
    two = (value - one).astype(BF16).astype(F32)
    return one, two, value - one - two


def rows8(*rows):
    index = lax.broadcasted_iota(jnp.int32, (8, rows[0].shape[1]), 0)
    out = jnp.zeros((8, rows[0].shape[1]), F32)
    for place, row in enumerate(rows):
        out = jnp.where(index == place, row, out)
    return out


def half_norm(points):
    return -0.5 * jnp.sum(points * points, axis=0, keepdims=True)


def left_side(points):
    one, two, three = split3(points)
    ones = jnp.ones((1, points.shape[1]), F32)
    tail = rows8(*split3(half_norm(points)), ones, ones, ones)
    pad = jnp.zeros((72, points.shape[1]), F32)
    return jnp.concatenate([one, one, two, two, one, three, tail, pad], axis=0).T.astype(BF16)


def right_side(points, tail):
    one, two, three = split3(points)
    pad = jnp.zeros((72, points.shape[1]), F32)
    return jnp.concatenate([one, two, one, two, three, one, tail, pad], axis=0).astype(BF16)


def kernel(
    xt_hbm, xc_hbm, tg_hbm, nz_hbm, om_hbm, ph_hbm, pw_hbm, packed,
    xt, xc, tg, nz, om, ph, pw,
    xls, xl, xcs, xcb, xp, by, bw, atl, km,
    pts, ptb, pcs, pcb, own0, own1, vb0, vb1, r0l, q0l,
    o1, o2, kr, krb, kq, ucs, ucb, wcs, wcb,
    sa_s, sa, sb_s, sb, ra_s, ra, rb_s, rb, qa_s, qa,
    isem, ssem, rsem,
):
    t, c = lax.axis_index("train"), lax.axis_index("cand")
    y_hi, z, core = t // 16, lax.rem(t, 16) // 2, lax.rem(t, 2)
    h = y_hi * 2 + core
    q = h * NC + c

    x, y = c // 2, y_hi * 2 + lax.rem(c, 2)

    y_lo = lax.rem(c, 2)
    ys = [lax.rem(y + k, 4) for k in range(4)]
    xs = [lax.rem(x + k, 4) for k in range(4)]
    zs = [lax.rem(z + k, NZ) for k in range(NZ)]
    cores = [core, 1 - core]

    def device(dx, dy, dz, dcore):
        return (
            (ys[dy] // 2) * 16 + zs[dz] * 2 + cores[dcore],
            xs[dx] * 2 + lax.rem(ys[dy], 2),
        )

    plane = [(device(*offset), offset[0]) for offset in PLANE_ORDER]
    everyone = [(device(*offset), None) for offset in EVERYONE]
    line = [(device(0, 0, k, 0), k) for k in LINE_ORDER[:-1]]
    blocks = [(device(0, j, 0, k), None) for j, k in ((2, 1), (2, 0), (0, 1))]
    near = 1 - y_lo
    cands = [
        ((t, xs[i] * 2 + j), (i, j))
        for i, j in (
            (2, near), (1, near), (3, near), (2, y_lo), (1, y_lo), (3, y_lo), (0, near),
        )
    ]
    sub = h * 2 + y_lo

    feat = pl.ds(pl.multiple_of(c * FEATS, FEATS), FEATS)
    inputs = [
        pltpu.make_async_copy(source, target, isem.at[number])
        for number, (source, target) in enumerate(
            (
                (xt_hbm, xt),
                (om_hbm.at[:, feat], om),
                (ph_hbm.at[:, feat], ph),
                (pw_hbm, pw.at[pl.ds(0, OWN)]),
                (pw_hbm, pw.at[pl.ds(OWN, OWN)]),
                (xc_hbm, xc),
                (tg_hbm, tg),
                (nz_hbm, nz),
            )
        )
    ]
    barrier = pltpu.get_barrier_semaphore()
    greeted = line[:3] + cands[:2] + line[3:5] + cands[2:6] + blocks + line[5:] + cands[6:]
    for peer, _ in greeted:
        pl.semaphore_signal(barrier, inc=1, device_id=peer, device_id_type=MESH)
    for copy in inputs:
        copy.start()

    def push(phase, peers, source, target):
        for peer, tag in peers:
            number = phase(tag) if callable(phase) else phase
            pltpu.make_async_remote_copy(
                src_ref=source(tag) if callable(source) else source,
                dst_ref=target(tag) if callable(target) else target,
                send_sem=ssem.at[number],
                recv_sem=rsem.at[number],
                device_id=peer,
                device_id_type=MESH,
            ).start()

    def settle(phase, sems, buf, count=None):
        ref = buf.at[pl.ds(0, count or buf.shape[0] - 1)]
        pltpu.make_async_copy(ref, ref, sems.at[phase]).wait()

    def arrived(phase, buf, count=None):
        settle(phase, rsem, buf, count)

    def gather(base, field):
        push(
            lambda i: base + -i % 4,
            plane,
            field.at[sub],
            lambda i: field.at[(-i % 4) * 8 + sub],
        )

    lane = lax.broadcasted_iota(jnp.int32, (1, 128), 1)
    low = lane < 64

    def swap(value):
        return pltpu.roll(value, 64, 1)

    def pair(first, second):
        return jnp.where(low, first, swap(second))

    def fold(value):
        row = jnp.sum(value, axis=0, keepdims=True)
        return row + swap(row)

    for copy in inputs[:5]:
        copy.wait()

    turn = 1.0 / (2.0 * math.pi)
    zero = jnp.zeros((1, FEATS), F32)
    bw[...] = right_side(om[...] * turn, rows8(zero, zero, zero, *split3(ph[...] * turn)))
    def prior_share(left):
        turns = jnp.dot(left, bw[...], preferred_element_type=F32)
        wave = jnp.abs(turns - jnp.floor(turns) - 0.5) - 0.25
        square = wave * wave
        scale = math.sqrt(2.0 / TOTAL_FEATS)
        value = square * (SIN[-1] * scale) + SIN[-2] * scale
        for coefficient in SIN[-3::-1]:
            value = value * square + coefficient * scale
        packed = (value * wave).astype(BF16)
        return lax.dot_general(
            packed, pw[...], (((1,), (1,)), ((), ())), preferred_element_type=F32
        )

    out = prior_share(left_side(xt[...]))
    for i in range(NC):
        pts[i] = jnp.where(low, out[64 * i : 64 * i + 32], out[64 * i + 32 : 64 * i + 64])
    pl.semaphore_wait(barrier, len(greeted))
    push(3, cands, lambda tag: pts.at[xs[tag[0]] * 2 + tag[1]], ptb.at[c])
    for copy in inputs[5:]:
        copy.wait()

    mine = xt[:, pl.ds(pl.multiple_of((c // 2) * 128, 128), 128)]
    mine = jnp.where(lax.rem(c, 2) == 1, swap(mine), mine)
    xls[...] = mine
    xl[place_of(0)] = mine
    xp[h] = xt[...]
    cand = xc[:, pl.ds(pl.multiple_of((t // 4) * 128, 128), 128)]
    cand = pltpu.roll(cand, lax.rem(128 - lax.rem(t, 4) * 32, 128), 1)
    xcs[...] = cand
    xcb[c] = cand
    push(0, blocks, xt, xp.at[h])
    push(1, line, xls, lambda k: xl.at[place_of(-k)])
    push(2, cands, xcs, xcb.at[c])
    ptb[c] = pts[c]

    row = tg[...]
    place = lax.broadcasted_iota(jnp.int32, (32, 64), 0)
    at = lax.broadcasted_iota(jnp.int32, (32, 64), 1)
    upper = jnp.sum(jnp.where(at == place, row, 0.0), axis=1, keepdims=True)
    lower = jnp.sum(jnp.where(at == place + 32, row, 0.0), axis=1, keepdims=True)
    noise = jnp.concatenate([nz[0:32, :], nz[32:64, :]], axis=1)
    base = jnp.where(low, upper, lower) - noise

    def line_cands(j):
        tile = xc[:, pl.ds(pl.multiple_of(y_hi * 512 + j * 128, 128), 128)]
        tile = pltpu.roll(tile, lax.rem(128 - core * 32, 128), 1)
        return jnp.where(lane < 32, tile, pltpu.roll(tile, 96, 1))

    for j in range(2):
        atl[512 + j * 128 : 640 + j * 128, :] = left_side(
            pair(line_cands(2 * j), line_cands(2 * j + 1))
        )

    def entries(first, count):
        rows = pl.ds(first, count)
        power = jnp.dot(atl[rows, :], by[...], preferred_element_type=F32)
        km[rows, :] = jnp.exp(power).astype(BF16)

    arrived(3, ptb)
    r0 = base - jnp.sum(ptb[...], axis=0)
    own0[...] = r0
    r0l[place_of(0)] = r0
    vb0[sub] = r0.astype(BF16)
    gather(18, vb0)
    push(5, line, own0, lambda k: r0l.at[place_of(-k)])
    rr_own = fold(r0 * r0)

    arrived(0, xp)
    for i in range(4):
        tiles = [xp[g, :, pl.ds(pl.multiple_of(xs[i] * 128, 128), 128)] for g in range(NH)]
        uppers = [jnp.where(lane < 32, a, pltpu.roll(a, 96, 1)) for a in tiles]
        lowers = [jnp.where(lane < 32, pltpu.roll(a, 96, 1), swap(a)) for a in tiles]
        for start, halves in ((i * 256, uppers), (1024 + i * 256, lowers)):
            points = jnp.concatenate([pair(*halves[:2]), pair(*halves[2:])], axis=1)
            ones = jnp.ones((1, 256), F32)
            tail = rows8(ones, ones, ones, *split3(half_norm(points)))
            by[:, start : start + 256] = right_side(points, tail)

    arrived(1, xl)
    for j in range(4):
        atl[j * 128 : j * 128 + 128, :] = left_side(pair(xl[2 * j], xl[2 * j + 1]))
    entries(0, 512)
    entries(512, 256)

    def multiply(first, count, field):
        rows = pl.ds(first, count)
        values = field[...].reshape(NP * 32, 128)
        o1[rows, :] = jnp.dot(km[rows, 0:1024], values, preferred_element_type=F32)
        o2[rows, :] = jnp.dot(km[rows, 1024:2048], values, preferred_element_type=F32)

    def joined(first, size):
        a1, b1 = o1[pl.ds(first, size), :], o1[pl.ds(first + size, size), :]
        a2, b2 = o2[pl.ds(first, size), :], o2[pl.ds(first + size, size), :]
        return jnp.where(low, a1, b2) + swap(jnp.where(low, b1, a2))

    def gathered(base, field):
        for i in range(4):
            arrived(base + i, field, 7 if i == 0 else 8)

    def train_product(first, count, pieces, field):
        multiply(64 * first, 64 * count, field)
        for k in range(first, first + count):
            pieces[k] = joined(64 * k, 32)

    def cand_product(pieces, field):
        multiply(512, 256, field)
        for i in range(NZ):
            pieces[i] = joined(512 + i * 32, 16)

    def ratio(part):
        other = swap(part)
        norms = jnp.where(low, other, part)
        return norms, jnp.where(low, part, other) / norms + NOISE_LEVEL

    gathered(18, vb0)
    for first in (0, 4):
        train_product(first, 4, kr, vb0)
        push(7, line[first : first + 4], lambda k: kr.at[place_of(k)], krb.at[z])
    arrived(5, r0l)
    curve = fold(jnp.sum(kr[...] * r0l[...], axis=0))
    part = jnp.where(low, curve, rr_own)
    sa_s[...] = part
    sa[q] = part
    push(8, plane, sa_s, sa.at[q])
    krb[z] = kr[place_of(0)]
    cand_product(ucs, vb0)

    arrived(2, xcb)
    tiles = []
    for j in range(2):
        tile = xcb[4 * j]
        for g in range(1, 4):
            tile = jnp.where(lane < 32 * g, tile, pltpu.roll(xcb[4 * j + g], 32 * g, 1))
        tiles.append(tile)
    out = prior_share(left_side(jnp.concatenate(tiles, axis=1)))
    for i in range(NC):
        pcs[i] = jnp.where(low, out[32 * i : 32 * i + 16], out[32 * i + 16 : 32 * i + 32])
    pcb[c] = pcs[c]

    arrived(8, sa)
    part = jnp.sum(sa[...], axis=0)
    sb_s[...] = part
    sb[z] = part
    push(10, line, sb_s, sb.at[z])
    norms, quotient = ratio(part)
    share = jnp.where(norms > 0.0, quotient, 0.0)
    arrived(7, krb)
    r0 = own0[...]
    image = jnp.sum(krb[...], axis=0) + NOISE_LEVEL * r0

    own1[...] = image
    q0l[place_of(0)] = image
    vb1[sub] = (image - share * r0).astype(BF16)
    gather(22, vb1)
    push(12, line, own1, lambda k: q0l.at[place_of(-k)])
    arrived(10, sb)
    rr0, quotient = ratio(jnp.sum(sb[...], axis=0))
    alpha1 = 1.0 / quotient
    r1 = r0 - alpha1 * image
    rr1_own = fold(r1 * r1)
    ra_s[...] = rr1_own
    ra[q] = rr1_own
    push(13, plane, ra_s, ra.at[q])
    push(9, line, lambda k: ucs.at[zs[k]], ucb.at[z])
    ucb[z] = ucs[z]
    push(6, cands, lambda tag: pcs.at[xs[tag[0]] * 2 + tag[1]], pcb.at[c])
    mixed_own = fold(r0 * r1)
    gathered(22, vb1)
    train_product(0, NZ, kq, vb1)
    arrived(12, q0l)
    r1l = r0l[...] - alpha1 * q0l[...]
    k1 = (1.0 - alpha1 * share) * kr[...] - alpha1 * kq[...]
    curve = fold(jnp.sum(r1l * k1, axis=0)) + NOISE_LEVEL * rr1_own
    mixed = fold(jnp.sum(r0l[...] * k1 + r1l * kr[...], axis=0)) + 2.0 * NOISE_LEVEL * mixed_own
    part = jnp.where(low, curve, mixed)
    qa_s[...] = part
    qa[z * NP + q] = part
    push(16, everyone, qa_s, qa.at[z * NP + q])
    cand_product(wcs, vb1)
    wcs[...] = wcs[...] + share * ucs[...]
    push(15, line, lambda k: wcs.at[zs[k]], wcb.at[z])
    wcb[z] = wcs[z]
    arrived(13, ra)
    part = jnp.sum(ra[...], axis=0)
    rb_s[...] = part
    rb[z] = part
    push(14, line, rb_s, rb.at[z])
    arrived(6, pcb)
    prior = jnp.sum(pcb[...], axis=0)
    arrived(9, ucb)
    first_part = jnp.sum(ucb[...], axis=0)
    arrived(14, rb)
    rr1 = jnp.sum(rb[...], axis=0)
    beta = rr1 / rr0
    arrived(15, wcb)
    second_part = first_part - alpha1 * jnp.sum(wcb[...], axis=0)
    r0 = own0[...]
    r1 = r0 - alpha1 * own1[...]
    d1 = r1 + beta * r0
    first_step = alpha1 * r0
    first_sample = prior + alpha1 * first_part
    sample_step = beta * first_part + second_part
    first_square = beta * beta * (rr0 / alpha1)

    whole = {
        0: xp, 1: xl, 2: xcb, 3: ptb, 5: r0l, 6: pcb, 7: krb, 8: sa, 9: ucb, 10: sb,
        12: q0l, 13: ra, 14: rb, 15: wcb, 16: qa,
    }
    for phase, buf in whole.items():
        settle(phase, ssem, buf)
    for base, buf in ((18, vb0), (22, vb1)):
        for i in range(4):
            settle(base + i, ssem, buf, 7 if i == 0 else 8)

    arrived(16, qa)
    part = jnp.sum(qa[...], axis=0)
    other = swap(part)
    curve, mixed = jnp.where(low, part, other), jnp.where(low, other, part)
    alpha2 = rr1 / (curve + beta * mixed + first_square)
    packed[0:32, :] = first_step + alpha2 * d1
    packed[32:48, :] = first_sample + alpha2 * sample_step


def unpack(packed, sam, sol):
    sol[0:32, :] = packed[0:32, 0:64]
    sol[32:64, :] = pltpu.roll(packed[0:32, :], 64, 1)[:, 0:64]
    sam[0:16, :] = packed[32:48, 0:64]
    sam[16:32, :] = pltpu.roll(packed[32:48, :], 64, 1)[:, 0:64]


def body(x_train, x_cand, targets, noise, omega, phase, prior_weights):
    vmem = pltpu.VMEM
    field = lambda n, rows, dtype=F32: vmem((n, rows, 128), dtype)
    tile, row = vmem((8, 128), F32), vmem((1, 128), F32)
    scratch = [
        vmem((8, 512), F32), vmem((8, 1024), F32), vmem((1, OWN), F32), vmem((OWN, OWN), F32),
        vmem((8, FEATS), F32), vmem((1, FEATS), F32), vmem((2 * OWN, FEATS), BF16),
        tile, field(NZ, 8), tile, field(NC, 8), vmem((NH, 8, 512), F32),
        vmem((128, 2048), BF16), vmem((128, FEATS), BF16), vmem((768, 128), BF16), vmem((768, 2048), BF16),
        field(NC, 32), field(NC, 32), field(NC, 16), field(NC, 16),
        vmem((32, 128), F32), vmem((32, 128), F32),
        field(NP, 32, BF16), field(NP, 32, BF16),
        field(NZ, 32), field(NZ, 32),
        vmem((768, 128), F32), vmem((768, 128), F32),
        field(NZ, 32), field(NZ, 32), field(NZ, 32),
        field(NZ, 16), field(NZ, 16), field(NZ, 16), field(NZ, 16),
        row, field(NP, 1), row, field(NZ, 1), row, field(NP, 1), row, field(NZ, 1),
        row, field(NZ * NP, 1),
        pltpu.SemaphoreType.DMA((8,)), pltpu.SemaphoreType.DMA((26,)),
        pltpu.SemaphoreType.DMA((26,)),
    ]
    operands = (
        x_train, x_cand, targets.reshape(1, OWN), noise, omega,
        phase.reshape(1, TOTAL_FEATS), prior_weights.T,
    )
    packed = pl.pallas_call(
        kernel,
        out_shape=jax.ShapeDtypeStruct((48, 128), F32),
        in_specs=[pl.BlockSpec(memory_space=pltpu.HBM)] * 7,
        out_specs=pl.BlockSpec(memory_space=vmem),
        scratch_shapes=scratch,
        compiler_params=pltpu.CompilerParams(
            collective_id=0, has_side_effects=True, vmem_limit_bytes=32 * 1024 * 1024
        ),
    )(*(pltpu.with_memory_space_constraint(value, pltpu.HBM) for value in operands))
    return pl.pallas_call(
        unpack,
        out_shape=(
            jax.ShapeDtypeStruct((CANDS, OWN), F32),
            jax.ShapeDtypeStruct((OWN, OWN), F32),
        ),
        in_specs=[pl.BlockSpec(memory_space=vmem)],
        out_specs=(pl.BlockSpec(memory_space=vmem),) * 2,
        compiler_params=pltpu.CompilerParams(vmem_limit_bytes=4 * 1024 * 1024),
    )(packed)


def solution(mesh):
    placed = (
        P(None, "train"),
        P(None, "cand"),
        P(("train", "cand")),
        P(("train", "cand"), None),
        P(),
        P(),
        P("cand", None),
    )
    return jax.shard_map(
        body,
        mesh=mesh,
        in_specs=placed,
        out_specs=(P(("cand", "train"), None), P(("train", "cand"), None)),
        check_vma=False,
    )
```
